512 devices in a mesh: corpus: 128 (over y, z, core), query: 4 (over x).
Axes of the slice: x: 4, y: 8, z: 8, core: 2. Of those that a mesh axis runs over, the one named last changes fastest.
Arguments:
- text_features: bfloat16 [2048, 768], P(('corpus', 'query')), may hold values from -6 to 6
- norm_gain: float32 [768], replicated, may hold values from 0.25 to 1.75
- norm_bias: float32 [768], replicated, may hold values from -3 to 3
- projection: bfloat16 [768, 768], replicated, may hold values from -0.21875 to 0.21875
- image_embeddings: bfloat16 [32768, 768], P('corpus'), may hold values from -6 to 6
- adapter: bfloat16 [768, 768], replicated, may hold values from -0.21875 to 0.21875
- slab_ids: int32 [32768], P('corpus'), may hold values from 0 to 8191
- positive_rows: int32 [2048], P(('corpus', 'query')), may hold values from 0 to 32767
Outputs:
- text_grad: float32 [2048, 768], P(('corpus', 'query'))
- gain_grad: float32 [768], replicated
- bias_grad: float32 [768], replicated
- projection_grad: bfloat16 [768, 768], replicated
- adapter_grad: float32 [768, 768], P('query', 'corpus')
The draws below stay inside these ranges and needn't reach their ends.
All inputs are finite; a program needn't handle non-finite values.
Results may differ from the reference program's by a relative error of at most 0.015.
Values may be sent and summed in bfloat16 or wider, within the bound.
A program may use at most 64 MiB of HBM per device.

```python
import jax
import jax.numpy as jnp
from jax import lax

D = 768
SLAB_DEV = 256
QUERY_DEV = 4
CORPUS = 32768
QUERIES = 2048
N_CORPUS = 128
N_QUERY = 4


def place_ends(entries, stream_key, smallest, top_value):
    place = [jax.random.randint(jax.random.fold_in(stream_key, axis), (), 0, length) for axis, length in enumerate(entries.shape)]
    main_axis = entries.shape.index(max(entries.shape))
    beside = place[:main_axis] + [(place[main_axis] + 1) % entries.shape[main_axis]] + place[main_axis + 1:]
    return entries.at[tuple(place)].set(smallest).at[tuple(beside)].set(top_value)


def block_scale(stream_key, extent, split, least, top_value):
    def one(dim, blocks):
        draws = jax.random.uniform(jax.random.fold_in(jax.random.fold_in(stream_key, 6), dim), (blocks,), jnp.float32, least / len(split), top_value / len(split))
        return jnp.repeat(jnp.exp(draws), extent[dim] // blocks).reshape((-1,) + (1,) * (len(extent) - dim - 1))

    gain = one(*split[0])
    for cut in split[1:]:
        gain = gain * one(*cut)
    return gain


def bell_draw(own_key, extent, scale, reach, pieces=(), kind=jnp.bfloat16):
    array = scale * jax.random.normal(own_key, extent, jnp.float32)
    if pieces:
        array = array * block_scale(own_key, extent, pieces, -0.22, 0.18)
    return jnp.clip(array, -reach, reach).astype(kind)


def setup_inputs(seed: int = 0) -> dict:
    key_list = jax.random.split(jax.random.key(seed), 9)
    text_features = bell_draw(key_list[0], (QUERIES, D), 1.0, 6.0, ((0, 512),))
    norm_gain = jnp.clip(1.0 + 0.15 * jax.random.normal(key_list[1], (D,), jnp.float32), 0.25, 1.75)
    norm_bias = bell_draw(key_list[2], (D,), 0.5, 3.0, (), jnp.float32)
    projection = bell_draw(key_list[3], (D, D), D ** -0.5, 0.21875)
    image_embeddings = bell_draw(key_list[4], (CORPUS, D), 1.0, 6.0, ((0, 128),))
    adapter = bell_draw(key_list[5], (D, D), D ** -0.5, 0.21875)
    slab_ids = place_ends(jax.random.randint(key_list[6], (CORPUS,), 0, SLAB_DEV * N_CORPUS // 4), jax.random.fold_in(key_list[6], 1), 0, (SLAB_DEV * N_CORPUS // 4) - 1).astype(jnp.int32)
    positive_rows = place_ends(jax.random.randint(key_list[7], (QUERIES,), 0, SLAB_DEV * N_CORPUS), jax.random.fold_in(key_list[7], 1), 0, (SLAB_DEV * N_CORPUS) - 1).astype(jnp.int32)
    return dict(text_features=text_features, norm_gain=norm_gain, norm_bias=norm_bias, projection=projection, image_embeddings=image_embeddings, adapter=adapter, slab_ids=slab_ids, positive_rows=positive_rows)


logit_scale = 64.0
epsilon = 1e-05

def forward_queries(text_features, norm_gain, norm_bias, projection):
    features = text_features.astype(jnp.float32)
    average = lax.optimization_barrier(jnp.mean(features, axis=1, keepdims=True))
    centred = features - average
    spread = jnp.sqrt(lax.optimization_barrier(jnp.mean(centred * centred, axis=1, keepdims=True)) + epsilon)
    normed = centred / spread
    shifted = (normed * norm_gain + norm_bias).astype(jnp.bfloat16)
    raw_query = jnp.dot(shifted, projection, preferred_element_type=jnp.float32)
    length = jnp.sqrt(lax.optimization_barrier(jnp.sum(raw_query * raw_query, axis=1, keepdims=True)) + 1e-06)
    unit_query = raw_query / length
    return (normed, spread, shifted, length, unit_query)

def reference(text_features, norm_gain, norm_bias, projection, image_embeddings, adapter, slab_ids, positive_rows):
    normed, spread, shifted, length, unit_query = forward_queries(text_features, norm_gain, norm_bias, projection)
    query_half = unit_query.astype(jnp.bfloat16)
    raw_key = jnp.dot(image_embeddings, adapter, preferred_element_type=jnp.float32)
    key_len = jnp.sqrt(lax.optimization_barrier(jnp.sum(raw_key * raw_key, axis=1, keepdims=True)) + 1e-06)
    unit_key = raw_key / key_len
    key_half = unit_key.astype(jnp.bfloat16)
    targets = slab_ids[positive_rows]
    model_width = query_half.shape[1]
    group_rows = N_CORPUS * QUERY_DEV
    grouped_q = query_half.reshape(N_CORPUS, N_QUERY, QUERY_DEV, model_width).transpose(1, 0, 2, 3).reshape(N_QUERY, group_rows, model_width)
    grouped_t = targets.reshape(N_CORPUS, N_QUERY, QUERY_DEV).transpose(1, 0, 2).reshape(N_QUERY, group_rows)

    def one_group(key_acc, inputs):
        group_queries, wanted = inputs
        scores = logit_scale * jnp.dot(group_queries, key_half.T, preferred_element_type=jnp.float32)
        exponent = jnp.exp(scores)
        totals = lax.optimization_barrier(jnp.sum(exponent, axis=1, keepdims=True))
        matches = slab_ids[None, :] == wanted[:, None]
        pos_totals = lax.optimization_barrier(jnp.sum(jnp.where(matches, exponent, jnp.float32(0.0)), axis=1, keepdims=True))
        weights = (logit_scale * (exponent / totals - jnp.where(matches, exponent / pos_totals, jnp.float32(0.0)))).astype(jnp.bfloat16)
        query_sum = jnp.dot(weights, key_half, preferred_element_type=jnp.float32)
        key_part = jnp.dot(weights.T, group_queries, preferred_element_type=jnp.float32)
        rounded = lax.optimization_barrier(key_part.astype(jnp.bfloat16))
        return (key_acc + rounded.astype(key_acc.dtype), query_sum)
    key_sum, query_sums = lax.scan(one_group, jnp.zeros(key_half.shape, jnp.float32), (grouped_q, grouped_t))
    query_sum = query_sums.reshape(N_QUERY, N_CORPUS, QUERY_DEV, model_width).transpose(1, 0, 2, 3).reshape(-1, model_width)
    key_raw_grad = ((key_sum - unit_key * lax.optimization_barrier(jnp.sum(unit_key * key_sum, axis=1, keepdims=True))) / key_len).astype(jnp.bfloat16)
    adapter_grad = jnp.dot(image_embeddings.T, key_raw_grad, preferred_element_type=jnp.float32)
    query_raw_grad = ((query_sum - unit_query * lax.optimization_barrier(jnp.sum(unit_query * query_sum, axis=1, keepdims=True))) / length).astype(jnp.bfloat16)
    projection_grad = jnp.dot(shifted.T, query_raw_grad, preferred_element_type=jnp.float32).astype(jnp.bfloat16)
    shifted_grad = jnp.dot(query_raw_grad, projection.T, preferred_element_type=jnp.float32)
    gain_grad = lax.optimization_barrier(jnp.sum(shifted_grad * normed, axis=0))
    bias_grad = lax.optimization_barrier(jnp.sum(shifted_grad, axis=0))
    scaled_grad = shifted_grad * norm_gain
    text_grad = (scaled_grad - lax.optimization_barrier(jnp.mean(scaled_grad, axis=1, keepdims=True)) - normed * lax.optimization_barrier(jnp.mean(scaled_grad * normed, axis=1, keepdims=True))) / spread
    return (text_grad, gain_grad, bias_grad, projection_grad, adapter_grad)
```

```python
import functools

import jax
import jax.numpy as jnp
from jax import lax
from jax.experimental import pallas as pl
from jax.experimental.pallas import tpu as pltpu
from jax.sharding import PartitionSpec as P

F32 = jnp.float32
BF16 = jnp.bfloat16
MESH = pl.DeviceIdType.MESH

D = 768
SLAB = 256
ROWS = 4
NA = 8
NX = 4
GROUP = 512
ORDER = (1, 7, 2, 6, 3, 5, 4)
XORDER = (1, 3, 2)


def dot(a, b):
    return jnp.dot(a, b, preferred_element_type=F32)


def dot_rows(a, b):
    return lax.dot_general(a, b, (((0,), (0,)), ((), ())), preferred_element_type=F32)


def dot_cols(a, b):
    return lax.dot_general(a, b, (((1,), (1,)), ((), ())), preferred_element_type=F32)


def iota(shape, axis):
    return lax.broadcasted_iota(jnp.int32, shape, axis)


def fold_matrix():
    row, col = iota((128, 128), 0), iota((128, 128), 1)
    source = ((row // 4) % 8) * 16 + 4 * (row // 32) + row % 4
    return jnp.where(source == col, F32(1.0), F32(0.0)).astype(BF16)


def fold_four(rows):
    return jnp.concatenate(
        [rows[:, :256], rows[:, 256:512], rows[:, 512:], jnp.zeros((ROWS, 256), F32)], axis=0
    )


def normalise(features, gain, bias):
    average = jnp.mean(features, axis=1, keepdims=True)
    centred = features - average
    spread = jnp.sqrt(jnp.mean(centred * centred, axis=1, keepdims=True) + 1e-5)
    normed = centred / spread
    return normed, spread, (normed * gain + bias).astype(BF16)


def unit_rows(raw):
    length = jnp.sqrt(jnp.sum(raw * raw, axis=1, keepdims=True) + 1e-6)
    return raw / length, length


def kernel(
    msg_ref, tf_ref, gain_ref, bias_ref, proj_ref, emb_ref, adapter_ref, ids_ref,
    text_out, gb_out, proj_out, adapter_out,
    g1, g2, own_norm, own_unit, own_col, unit_key, key_half, key_len, emb_sel, perm,
    normed_all, shifted_all, query_half, xt, expo, pexpo, weights,
    stat_send, stat_core, stat_a, stat_b,
    q_send, q_own, q_core, qb_send, qb_recv, qa_send, qa_recv, qrg_all,
    k_send, k_recv, krg, s_own, s_send, s_core, sb_send, sb_recv, sa_send, sa_recv, s_wide,
    p_send, p_recv, p_out, gb_recv,
    ag1_ss, ag1_rs, st_ss, st_rs, q_ss, q_rs, ag2_ss, ag2_rs, k_ss, k_rs, s_ss, s_rs, p_ss, p_rs,
    out_sem,
):
    corpus = lax.axis_index("corpus")
    x = lax.axis_index("query")
    c = lax.rem(corpus, 2)
    y = corpus // 16
    z = lax.rem(corpus // 2, 8)
    a = z + c * (y - z)
    b = y + c * (z - y)
    step_a = 2 + 14 * c
    step_b = 16 - 14 * c

    def on_a(k):
        place = lax.rem(a + k, NA)
        return place, (place * step_a + b * step_b + c, x)

    def on_b(k):
        place = lax.rem(b + k, NA)
        return place, (a * step_a + place * step_b + c, x)

    def on_x(k):
        place = lax.rem(x + k, NX)
        return place, (corpus, place)

    partner = (corpus + 1 - 2 * c, x)
    pending = []

    def send(src, dst, send_sem, recv_sem, device):
        copy = pltpu.make_async_remote_copy(
            src_ref=src, dst_ref=dst, send_sem=send_sem, recv_sem=recv_sem,
            device_id=device, device_id_type=MESH,
        )
        copy.start()
        pending.append(copy)

    def arrived(dst, recv_sem):
        pltpu.make_async_remote_copy(
            src_ref=dst, dst_ref=dst, send_sem=recv_sem, recv_sem=recv_sem,
            device_id=partner, device_id_type=MESH,
        ).wait_recv()

    barrier = pltpu.get_barrier_semaphore()
    pl.semaphore_signal(barrier, inc=1, device_id=partner, device_id_type=MESH)
    for k in range(1, NA):
        pl.semaphore_signal(barrier, inc=1, device_id=on_a(k)[1], device_id_type=MESH)
        pl.semaphore_signal(barrier, inc=1, device_id=on_b(k)[1], device_id_type=MESH)
    for k in range(1, NX):
        pl.semaphore_signal(barrier, inc=1, device_id=on_x(k)[1], device_id_type=MESH)

    gain = gain_ref[...]
    bias = bias_ref[...]
    g1[0, b, pl.ds(pl.multiple_of(a * 16, 16), 16), :] = msg_ref[...]
    pl.semaphore_wait(barrier, 2 * (NA - 1) + NX)

    def gather_start(g, ss, rs):
        own = g.at[0, b, pl.ds(pl.multiple_of(a * 16, 16), 16), :]
        for k in ORDER:
            send(own, own, ss.at[k], rs.at[k], on_a(k)[1])

    def gather_middle(g, ss, rs):
        for k in ORDER:
            place = on_a(NA - k)[0]
            arrived(g.at[0, b, pl.ds(pl.multiple_of(place * 16, 16), 16), :], rs.at[k])
        for k in ORDER:
            send(g.at[0, b], g.at[0, b], ss.at[8 + k], rs.at[8 + k], on_b(k)[1])
        send(g.at[0, b], g.at[1, b], ss.at[16], rs.at[16], partner)

    def gather_forward(g, ss, rs):
        for k in ORDER:
            place = on_b(NA - k)[0]
            arrived(g.at[0, place], rs.at[8 + k])
            send(g.at[0, place], g.at[1, place], ss.at[16 + k], rs.at[16 + k], partner)

    def gather_end(g, ss, rs):
        arrived(g.at[1, a], rs.at[16])
        for k in ORDER:
            arrived(g.at[1, lax.rem(a + NA - k, NA)], rs.at[16 + k])

    gather_start(g1, ag1_ss, ag1_rs)

    @pl.loop(0, SLAB // 128)
    def _(i):
        rows = pl.ds(pl.multiple_of(i * 128, 128), 128)
        unit, length = unit_rows(dot(emb_ref[rows, :], adapter_ref[...]))
        unit_key[rows, :] = unit
        key_half[rows, :] = unit.astype(BF16)
        key_len[rows, :] = jnp.broadcast_to(length, (128, 128))

    gather_middle(g1, ag1_ss, ag1_rs)

    pick = jnp.where(
        (iota((D, 256), 0) == iota((D, 256), 1) + x * 192) & (iota((D, 256), 1) < 192),
        F32(1.0), F32(0.0),
    ).astype(BF16)
    emb_sel[...] = dot(emb_ref[...], pick).astype(BF16)

    own4 = tf_ref[...].astype(F32)
    own16 = jnp.concatenate([own4, own4, own4, own4], axis=0)
    normed, spread, shifted = normalise(own16, gain, bias)
    unit, length = unit_rows(dot(shifted, proj_ref[...]))
    own_norm[...] = normed
    own_unit[...] = unit
    own_col[0] = jnp.broadcast_to(spread, (16, 128))
    own_col[1] = jnp.broadcast_to(length, (16, 128))

    gather_forward(g1, ag1_ss, ag1_rs)

    place = iota((1, 1024), 1)
    core = lax.rem(place // 512 + c, 2)
    place_b, place_a = (place // 64) % 8, (place // 8) % 8
    place_y = jnp.where(core == 0, place_b, place_a)
    place_z = place_a + place_b - place_y
    column = jnp.where(
        place % 8 < 6, 6 * (place_y * 16 + place_z * 2 + core) + place % 8, -1
    )

    @pl.loop(0, D // 128)
    def _(i):
        rows = pl.ds(pl.multiple_of(i * 128, 128), 128)
        perm[rows, :] = jnp.where(
            iota((128, 1024), 0) + i * 128 == column, F32(1.0), F32(0.0)
        ).astype(BF16)

    gather_end(g1, ag1_ss, ag1_rs)

    unfold = fold_matrix()

    @pl.loop(0, 4)
    def _(i):
        tables = []
        for j in range(4):
            block = dot(unfold, g1[i // 2, (i % 2) * 4 + j])
            features = jnp.concatenate([block[0:32], block[32:64], block[64:96]], axis=1)
            normed, _, shifted = normalise(features, gain, bias)
            rows = pl.ds(pl.multiple_of(i * 128 + j * 32, 32), 32)
            normed_all[rows, :] = normed
            shifted_all[rows, :] = shifted
            tables.append(block[96:128])
        table = jnp.concatenate(tables, axis=0)
        xt[:, pl.ds(pl.multiple_of(i * 128, 128), 128)] = table.T

    @pl.loop(0, 4)
    def _(i):
        rows = pl.ds(pl.multiple_of(i * 128, 128), 128)
        unit, _ = unit_rows(dot(shifted_all[rows, :], proj_ref[...]))
        query_half[rows, :] = unit.astype(BF16)

    high = xt[128:129, :].astype(jnp.int32)
    low = xt[129:130, :].astype(jnp.int32)
    lane = xt[130:131, :].astype(jnp.int32)
    slot = lax.rem(high * 8 + low + 256 * c, 512)
    choose = jnp.where(iota((512, 512), 0) == slot, F32(1.0), F32(0.0)).astype(BF16)
    found = dot(xt[0:128, :].astype(BF16), choose)
    where_row = iota((128, 512), 0)
    target = jnp.sum(
        jnp.where(where_row == lane, found * 128.0, F32(0.0))
        + jnp.where(where_row == lane + 64, found, F32(0.0)),
        axis=0, keepdims=True,
    )
    own_ids = jnp.broadcast_to(ids_ref[...].astype(F32), (128, SLAB)).T[:, 0:1]

    totals, positives = [], []
    for i in range(4):
        cols = slice(i * 128, i * 128 + 128)
        e = jnp.exp(64.0 * dot_cols(key_half[...], query_half[cols, :]))
        p = jnp.where(own_ids == target[:, cols], e, F32(0.0))
        expo[:, cols] = e
        pexpo[:, cols] = p
        totals.append(jnp.sum(e, axis=0, keepdims=True))
        positives.append(jnp.sum(p, axis=0, keepdims=True))
    mine = jnp.concatenate(totals + positives, axis=0)
    stat_send[0] = jnp.concatenate(
        [totals[2], totals[3], totals[0], totals[1],
         positives[2], positives[3], positives[0], positives[1]], axis=0
    )

    send(stat_send.at[0], stat_core, st_ss.at[0], st_rs.at[0], partner)
    arrived(stat_core, st_rs.at[0])
    mine = mine + stat_core[...]
    stat_a[a] = mine
    for k in ORDER:
        send(stat_a.at[a], stat_a.at[a], st_ss.at[k], st_rs.at[k], on_a(k)[1])
    for k in ORDER:
        arrived(stat_a.at[on_a(NA - k)[0]], st_rs.at[k])
    stat_b[b] = jnp.sum(stat_a[...], axis=0)
    for k in ORDER:
        send(stat_b.at[b], stat_b.at[b], st_ss.at[8 + k], st_rs.at[8 + k], on_b(k)[1])
    for k in ORDER:
        arrived(stat_b.at[on_b(NA - k)[0]], st_rs.at[8 + k])
    factors = 64.0 / jnp.sum(stat_b[...], axis=0)

    for i in (2, 3, 0, 1):
        cols = slice(i * 128, i * 128 + 128)
        weights[:, cols] = (
            expo[:, cols] * factors[i:i + 1, :] - pexpo[:, cols] * factors[4 + i:5 + i, :]
        ).astype(BF16)

    q_send[...] = dot_rows(weights[:, 256:512], key_half[...]).astype(BF16)
    send(q_send, q_core, q_ss.at[0], q_rs.at[0], partner)
    q_own[...] = dot_rows(weights[:, 0:256], key_half[...])

    @pl.loop(0, NX)
    def _(i):
        rows = pl.ds(pl.multiple_of(i * 64, 64), 64)
        k_send[i] = dot(weights[rows, :], query_half[...]).astype(BF16)

    for k in XORDER:
        there, device = on_x(k)
        send(k_send.at[there], k_recv.at[x], k_ss.at[k], k_rs.at[k], device)
    k_recv[x] = k_send[x]

    arrived(q_core, q_rs.at[0])

    @pl.loop(0, NA)
    def _(i):
        rows = pl.ds(pl.multiple_of(i * 32, 32), 32)
        qb_send[i] = (q_own[rows, :] + q_core[rows, :].astype(F32)).astype(BF16)

    for k in ORDER:
        there, device = on_b(k)
        send(qb_send.at[there], qb_recv.at[b], q_ss.at[8 + k], q_rs.at[8 + k], device)
    qb_recv[b] = qb_send[b]

    for k in XORDER:
        arrived(k_recv.at[on_x(NX - k)[0]], k_rs.at[k])
    quarter = pl.ds(pl.multiple_of(x * 64, 64), 64)
    key_sum = (
        (k_recv[0].astype(F32) + k_recv[1].astype(F32)) + k_recv[2].astype(F32)
    ) + k_recv[3].astype(F32)
    unit = unit_key[quarter, :]
    krg[x] = (
        (key_sum - unit * jnp.sum(unit * key_sum, axis=1, keepdims=True))
        / key_len[quarter, 0:1]
    ).astype(BF16)
    for k in XORDER:
        send(krg.at[x], krg.at[x], k_ss.at[4 + k], k_rs.at[4 + k], on_x(k)[1])

    for k in ORDER:
        arrived(qb_recv.at[on_b(NA - k)[0]], q_rs.at[8 + k])
    part = qb_recv[0].astype(F32)
    for i in range(1, NA):
        part = part + qb_recv[i].astype(F32)
    part = part.astype(BF16)
    stacked = jnp.concatenate(
        [part[:, 0:256], part[:, 256:512], part[:, 512:768], jnp.zeros((32, 256), BF16)], axis=0
    )
    folded = dot_rows(unfold, stacked).astype(BF16)
    for i in range(NA):
        qa_send[i] = folded[i * 16:i * 16 + 16, :]
    for k in ORDER:
        there, device = on_a(k)
        send(qa_send.at[there], qa_recv.at[a], q_ss.at[k], q_rs.at[k], device)
    qa_recv[a] = qa_send[a]

    for k in XORDER:
        arrived(krg.at[on_x(NX - k)[0]], k_rs.at[4 + k])
    grads = krg[...].reshape(SLAB, D)

    @pl.loop(0, 4)
    def _(i):
        half = i // 2
        cols = pl.ds(pl.multiple_of((3 - i) * 256, 256), 256)
        spread_out = dot(grads, perm[:, cols]).astype(BF16)
        share = dot_rows(spread_out, emb_sel[...])
        rows = pl.ds(pl.multiple_of((3 - i) * 256, 256), 256)
        s_own[rows, :] = share

    s_send[...] = s_own[512:1024, :].astype(BF16)
    send(s_send, s_core, s_ss.at[0], s_rs.at[0], partner)

    for k in ORDER:
        arrived(qa_recv.at[on_a(NA - k)[0]], q_rs.at[k])
    part = qa_recv[0].astype(F32)
    for i in range(1, NA):
        part = part + qa_recv[i].astype(F32)
    four = jnp.concatenate([part[0:4], part[4:8], part[8:12]], axis=1)
    query_sum = jnp.concatenate([four, four, four, four], axis=0)
    unit = own_unit[...]
    qrg = (
        query_sum - unit * jnp.sum(unit * query_sum, axis=1, keepdims=True)
    ) / own_col[1, :, 0:1]
    g2[0, b, pl.ds(pl.multiple_of(a * 16, 16), 16), :] = fold_four(qrg[0:4]).astype(BF16)
    gather_start(g2, ag2_ss, ag2_rs)

    arrived(s_core, s_rs.at[0])
    for i in range(NA):
        rows = slice(i * 64, i * 64 + 64)
        sb_send[i] = (s_own[rows, :] + s_core[rows, :].astype(F32)).astype(BF16)
    for k in ORDER:
        there, device = on_b(k)
        send(sb_send.at[there], sb_recv.at[b], s_ss.at[8 + k], s_rs.at[8 + k], device)
    sb_recv[b] = sb_send[b]

    gather_middle(g2, ag2_ss, ag2_rs)

    shifted_grad = dot_cols(qrg.astype(BF16), proj_ref[...])
    scaled = shifted_grad * gain
    normed = own_norm[...]
    text = (
        scaled
        - jnp.mean(scaled, axis=1, keepdims=True)
        - normed * jnp.mean(scaled * normed, axis=1, keepdims=True)
    ) / own_col[0, :, 0:1]
    text_out[...] = text[0:4]

    for k in ORDER:
        arrived(sb_recv.at[on_b(NA - k)[0]], s_rs.at[8 + k])
    part = sb_recv[0].astype(F32)
    for i in range(1, NA):
        part = part + sb_recv[i].astype(F32)
    for i in range(NA):
        sa_send[i] = part[i * 8:i * 8 + 8, :]
    for k in ORDER:
        there, device = on_a(k)
        send(sa_send.at[there], sa_recv.at[a], s_ss.at[k], s_rs.at[k], device)
    sa_recv[a] = sa_send[a]

    gather_forward(g2, ag2_ss, ag2_rs)

    for k in ORDER:
        arrived(sa_recv.at[on_a(NA - k)[0]], s_rs.at[k])
    s_wide[...] = jnp.zeros((128, 256), F32)
    s_wide[0:8, :] = jnp.sum(sa_recv[...], axis=0)
    adapter_out[...] = s_wide[...].T[0:192, 0:6]

    gather_end(g2, ag2_ss, ag2_rs)

    @pl.loop(0, 4)
    def _(i):
        for j in range(4):
            block = dot(unfold, g2[i // 2, (i % 2) * 4 + j])
            rows = pl.ds(pl.multiple_of(i * 128 + j * 32, 32), 32)
            qrg_all[rows, :] = jnp.concatenate(
                [block[0:32], block[32:64], block[64:96]], axis=1
            ).astype(BF16)

    cols = pl.ds(pl.multiple_of(c * 384, 128), 384)
    half = qrg_all[:, cols]
    for i in range(D // 128):
        band = slice(i * 128, i * 128 + 128)
        p_send[band, :] = dot_rows(shifted_all[:, band], half).astype(BF16)
    for k in XORDER:
        there, device = on_x(k)
        send(p_send.at[pl.ds(pl.multiple_of(there * 192, 64), 192), :], p_recv.at[x],
             p_ss.at[k], p_rs.at[k], device)
    p_recv[x] = p_send[pl.ds(pl.multiple_of(x * 192, 64), 192), :]

    gain_sum = jnp.zeros((1, D), F32)
    bias_sum = jnp.zeros((1, D), F32)
    for i in range(4):
        rows = slice(i * 128, i * 128 + 128)
        grad = dot_cols(qrg_all[rows, :], proj_ref[...])
        gain_sum = gain_sum + jnp.sum(grad * normed_all[rows, :], axis=0, keepdims=True)
        bias_sum = bias_sum + jnp.sum(grad, axis=0, keepdims=True)
    gb_recv[x] = jnp.concatenate([gain_sum, bias_sum, jnp.zeros((6, D), F32)], axis=0)
    for k in XORDER:
        send(gb_recv.at[x], gb_recv.at[x], p_ss.at[4 + k], p_rs.at[4 + k], on_x(k)[1])

    for k in XORDER:
        arrived(p_recv.at[on_x(NX - k)[0]], p_rs.at[k])
    total = (
        (p_recv[0].astype(F32) + p_recv[1].astype(F32)) + p_recv[2].astype(F32)
    ) + p_recv[3].astype(F32)
    p_out[0, x] = total.astype(BF16)
    for k in XORDER:
        send(p_out.at[0, x], p_out.at[0, x], p_ss.at[8 + k], p_rs.at[8 + k], on_x(k)[1])
    send(p_out.at[0, x], p_out.at[1, x], p_ss.at[12], p_rs.at[12], partner)

    for k in XORDER:
        arrived(gb_recv.at[on_x(NX - k)[0]], p_rs.at[4 + k])
    gb_out[...] = jnp.sum(gb_recv[...], axis=0)

    for k in XORDER:
        there = on_x(NX - k)[0]
        arrived(p_out.at[0, there], p_rs.at[8 + k])
        send(p_out.at[0, there], p_out.at[1, there], p_ss.at[12 + k], p_rs.at[12 + k], partner)
    for i in range(NX):
        proj_out[i * 192:i * 192 + 192, cols] = p_out[0, i]
    arrived(p_out.at[1, x], p_rs.at[12])
    for k in XORDER:
        arrived(p_out.at[1, on_x(NX - k)[0]], p_rs.at[12 + k])
    other = pl.ds(pl.multiple_of((1 - c) * 384, 128), 384)
    for i in range(NX):
        proj_out[i * 192:i * 192 + 192, other] = p_out[1, i]

    for copy in pending:
        copy.wait_send()


def message(text_features, slab_ids, positive_rows):
    fold = text_features.reshape(ROWS, 3, 256).transpose(1, 0, 2).reshape(12, 256)
    ids = slab_ids.reshape(ROWS, 64)
    device, inner = positive_rows // 256, positive_rows % 256
    core, y, z = device % 2, device // 16, (device // 2) % 8
    slot = core * 64 + jnp.where(core == 0, y * 8 + z, z * 8 + y)
    row = slot * 4 + inner // 64
    places = jnp.stack([row // 8, row % 8, inner % 64], axis=1)
    rest = jnp.concatenate(
        [ids // 128, ids % 128, places, jnp.zeros((ROWS, 125), jnp.int32)], axis=1
    ).astype(BF16)
    return jnp.concatenate([fold, rest], axis=0)


def shards(
    text_features, norm_gain, norm_bias, projection, image_embeddings, adapter, slab_ids,
    positive_rows,
):
    whole = pl.BlockSpec(memory_space=pltpu.VMEM)
    dma = pltpu.SemaphoreType.DMA
    text_grad, gain_bias, projection_grad, adapter_grad = pl.pallas_call(
        kernel,
        out_shape=(
            jax.ShapeDtypeStruct((ROWS, D), F32),
            jax.ShapeDtypeStruct((8, D), F32),
            jax.ShapeDtypeStruct((D, D), BF16),
            jax.ShapeDtypeStruct((192, 6), F32),
        ),
        in_specs=[whole] * 8,
        out_specs=(whole,) * 4,
        scratch_shapes=[
            pltpu.VMEM((2, NA, 128, 256), BF16),
            pltpu.VMEM((2, NA, 128, 256), BF16),
            pltpu.VMEM((16, D), F32),
            pltpu.VMEM((16, D), F32),
            pltpu.VMEM((2, 16, 128), F32),
            pltpu.VMEM((SLAB, D), F32),
            pltpu.VMEM((SLAB, D), BF16),
            pltpu.VMEM((SLAB, 128), F32),
            pltpu.VMEM((SLAB, 256), BF16),
            pltpu.VMEM((D, 1024), BF16),
            pltpu.VMEM((GROUP, D), F32),
            pltpu.VMEM((GROUP, D), BF16),
            pltpu.VMEM((GROUP, D), BF16),
            pltpu.VMEM((256, GROUP), F32),
            pltpu.VMEM((SLAB, GROUP), F32),
            pltpu.VMEM((SLAB, GROUP), F32),
            pltpu.VMEM((SLAB, GROUP), BF16),
            pltpu.VMEM((1, 8, 128), F32),
            pltpu.VMEM((8, 128), F32),
            pltpu.VMEM((NA, 8, 128), F32),
            pltpu.VMEM((NA, 8, 128), F32),
            pltpu.VMEM((256, D), BF16),
            pltpu.VMEM((256, D), F32),
            pltpu.VMEM((256, D), BF16),
            pltpu.VMEM((NA, 32, D), BF16),
            pltpu.VMEM((NA, 32, D), BF16),
            pltpu.VMEM((NA, 16, 256), BF16),
            pltpu.VMEM((NA, 16, 256), BF16),
            pltpu.VMEM((GROUP, D), BF16),
            pltpu.VMEM((NX, 64, D), BF16),
            pltpu.VMEM((NX, 64, D), BF16),
            pltpu.VMEM((NX, 64, D), BF16),
            pltpu.VMEM((1024, 256), F32),
            pltpu.VMEM((512, 256), BF16),
            pltpu.VMEM((512, 256), BF16),
            pltpu.VMEM((NA, 64, 256), BF16),
            pltpu.VMEM((NA, 64, 256), BF16),
            pltpu.VMEM((NA, 8, 256), F32),
            pltpu.VMEM((NA, 8, 256), F32),
            pltpu.VMEM((128, 256), F32),
            pltpu.VMEM((D, 384), BF16),
            pltpu.VMEM((NX, 192, 384), BF16),
            pltpu.VMEM((2, NX, 192, 384), BF16),
            pltpu.VMEM((NX, 8, D), F32),
            dma((24,)), dma((24,)),
            dma((16,)), dma((16,)),
            dma((16,)), dma((16,)),
            dma((24,)), dma((24,)),
            dma((8,)), dma((8,)),
            dma((16,)), dma((16,)),
            dma((16,)), dma((16,)),
            dma,
        ],
        compiler_params=pltpu.CompilerParams(
            collective_id=0, has_side_effects=True, vmem_limit_bytes=48 * 1024 * 1024
        ),
    )(
        message(text_features, slab_ids, positive_rows),
        text_features,
        norm_gain.reshape(1, D),
        norm_bias.reshape(1, D),
        projection,
        image_embeddings,
        adapter,
        slab_ids.reshape(1, SLAB),
    )
    return text_grad, gain_bias[0], gain_bias[1], projection_grad, adapter_grad


def solution(mesh):
    placed = (
        P(("corpus", "query"), None),
        P(),
        P(),
        P(),
        P("corpus", None),
        P(),
        P("corpus"),
        P(("corpus", "query")),
    )
    return jax.shard_map(
        shards,
        mesh=mesh,
        in_specs=placed,
        out_specs=(P(("corpus", "query"), None), P(), P(), P(), P("query", "corpus")),
        check_vma=False,
    )
```

```python
import functools

import jax
import jax.numpy as jnp
from jax import lax
from jax.experimental import pallas as pl
from jax.experimental.pallas import tpu as pltpu
from jax.sharding import PartitionSpec as P

F32 = jnp.float32
BF16 = jnp.bfloat16
MESH = pl.DeviceIdType.MESH

D = 768
SLAB = 256
ROWS = 4
NA = 8
NX = 4
GROUP = 512
ORDER = (1, 7, 2, 6, 3, 5, 4)
XORDER = (1, 3, 2)


def dot(a, b):
    return jnp.dot(a, b, preferred_element_type=F32)


def dot_rows(a, b):
    return lax.dot_general(a, b, (((0,), (0,)), ((), ())), preferred_element_type=F32)


def dot_cols(a, b):
    return lax.dot_general(a, b, (((1,), (1,)), ((), ())), preferred_element_type=F32)


def iota(shape, axis):
    return lax.broadcasted_iota(jnp.int32, shape, axis)


def fold_matrix():
    row, col = iota((128, 128), 0), iota((128, 128), 1)
    source = ((row // 4) % 8) * 16 + 4 * (row // 32) + row % 4
    return jnp.where(source == col, F32(1.0), F32(0.0)).astype(BF16)


def normalise(features, gain, bias):
    average = jnp.mean(features, axis=1, keepdims=True)
    centred = features - average
    spread = jnp.sqrt(jnp.mean(centred * centred, axis=1, keepdims=True) + 1e-5)
    normed = centred / spread
    return normed, spread, (normed * gain + bias).astype(BF16)


def unit_rows(raw):
    length = jnp.sqrt(jnp.sum(raw * raw, axis=1, keepdims=True) + 1e-6)
    return raw / length, length


def kernel(
    tf_hbm, gain_hbm, bias_hbm, proj_hbm, emb_hbm, adapter_hbm, ids_hbm, rows_hbm,
    text_out, gb_out, proj_out, adapter_out,
    tf_ref, gain_ref, bias_ref, proj_ref, emb_ref, adapter_ref, ids_ref, rows_ref,
    g0, g1, g2, unit_key, key_half, key_len, emb_sel, perm,
    normed_all, shifted_all, query_half, unit_all, len_all, spread_all, xt,
    negs, poss, negs_half, poss_half, weights,
    stat_send, stat_core, stat_a, stat_b,
    q_send, q_own, q_core, qb_send, qb_recv, qa_recv,
    k_send, k_recv, krg, s_own, s_send, s_core, sb_send, sb_recv, sa_send, sa_recv, s_wide,
    p_send, p_recv, p_out, gb_recv,
    ag1_ss, ag1_rs, x_ss, x_rs, st_ss, st_rs, q_ss, q_rs, ag2_ss, ag2_rs, k_ss, k_rs,
    s_ss, s_rs, p_ss, p_rs, in_sem,
):
    corpus = lax.axis_index("corpus")
    x = lax.axis_index("query")
    c = lax.rem(corpus, 2)
    y = corpus // 16
    z = lax.rem(corpus // 2, 8)
    a = z + c * (y - z)
    b = y + c * (z - y)
    step_a = 2 + 14 * c
    step_b = 16 - 14 * c

    def on_a(k):
        place = lax.rem(a + k, NA)
        return place, (place * step_a + b * step_b + c, x)

    def on_b(k):
        place = lax.rem(b + k, NA)
        return place, (a * step_a + place * step_b + c, x)

    def on_x(k):
        place = lax.rem(x + k, NX)
        return place, (corpus, place)

    partner = (corpus + 1 - 2 * c, x)
    pending = []

    def send(src, dst, send_sem, recv_sem, device):
        copy = pltpu.make_async_remote_copy(
            src_ref=src, dst_ref=dst, send_sem=send_sem, recv_sem=recv_sem,
            device_id=device, device_id_type=MESH,
        )
        copy.start()
        pending.append(copy)

    def arrived(dst, recv_sem):
        pltpu.make_async_remote_copy(
            src_ref=dst, dst_ref=dst, send_sem=recv_sem, recv_sem=recv_sem,
            device_id=partner, device_id_type=MESH,
        ).wait_recv()

    barrier = pltpu.get_barrier_semaphore()
    pl.semaphore_signal(barrier, inc=1, device_id=partner, device_id_type=MESH)
    for k in range(1, NA):
        pl.semaphore_signal(barrier, inc=1, device_id=on_a(k)[1], device_id_type=MESH)
        pl.semaphore_signal(barrier, inc=1, device_id=on_b(k)[1], device_id_type=MESH)
    for k in range(1, NX):
        pl.semaphore_signal(barrier, inc=1, device_id=on_x(k)[1], device_id_type=MESH)

    loads = [
        pltpu.make_async_copy(src, dst, in_sem.at[i])
        for i, (src, dst) in enumerate((
            (tf_hbm, tf_ref), (ids_hbm, ids_ref), (rows_hbm, rows_ref), (emb_hbm, emb_ref),
            (adapter_hbm, adapter_ref), (gain_hbm, gain_ref), (bias_hbm, bias_ref),
            (proj_hbm, proj_ref),
        ))
    ]
    for load in loads:
        load.start()

    for load in loads[:3]:
        load.wait()
    id_row = ids_ref[...].reshape(1, SLAB)
    own4 = tf_ref[...].astype(F32)
    row16, col16 = iota((16, SLAB), 0), iota((16, SLAB), 1)
    quarter_ids = jnp.where(col16 // 64 == row16, id_row, 0)
    both = jnp.concatenate([quarter_ids // 128, quarter_ids % 128], axis=1)
    bring = jnp.where(
        iota((512, 128), 1) == iota((512, 128), 0) % 64 + 64 * (iota((512, 128), 0) // 256),
        F32(1.0), F32(0.0),
    ).astype(BF16)
    listed = dot(both.astype(F32).astype(BF16), bring)
    wanted_row = jnp.sum(
        jnp.where(
            iota((16, ROWS), 0) == iota((16, ROWS), 1),
            rows_ref[...].reshape(1, ROWS).astype(F32), F32(0.0),
        ),
        axis=1, keepdims=True,
    ).astype(jnp.int32)
    device, inner = wanted_row // 256, wanted_row % 256
    core, there_y, there_z = device % 2, device // 16, (device // 2) % 8
    slot = core * 64 + jnp.where(core == 0, there_y * 8 + there_z, there_z * 8 + there_y)
    row = slot * 4 + inner // 64
    lane = iota((16, 128), 1)
    places = jnp.where(
        lane == 0, row // 8, jnp.where(lane == 1, row % 8, jnp.where(lane == 2, inner % 64, 0))
    ).astype(F32)
    rest = jnp.concatenate([listed, places], axis=1)
    message = jnp.concatenate(
        [own4[:, :256], own4[:, 256:512], own4[:, 512:], rest[0:4]], axis=0
    ).astype(BF16)
    g0[pl.ds(pl.multiple_of(a * 16, 16), 16), :] = message
    pl.semaphore_wait(barrier, 2 * (NA - 1) + NX)

    own = g0.at[pl.ds(pl.multiple_of(a * 16, 16), 16), :]
    for k in ORDER:
        send(own, own, ag1_ss.at[k], ag1_rs.at[k], on_a(k)[1])

    for load in loads[3:]:
        load.wait()
    gain = gain_ref[...].reshape(1, D)
    bias = bias_ref[...].reshape(1, D)

    @pl.loop(0, SLAB // 128)
    def _(i):
        rows = pl.ds(pl.multiple_of(i * 128, 128), 128)
        unit, length = unit_rows(dot(emb_ref[rows, :], adapter_ref[...]))
        unit_key[rows, :] = unit
        key_half[rows, :] = unit.astype(BF16)
        key_len[rows, :] = jnp.broadcast_to(length, (128, 128))

    for k in ORDER:
        place = on_a(NA - k)[0]
        arrived(g0.at[pl.ds(pl.multiple_of(place * 16, 16), 16), :], ag1_rs.at[k])

    unfold = fold_matrix()
    g1[0, b] = dot(unfold, g0[...]).astype(BF16)
    text_of = lambda region, place: g1.at[region, place, pl.ds(0, 96), :]
    ids_of = lambda region, place: g1.at[region, place, pl.ds(96, 32), :]
    for part, ss, rs in ((text_of, ag1_ss, ag1_rs), (ids_of, x_ss, x_rs)):
        for k in ORDER:
            send(part(0, b), part(0, b), ss.at[8 + k], rs.at[8 + k], on_b(k)[1])
        send(part(0, b), part(1, b), ss.at[16], rs.at[16], partner)

    def forward(part, ss, rs, k):
        place = on_b(NA - k)[0]
        arrived(part(0, place), rs.at[8 + k])
        send(part(0, place), part(1, place), ss.at[16 + k], rs.at[16 + k], partner)

    def from_core(k):
        return lax.rem(a + NA - k, NA) if k else a

    def query_block(region, places):
        shifts = []
        for place in places:
            block = g1[region, place, 0:96, :].astype(F32)
            features = jnp.concatenate([block[0:32], block[32:64], block[64:96]], axis=1)
            normed, spread, shifted = normalise(features, gain, bias)
            rows = pl.ds(pl.multiple_of(region * 256 + place * 32, 32), 32)
            normed_all[rows, :] = normed
            shifted_all[rows, :] = shifted
            if region == 0:
                spread_all[rows, :] = jnp.broadcast_to(spread, (32, 128))
            shifts.append(shifted)
        unit, length = unit_rows(dot(jnp.concatenate(shifts, axis=0), proj_ref[...]))
        for i, place in enumerate(places):
            rows = pl.ds(pl.multiple_of(region * 256 + place * 32, 32), 32)
            piece = slice(i * 32, i * 32 + 32)
            query_half[rows, :] = unit[piece].astype(BF16)
            if region == 0:
                unit_all[rows, :] = unit[piece]
                len_all[rows, :] = jnp.broadcast_to(length[piece], (32, 128))

    near, far = ORDER[:3], ORDER[3:]
    for k in near:
        forward(text_of, ag1_ss, ag1_rs, k)
    query_block(0, [b] + [on_b(NA - k)[0] for k in near])
    for k in (0,) + near:
        arrived(text_of(1, from_core(k)), ag1_rs.at[16 + k])
    query_block(1, [from_core(k) for k in (0,) + near])
    for k in far:
        forward(text_of, ag1_ss, ag1_rs, k)
    query_block(0, [on_b(NA - k)[0] for k in far])
    for k in ORDER:
        forward(ids_of, x_ss, x_rs, k)
    for k in far:
        arrived(text_of(1, from_core(k)), ag1_rs.at[16 + k])
    query_block(1, [from_core(k) for k in far])
    for k in (0,) + ORDER:
        arrived(ids_of(1, from_core(k)), x_rs.at[16 + k])

    for region in range(2):
        for i in range(2):
            table = jnp.concatenate(
                [g1[region, i * 4 + j, 96:128, :] for j in range(4)], axis=0
            ).astype(F32)
            first = region * 256 + i * 128
            xt[:, first:first + 128] = table.T

    high = xt[128:129, :].astype(jnp.int32)
    low = xt[129:130, :].astype(jnp.int32)
    lane = xt[130:131, :].astype(jnp.int32)
    slot = lax.rem(high * 8 + low + 256 * c, 512)
    choose = jnp.where(iota((512, 512), 0) == slot, F32(1.0), F32(0.0)).astype(BF16)
    found = dot(xt[0:128, :].astype(BF16), choose)
    where_row = iota((128, 512), 0)
    target = jnp.sum(
        jnp.where(where_row == lane, found * 128.0, F32(0.0))
        + jnp.where(where_row == lane + 64, found, F32(0.0)),
        axis=0, keepdims=True,
    )
    own_ids = jnp.broadcast_to(id_row.astype(F32), (128, SLAB)).T[:, 0:1]

    negatives, positives = [], []
    for i in range(4):
        cols = slice(i * 128, i * 128 + 128)
        e = jnp.exp(64.0 * dot_cols(key_half[...], query_half[cols, :]))
        hit = own_ids == target[:, cols]
        n = jnp.where(hit, F32(0.0), e)
        p = jnp.where(hit, e, F32(0.0))
        negs[:, cols] = n
        poss[:, cols] = p
        negs_half[:, cols] = n.astype(BF16)
        poss_half[:, cols] = p.astype(BF16)
        negatives.append(jnp.sum(n, axis=0, keepdims=True))
        positives.append(jnp.sum(p, axis=0, keepdims=True))
    mine = jnp.concatenate(negatives + positives, axis=0)
    stat_send[0] = jnp.concatenate(
        [negatives[2], negatives[3], negatives[0], negatives[1],
         positives[2], positives[3], positives[0], positives[1]], axis=0
    )

    send(stat_send.at[0], stat_core, st_ss.at[0], st_rs.at[0], partner)
    for part, half in enumerate((negs_half, poss_half)):
        q_send[part] = dot_rows(half[:, 256:512], key_half[...]).astype(BF16)
        send(q_send.at[part], q_core.at[part], q_ss.at[part], q_rs.at[part], partner)

    arrived(stat_core, st_rs.at[0])
    mine = mine + stat_core[...]
    stat_a[a] = mine
    for k in ORDER:
        send(stat_a.at[a], stat_a.at[a], st_ss.at[k], st_rs.at[k], on_a(k)[1])

    for part, half in enumerate((negs_half, poss_half)):
        q_own[part] = dot_rows(half[:, 0:256], key_half[...])
    for part in range(2):
        arrived(q_core.at[part], q_rs.at[part])

    @pl.loop(0, NA)
    def _(i):
        rows = pl.ds(pl.multiple_of(i * 32, 32), 32)
        for part in range(2):
            qb_send[i, part] = (
                q_own[part, rows, :] + q_core[part, rows, :].astype(F32)
            ).astype(BF16)

    for k in ORDER:
        there, device = on_b(k)
        send(qb_send.at[there], qb_recv.at[b], q_ss.at[8 + k], q_rs.at[8 + k], device)
    qb_recv[b] = qb_send[b]

    for k in ORDER:
        arrived(stat_a.at[on_a(NA - k)[0]], st_rs.at[k])
    stat_b[b] = jnp.sum(stat_a[...], axis=0)
    for k in ORDER:
        send(stat_b.at[b], stat_b.at[b], st_ss.at[8 + k], st_rs.at[8 + k], on_b(k)[1])

    pick = jnp.where(
        (iota((D, 256), 0) == iota((D, 256), 1) + x * 192) & (iota((D, 256), 1) < 192),
        F32(1.0), F32(0.0),
    ).astype(BF16)
    emb_sel[...] = dot(emb_ref[...], pick).astype(BF16)
    place = iota((1, 1024), 1)
    core = lax.rem(place // 512 + c, 2)
    place_b, place_a = (place // 64) % 8, (place // 8) % 8
    place_y = jnp.where(core == 0, place_b, place_a)
    place_z = place_a + place_b - place_y
    column = jnp.where(
        place % 8 < 6, 6 * (place_y * 16 + place_z * 2 + core) + place % 8, -1
    )

    @pl.loop(0, D // 128)
    def _(i):
        rows = pl.ds(pl.multiple_of(i * 128, 128), 128)
        perm[rows, :] = jnp.where(
            iota((128, 1024), 0) + i * 128 == column, F32(1.0), F32(0.0)
        ).astype(BF16)

    for k in ORDER:
        arrived(stat_b.at[on_b(NA - k)[0]], st_rs.at[8 + k])
    stats = jnp.sum(stat_b[...], axis=0)
    by_total = 64.0 / (stats[0:4] + stats[4:8])
    by_positive = 1.0 / stats[4:8]
    share_negative = stats[0:4] * by_total

    for i in range(4):
        cols = slice(i * 128, i * 128 + 128)
        weights[:, cols] = (
            negs[:, cols] * by_total[i:i + 1, :]
            - (poss[:, cols] * by_positive[i:i + 1, :]) * share_negative[i:i + 1, :]
        ).astype(BF16)

    @pl.loop(0, NX)
    def _(i):
        rows = pl.ds(pl.multiple_of(i * 64, 64), 64)
        k_send[i] = dot(weights[rows, :], query_half[...]).astype(BF16)

    for k in XORDER:
        there, device = on_x(k)
        send(k_send.at[there], k_recv.at[x], k_ss.at[k], k_rs.at[k], device)
    k_recv[x] = k_send[x]

    diagonal = iota((32, SLAB), 1) == iota((32, SLAB), 0) + b * 32

    def as_column(rows):
        wide = jnp.concatenate([rows[0:1], rows[1:2]], axis=1)
        return jnp.sum(jnp.where(diagonal, wide, F32(0.0)), axis=1, keepdims=True)

    for k in ORDER:
        arrived(qb_recv.at[on_b(NA - k)[0]], q_rs.at[8 + k])
    sums = []
    for part in range(2):
        total = qb_recv[0, part].astype(F32)
        for i in range(1, NA):
            total = total + qb_recv[i, part].astype(F32)
        sums.append(total)
    qa_recv[a] = (
        sums[0] * as_column(by_total)
        - (sums[1] * as_column(by_positive)) * as_column(share_negative)
    ).astype(BF16)
    for k in ORDER:
        send(qa_recv.at[a], qa_recv.at[a], q_ss.at[16 + k], q_rs.at[16 + k], on_a(k)[1])

    for k in XORDER:
        arrived(k_recv.at[on_x(NX - k)[0]], k_rs.at[k])
    quarter = pl.ds(pl.multiple_of(x * 64, 64), 64)
    key_sum = (
        (k_recv[0].astype(F32) + k_recv[1].astype(F32)) + k_recv[2].astype(F32)
    ) + k_recv[3].astype(F32)
    unit = unit_key[quarter, :]
    krg[x] = (
        (key_sum - unit * jnp.sum(unit * key_sum, axis=1, keepdims=True))
        / key_len[quarter, 0:1]
    ).astype(BF16)
    for k in XORDER:
        send(krg.at[x], krg.at[x], k_ss.at[4 + k], k_rs.at[4 + k], on_x(k)[1])

    for k in XORDER:
        arrived(krg.at[on_x(NX - k)[0]], k_rs.at[4 + k])
    grads = krg[...].reshape(SLAB, D)

    @pl.loop(0, 4)
    def _(i):
        half = i // 2
        cols = pl.ds(pl.multiple_of((3 - i) * 256, 256), 256)
        spread_out = dot(grads, perm[:, cols]).astype(BF16)
        share = dot_rows(spread_out, emb_sel[...])
        rows = pl.ds(pl.multiple_of((3 - i) * 256, 256), 256)
        s_own[rows, :] = share

    s_send[...] = s_own[512:1024, :].astype(BF16)
    send(s_send, s_core, s_ss.at[0], s_rs.at[0], partner)

    for k in ORDER:
        arrived(qa_recv.at[on_a(NA - k)[0]], q_rs.at[16 + k])
    query_sum = qa_recv[0].astype(F32)
    for i in range(1, NA):
        query_sum = query_sum + qa_recv[i].astype(F32)
    block = pl.ds(pl.multiple_of(b * 32, 32), 32)
    unit = unit_all[block, :]
    qrg = (
        (query_sum - unit * jnp.sum(unit * query_sum, axis=1, keepdims=True))
        / len_all[block, 0:1]
    ).astype(BF16)
    g2[0, b] = qrg
    for k in ORDER:
        send(g2.at[0, b], g2.at[0, b], ag2_ss.at[k], ag2_rs.at[k], on_b(k)[1])
    send(g2.at[0, b], g2.at[1, b], ag2_ss.at[8], ag2_rs.at[8], partner)

    arrived(s_core, s_rs.at[0])
    for i in range(NA):
        rows = slice(i * 64, i * 64 + 64)
        sb_send[i] = (s_own[rows, :] + s_core[rows, :].astype(F32)).astype(BF16)
    for k in ORDER:
        there, device = on_b(k)
        send(sb_send.at[there], sb_recv.at[b], s_ss.at[8 + k], s_rs.at[8 + k], device)
    sb_recv[b] = sb_send[b]

    shifted_grad = dot_cols(qrg, proj_ref[...])
    scaled = shifted_grad * gain
    normed = normed_all[block, :]
    text = (
        scaled
        - jnp.mean(scaled, axis=1, keepdims=True)
        - normed * jnp.mean(scaled * normed, axis=1, keepdims=True)
    ) / spread_all[block, 0:1]
    own_text = text[0:4]
    for i in range(1, NA):
        own_text = jnp.where(a == i, text[i * 4:i * 4 + 4], own_text)
    text_out[...] = own_text

    for k in ORDER:
        arrived(sb_recv.at[on_b(NA - k)[0]], s_rs.at[8 + k])
    part = sb_recv[0].astype(F32)
    for i in range(1, NA):
        part = part + sb_recv[i].astype(F32)
    for i in range(NA):
        sa_send[i] = part[i * 8:i * 8 + 8, :]
    for k in ORDER:
        there, device = on_a(k)
        send(sa_send.at[there], sa_recv.at[a], s_ss.at[k], s_rs.at[k], device)
    sa_recv[a] = sa_send[a]

    for k in ORDER:
        place = on_b(NA - k)[0]
        arrived(g2.at[0, place], ag2_rs.at[k])
        send(g2.at[0, place], g2.at[1, place], ag2_ss.at[8 + k], ag2_rs.at[8 + k], partner)

    for k in ORDER:
        arrived(sa_recv.at[on_a(NA - k)[0]], s_rs.at[k])
    s_wide[...] = jnp.zeros((128, 256), F32)
    s_wide[0:8, :] = jnp.sum(sa_recv[...], axis=0)
    adapter_out[...] = s_wide[...].T[0:192, 0:6]

    for k in (0,) + ORDER:
        arrived(g2.at[1, from_core(k)], ag2_rs.at[8 + k])

    cols = pl.ds(pl.multiple_of(c * 384, 128), 384)
    half = g2[:, :, :, cols].reshape(GROUP, 384)
    for i in range(D // 128):
        band = slice(i * 128, i * 128 + 128)
        p_send[band, :] = dot_rows(shifted_all[:, band], half).astype(BF16)
    for h in range(2):
        for k in XORDER:
            there, device = on_x(k)
            send(p_send.at[pl.ds(pl.multiple_of(there * 192 + h * 96, 32), 96), :],
                 p_recv.at[h, x], p_ss.at[4 * h + k], p_rs.at[4 * h + k], device)
        p_recv[h, x] = p_send[pl.ds(pl.multiple_of(x * 192 + h * 96, 32), 96), :]

    gain_sum = jnp.zeros((1, D), F32)
    bias_sum = jnp.zeros((1, D), F32)
    for i in range(4):
        rows = slice(i * 128, i * 128 + 128)
        quads = slice(i % 2 * 4, i % 2 * 4 + 4)
        grad = dot_cols(g2[i // 2, quads].reshape(128, D), proj_ref[...])
        gain_sum = gain_sum + jnp.sum(grad * normed_all[rows, :], axis=0, keepdims=True)
        bias_sum = bias_sum + jnp.sum(grad, axis=0, keepdims=True)
    gb_recv[x] = jnp.concatenate([gain_sum, bias_sum, jnp.zeros((6, D), F32)], axis=0)
    for k in XORDER:
        send(gb_recv.at[x], gb_recv.at[x], p_ss.at[8 + k], p_rs.at[8 + k], on_x(k)[1])

    for h in range(2):
        for k in XORDER:
            arrived(p_recv.at[h, on_x(NX - k)[0]], p_rs.at[4 * h + k])
        total = (
            (p_recv[h, 0].astype(F32) + p_recv[h, 1].astype(F32)) + p_recv[h, 2].astype(F32)
        ) + p_recv[h, 3].astype(F32)
        p_out[0, x, h] = total.astype(BF16)
        for k in XORDER:
            send(p_out.at[0, x, h], p_out.at[0, x, h],
                 p_ss.at[12 + 4 * h + k], p_rs.at[12 + 4 * h + k], on_x(k)[1])
        send(p_out.at[0, x, h], p_out.at[1, x, h], p_ss.at[20 + 4 * h], p_rs.at[20 + 4 * h], partner)

    for k in XORDER:
        arrived(gb_recv.at[on_x(NX - k)[0]], p_rs.at[8 + k])
    gb_out[...] = jnp.sum(gb_recv[...], axis=0)

    for h in range(2):
        for k in XORDER:
            there = on_x(NX - k)[0]
            arrived(p_out.at[0, there, h], p_rs.at[12 + 4 * h + k])
            send(p_out.at[0, there, h], p_out.at[1, there, h],
                 p_ss.at[20 + 4 * h + k], p_rs.at[20 + 4 * h + k], partner)
    for i in range(NX):
        proj_out[i * 192:i * 192 + 192, cols] = p_out[0, i].reshape(192, 384)
    other = pl.ds(pl.multiple_of((1 - c) * 384, 128), 384)
    for h in range(2):
        arrived(p_out.at[1, x, h], p_rs.at[20 + 4 * h])
        for k in XORDER:
            arrived(p_out.at[1, on_x(NX - k)[0], h], p_rs.at[20 + 4 * h + k])
    for i in range(NX):
        proj_out[i * 192:i * 192 + 192, other] = p_out[1, i].reshape(192, 384)

    for copy in pending:
        copy.wait_send()


def shards(
    text_features, norm_gain, norm_bias, projection, image_embeddings, adapter, slab_ids,
    positive_rows,
):
    whole = pl.BlockSpec(memory_space=pltpu.VMEM)
    dma = pltpu.SemaphoreType.DMA
    text_grad, gain_bias, projection_grad, adapter_grad = pl.pallas_call(
        kernel,
        out_shape=(
            jax.ShapeDtypeStruct((ROWS, D), F32),
            jax.ShapeDtypeStruct((8, D), F32),
            jax.ShapeDtypeStruct((D, D), BF16),
            jax.ShapeDtypeStruct((192, 6), F32),
        ),
        in_specs=[pl.BlockSpec(memory_space=pl.ANY)] * 8,
        out_specs=(whole,) * 4,
        scratch_shapes=[
            pltpu.VMEM((ROWS, D), BF16),
            pltpu.VMEM((D,), F32),
            pltpu.VMEM((D,), F32),
            pltpu.VMEM((D, D), BF16),
            pltpu.VMEM((SLAB, D), BF16),
            pltpu.VMEM((D, D), BF16),
            pltpu.VMEM((SLAB,), jnp.int32),
            pltpu.VMEM((ROWS,), jnp.int32),
            pltpu.VMEM((128, 256), BF16),
            pltpu.VMEM((2, NA, 128, 256), BF16),
            pltpu.VMEM((2, NA, 32, D), BF16),
            pltpu.VMEM((SLAB, D), F32),
            pltpu.VMEM((SLAB, D), BF16),
            pltpu.VMEM((SLAB, 128), F32),
            pltpu.VMEM((SLAB, 256), BF16),
            pltpu.VMEM((D, 1024), BF16),
            pltpu.VMEM((GROUP, D), F32),
            pltpu.VMEM((GROUP, D), BF16),
            pltpu.VMEM((GROUP, D), BF16),
            pltpu.VMEM((GROUP // 2, D), F32),
            pltpu.VMEM((GROUP // 2, 128), F32),
            pltpu.VMEM((GROUP // 2, 128), F32),
            pltpu.VMEM((256, GROUP), F32),
            pltpu.VMEM((SLAB, GROUP), F32),
            pltpu.VMEM((SLAB, GROUP), F32),
            pltpu.VMEM((SLAB, GROUP), BF16),
            pltpu.VMEM((SLAB, GROUP), BF16),
            pltpu.VMEM((SLAB, GROUP), BF16),
            pltpu.VMEM((1, 8, 128), F32),
            pltpu.VMEM((8, 128), F32),
            pltpu.VMEM((NA, 8, 128), F32),
            pltpu.VMEM((NA, 8, 128), F32),
            pltpu.VMEM((2, 256, D), BF16),
            pltpu.VMEM((2, 256, D), F32),
            pltpu.VMEM((2, 256, D), BF16),
            pltpu.VMEM((NA, 2, 32, D), BF16),
            pltpu.VMEM((NA, 2, 32, D), BF16),
            pltpu.VMEM((NA, 32, D), BF16),
            pltpu.VMEM((NX, 64, D), BF16),
            pltpu.VMEM((NX, 64, D), BF16),
            pltpu.VMEM((NX, 64, D), BF16),
            pltpu.VMEM((1024, 256), F32),
            pltpu.VMEM((512, 256), BF16),
            pltpu.VMEM((512, 256), BF16),
            pltpu.VMEM((NA, 64, 256), BF16),
            pltpu.VMEM((NA, 64, 256), BF16),
            pltpu.VMEM((NA, 8, 256), F32),
            pltpu.VMEM((NA, 8, 256), F32),
            pltpu.VMEM((128, 256), F32),
            pltpu.VMEM((D, 384), BF16),
            pltpu.VMEM((2, NX, 96, 384), BF16),
            pltpu.VMEM((2, NX, 2, 96, 384), BF16),
            pltpu.VMEM((NX, 8, D), F32),
            dma((24,)), dma((24,)),
            dma((24,)), dma((24,)),
            dma((16,)), dma((16,)),
            dma((24,)), dma((24,)),
            dma((16,)), dma((16,)),
            dma((8,)), dma((8,)),
            dma((16,)), dma((16,)),
            dma((28,)), dma((28,)),
            dma((8,)),
        ],
        compiler_params=pltpu.CompilerParams(
            collective_id=0, has_side_effects=True, vmem_limit_bytes=48 * 1024 * 1024
        ),
    )(
        text_features,
        norm_gain,
        norm_bias,
        projection,
        image_embeddings,
        adapter,
        slab_ids,
        positive_rows,
    )
    return text_grad, gain_bias[0], gain_bias[1], projection_grad, adapter_grad


def solution(mesh):
    placed = (
        P(("corpus", "query"), None),
        P(),
        P(),
        P(),
        P("corpus", None),
        P(),
        P("corpus"),
        P(("corpus", "query")),
    )
    return jax.shard_map(
        shards,
        mesh=mesh,
        in_specs=placed,
        out_specs=(P(("corpus", "query"), None), P(), P(), P(), P("query", "corpus")),
        check_vma=False,
    )
```

```python
import functools

import jax
import jax.numpy as jnp
from jax import lax
from jax.experimental import pallas as pl
from jax.experimental.pallas import tpu as pltpu
from jax.sharding import PartitionSpec as P

F32 = jnp.float32
BF16 = jnp.bfloat16
MESH = pl.DeviceIdType.MESH

D = 768
SLAB = 256
ROWS = 4
NA = 8
NX = 4
GROUP = 512
ORDER = (1, 7, 2, 6, 3, 5, 4)
XORDER = (1, 3, 2)


def dot(a, b):
    return jnp.dot(a, b, preferred_element_type=F32)


def dot_rows(a, b):
    return lax.dot_general(a, b, (((0,), (0,)), ((), ())), preferred_element_type=F32)


def dot_cols(a, b):
    return lax.dot_general(a, b, (((1,), (1,)), ((), ())), preferred_element_type=F32)


def iota(shape, axis):
    return lax.broadcasted_iota(jnp.int32, shape, axis)


def spread_matrix():
    row, col = iota((32, 128), 0), iota((32, 128), 1)
    return jnp.where((row >> 2) * 16 + (row & 3) == col, F32(1.0), F32(0.0)).astype(BF16)


def normalise(features, gain, bias):
    average = jnp.mean(features, axis=1, keepdims=True)
    centred = features - average
    spread = jnp.sqrt(jnp.mean(centred * centred, axis=1, keepdims=True) + 1e-5)
    normed = centred * (1.0 / spread)
    return normed, spread, (normed * gain + bias).astype(BF16)


def unit_rows(raw):
    length = jnp.sqrt(jnp.sum(raw * raw, axis=1, keepdims=True) + 1e-6)
    return raw * (1.0 / length), length


def kernel(
    tf_hbm, gain_hbm, bias_hbm, proj_hbm, emb_hbm, adapter_hbm, ids_hbm, rows_hbm,
    small_out, proj_out,
    tf_ref, gain_ref, bias_ref, proj_ref, emb_ref, adapter_ref, ids_ref, rows_ref,
    gt, g0, g1, gx, g2, unit_key, key_half, key_len, emb_sel, perm,
    normed_all, shifted_all, query_half, unit_all, len_all, spread_all, xt,
    negs, poss, negs_half, poss_half, weights,
    stat_send, stat_core, stat_a, stat_b,
    q_send, q_own, q_core, qb_send, qb_recv, qa_recv,
    k_send, k_recv, krg, s_own, s_send, s_core, sb_send, sb_recv, sa_send, sa_recv,
    p_send, p_recv, p_out, gb_recv,
    ag1_ss, ag1_rs, x_ss, x_rs, st_ss, st_rs, q_ss, q_rs, ag2_ss, ag2_rs, k_ss, k_rs,
    s_ss, s_rs, p_ss, p_rs, in_sem,
):
    corpus = lax.axis_index("corpus")
    x = lax.axis_index("query")
    c = lax.rem(corpus, 2)
    y = corpus // 16
    z = lax.rem(corpus // 2, 8)
    a = z + c * (y - z)
    b = y + c * (z - y)
    step_a = 2 + 14 * c
    step_b = 16 - 14 * c

    def on_a(k):
        place = lax.rem(a + k, NA)
        return place, (place * step_a + b * step_b + c, x)

    def on_b(k):
        place = lax.rem(b + k, NA)
        return place, (a * step_a + place * step_b + c, x)

    def on_x(k):
        place = lax.rem(x + k, NX)
        return place, (corpus, place)

    partner = (corpus + 1 - 2 * c, x)
    pending = []

    def send(src, dst, send_sem, recv_sem, device):
        copy = pltpu.make_async_remote_copy(
            src_ref=src, dst_ref=dst, send_sem=send_sem, recv_sem=recv_sem,
            device_id=device, device_id_type=MESH,
        )
        copy.start()
        pending.append(copy)

    def arrived(dst, recv_sem):
        pltpu.make_async_remote_copy(
            src_ref=dst, dst_ref=dst, send_sem=recv_sem, recv_sem=recv_sem,
            device_id=partner, device_id_type=MESH,
        ).wait_recv()

    barrier = pltpu.get_barrier_semaphore()
    pl.semaphore_signal(barrier, inc=1, device_id=partner, device_id_type=MESH)
    for k in range(1, NA):
        pl.semaphore_signal(barrier, inc=1, device_id=on_a(k)[1], device_id_type=MESH)
        pl.semaphore_signal(barrier, inc=1, device_id=on_b(k)[1], device_id_type=MESH)
    for k in range(1, NX):
        pl.semaphore_signal(barrier, inc=1, device_id=on_x(k)[1], device_id_type=MESH)

    loads = [
        pltpu.make_async_copy(src, dst, in_sem.at[i])
        for i, (src, dst) in enumerate((
            (tf_hbm, tf_ref), (ids_hbm, ids_ref), (rows_hbm, rows_ref), (emb_hbm, emb_ref),
            (adapter_hbm, adapter_ref), (gain_hbm, gain_ref), (bias_hbm, bias_ref),
            (proj_hbm, proj_ref),
        ))
    ]
    for load in loads:
        load.start()

    loads[0].wait()
    gt[a] = tf_ref[...]
    pl.semaphore_wait(barrier, 2 * (NA - 1) + NX)
    for k in ORDER:
        send(gt.at[a], gt.at[a], ag1_ss.at[k], ag1_rs.at[k], on_a(k)[1])

    for load in loads[1:3]:
        load.wait()
    id_row = ids_ref[...].reshape(1, SLAB)
    row16, col16 = iota((16, SLAB), 0), iota((16, SLAB), 1)
    quarter_ids = jnp.where(col16 >> 6 == row16, id_row, 0)
    both = jnp.concatenate([quarter_ids >> 7, quarter_ids & 127], axis=1)
    bring = jnp.where(
        iota((512, 128), 1) == (iota((512, 128), 0) & 63) + 64 * (iota((512, 128), 0) >> 8),
        F32(1.0), F32(0.0),
    ).astype(BF16)
    listed = dot(both.astype(F32).astype(BF16), bring)
    wanted_row = jnp.sum(
        jnp.where(
            iota((16, ROWS), 0) == iota((16, ROWS), 1),
            rows_ref[...].reshape(1, ROWS).astype(F32), F32(0.0),
        ),
        axis=1, keepdims=True,
    ).astype(jnp.int32)
    device, inner = wanted_row >> 8, wanted_row & 255
    core, there_y, there_z = device & 1, device >> 4, (device >> 1) & 7
    slot = core * 64 + jnp.where(core == 0, there_y * 8 + there_z, there_z * 8 + there_y)
    row = slot * 4 + (inner >> 6)
    lane = iota((16, 128), 1)
    places = jnp.where(
        lane == 0, row >> 3, jnp.where(lane == 1, row & 7, jnp.where(lane == 2, inner & 63, 0))
    ).astype(F32)
    rest = jnp.concatenate([listed, places], axis=1)
    own = g0.at[pl.ds(pl.multiple_of(a * 16, 16), 16), :]
    g0[pl.ds(pl.multiple_of(a * 16, 16), 16), :] = rest.astype(BF16)
    for k in ORDER:
        send(own, own, x_ss.at[k], x_rs.at[k], on_a(k)[1])

    for load in loads[3:]:
        load.wait()
    gain = gain_ref[...].reshape(1, D)
    bias = bias_ref[...].reshape(1, D)

    @pl.loop(0, SLAB // 128)
    def _(i):
        rows = pl.ds(pl.multiple_of(i * 128, 128), 128)
        unit, length = unit_rows(dot(emb_ref[rows, :], adapter_ref[...]))
        unit_key[rows, :] = unit
        key_half[rows, :] = unit.astype(BF16)
        key_len[rows, :] = jnp.broadcast_to(length, (128, 128))

    for k in ORDER:
        arrived(gt.at[on_a(NA - k)[0]], ag1_rs.at[k])

    def widen(g, ss, rs):
        for k in ORDER:
            send(g.at[0, b], g.at[0, b], ss.at[8 + k], rs.at[8 + k], on_b(k)[1])
        send(g.at[0, b], g.at[1, b], ss.at[16], rs.at[16], partner)

    g1[0, b] = jnp.concatenate([gt[i].astype(F32) for i in range(NA)], axis=0).astype(BF16)
    widen(g1, ag1_ss, ag1_rs)
    for k in ORDER:
        place = on_a(NA - k)[0]
        arrived(g0.at[pl.ds(pl.multiple_of(place * 16, 16), 16), :], x_rs.at[k])
    gx[0, b] = dot(spread_matrix(), g0[...]).astype(BF16)
    widen(gx, x_ss, x_rs)

    def forward(g, ss, rs, k):
        place = on_b(NA - k)[0]
        arrived(g.at[0, place], rs.at[8 + k])
        send(g.at[0, place], g.at[1, place], ss.at[16 + k], rs.at[16 + k], partner)

    def from_core(k):
        return lax.rem(a + NA - k, NA) if k else a

    def query_block(region, places):
        shifts = []
        for place in places:
            normed, spread, shifted = normalise(g1[region, place].astype(F32), gain, bias)
            rows = pl.ds(pl.multiple_of(region * 256 + place * 32, 32), 32)
            normed_all[rows, :] = normed
            shifted_all[rows, :] = shifted
            if region == 0:
                spread_all[rows, :] = jnp.broadcast_to(spread, (32, 128))
            shifts.append(shifted)
        unit, length = unit_rows(dot(jnp.concatenate(shifts, axis=0), proj_ref[...]))
        for i, place in enumerate(places):
            rows = pl.ds(pl.multiple_of(region * 256 + place * 32, 32), 32)
            piece = slice(i * 32, i * 32 + 32)
            query_half[rows, :] = unit[piece].astype(BF16)
            if region == 0:
                unit_all[rows, :] = unit[piece]
                len_all[rows, :] = jnp.broadcast_to(length[piece], (32, 128))

    near, far = ORDER[:3], ORDER[3:]
    for k in near:
        forward(g1, ag1_ss, ag1_rs, k)
    query_block(0, [b] + [on_b(NA - k)[0] for k in near])
    for k in (0,) + near:
        arrived(g1.at[1, from_core(k)], ag1_rs.at[16 + k])
    query_block(1, [from_core(k) for k in (0,) + near])
    for k in far:
        forward(g1, ag1_ss, ag1_rs, k)
    query_block(0, [on_b(NA - k)[0] for k in far])
    for k in ORDER:
        forward(gx, x_ss, x_rs, k)
    for k in far:
        arrived(g1.at[1, from_core(k)], ag1_rs.at[16 + k])
    query_block(1, [from_core(k) for k in far])
    for k in (0,) + ORDER:
        arrived(gx.at[1, from_core(k)], x_rs.at[16 + k])

    for region in range(2):
        for i in range(2):
            table = gx[region, i * 4:i * 4 + 4].reshape(128, 256).astype(F32)
            first = region * 256 + i * 128
            xt[:, first:first + 128] = table.T

    high = xt[128:129, :].astype(jnp.int32)
    low = xt[129:130, :].astype(jnp.int32)
    lane = xt[130:131, :].astype(jnp.int32)
    slot = (high * 8 + low + 256 * c) & 511
    choose = jnp.where(iota((512, 512), 0) == slot, F32(1.0), F32(0.0)).astype(BF16)
    found = dot(xt[0:128, :].astype(BF16), choose)
    where_row = iota((128, 512), 0)
    target = jnp.sum(
        jnp.where(where_row == lane, found * 128.0, F32(0.0))
        + jnp.where(where_row == lane + 64, found, F32(0.0)),
        axis=0, keepdims=True,
    )
    own_ids = jnp.broadcast_to(id_row.astype(F32), (128, SLAB)).T[:, 0:1]

    negatives, positives = [], []
    for i in range(4):
        cols = slice(i * 128, i * 128 + 128)
        e = jnp.exp(64.0 * dot_cols(key_half[...], query_half[cols, :]))
        hit = own_ids == target[:, cols]
        n = jnp.where(hit, F32(0.0), e)
        p = jnp.where(hit, e, F32(0.0))
        negs[:, cols] = n
        poss[:, cols] = p
        negs_half[:, cols] = n.astype(BF16)
        poss_half[:, cols] = p.astype(BF16)
        negatives.append(jnp.sum(n, axis=0, keepdims=True))
        positives.append(jnp.sum(p, axis=0, keepdims=True))
    mine = jnp.concatenate(negatives + positives, axis=0)
    stat_send[0] = jnp.concatenate(
        [negatives[2], negatives[3], negatives[0], negatives[1],
         positives[2], positives[3], positives[0], positives[1]], axis=0
    )

    send(stat_send.at[0], stat_core, st_ss.at[0], st_rs.at[0], partner)
    for part, half in enumerate((negs_half, poss_half)):
        q_send[part] = dot_rows(half[:, 256:512], key_half[...]).astype(BF16)
        send(q_send.at[part], q_core.at[part], q_ss.at[part], q_rs.at[part], partner)

    arrived(stat_core, st_rs.at[0])
    mine = mine + stat_core[...]
    stat_a[a] = mine
    for k in ORDER:
        send(stat_a.at[a], stat_a.at[a], st_ss.at[k], st_rs.at[k], on_a(k)[1])

    for part, half in enumerate((negs_half, poss_half)):
        q_own[part] = dot_rows(half[:, 0:256], key_half[...])
    for part in range(2):
        arrived(q_core.at[part], q_rs.at[part])

    @pl.loop(0, NA)
    def _(i):
        for h in range(2):
            rows = pl.ds(pl.multiple_of(i * 32 + h * 16, 16), 16)
            for part in range(2):
                qb_send[i, h, part] = (
                    q_own[part, rows, :] + q_core[part, rows, :].astype(F32)
                ).astype(BF16)

    for h in range(2):
        for k in ORDER:
            there, device = on_b(k)
            send(qb_send.at[there, h], qb_recv.at[b, h],
                 q_ss.at[8 + 8 * h + k], q_rs.at[8 + 8 * h + k], device)
    qb_recv[b] = qb_send[b]

    for k in ORDER:
        arrived(stat_a.at[on_a(NA - k)[0]], st_rs.at[k])
    stat_b[b] = jnp.sum(stat_a[...], axis=0)
    for k in ORDER:
        send(stat_b.at[b], stat_b.at[b], st_ss.at[8 + k], st_rs.at[8 + k], on_b(k)[1])

    pick = jnp.where(
        (iota((D, 256), 0) == iota((D, 256), 1) + x * 192) & (iota((D, 256), 1) < 192),
        F32(1.0), F32(0.0),
    ).astype(BF16)
    emb_sel[...] = dot(emb_ref[...], pick).astype(BF16)
    place = iota((1, 1024), 1)
    core = ((place >> 9) + c) & 1
    place_b, place_a = (place >> 6) & 7, (place >> 3) & 7
    place_y = jnp.where(core == 0, place_b, place_a)
    place_z = place_a + place_b - place_y
    column = jnp.where(
        (place & 7) < 6, 6 * (place_y * 16 + place_z * 2 + core) + (place & 7), -1
    )

    @pl.loop(0, D // 128)
    def _(i):
        rows = pl.ds(pl.multiple_of(i * 128, 128), 128)
        perm[rows, :] = jnp.where(
            iota((128, 1024), 0) + i * 128 == column, F32(1.0), F32(0.0)
        ).astype(BF16)

    for k in ORDER:
        arrived(stat_b.at[on_b(NA - k)[0]], st_rs.at[8 + k])
    stats = jnp.sum(stat_b[...], axis=0)
    by_total = 64.0 / (stats[0:4] + stats[4:8])
    by_positive = 1.0 / stats[4:8]
    share_negative = stats[0:4] * by_total

    for i in range(4):
        cols = slice(i * 128, i * 128 + 128)
        weights[:, cols] = (
            negs[:, cols] * by_total[i:i + 1, :]
            - (poss[:, cols] * by_positive[i:i + 1, :]) * share_negative[i:i + 1, :]
        ).astype(BF16)

    @pl.loop(0, NX)
    def _(i):
        rows = pl.ds(pl.multiple_of(i * 64, 64), 64)
        k_send[i] = dot(weights[rows, :], query_half[...]).astype(BF16)

    for k in XORDER:
        there, device = on_x(k)
        send(k_send.at[there], k_recv.at[x], k_ss.at[k], k_rs.at[k], device)
    k_recv[x] = k_send[x]

    def as_column(rows, h):
        wide = jnp.concatenate([rows[0:1], rows[1:2]], axis=1)
        diagonal = iota((16, SLAB), 1) == iota((16, SLAB), 0) + (b * 32 + h * 16)
        return jnp.sum(jnp.where(diagonal, wide, F32(0.0)), axis=1, keepdims=True)

    for h in range(2):
        for k in ORDER:
            arrived(qb_recv.at[on_b(NA - k)[0], h], q_rs.at[8 + 8 * h + k])
        sums = []
        for part in range(2):
            total = qb_recv[0, h, part].astype(F32)
            for i in range(1, NA):
                total = total + qb_recv[i, h, part].astype(F32)
            sums.append(total)
        qa_recv[h, a] = (
            sums[0] * as_column(by_total, h)
            - (sums[1] * as_column(by_positive, h)) * as_column(share_negative, h)
        ).astype(BF16)
        for k in ORDER:
            send(qa_recv.at[h, a], qa_recv.at[h, a],
                 q_ss.at[24 + 8 * h + k], q_rs.at[24 + 8 * h + k], on_a(k)[1])

    for k in XORDER:
        arrived(k_recv.at[on_x(NX - k)[0]], k_rs.at[k])
    quarter = pl.ds(pl.multiple_of(x * 64, 64), 64)
    key_sum = (
        (k_recv[0].astype(F32) + k_recv[1].astype(F32)) + k_recv[2].astype(F32)
    ) + k_recv[3].astype(F32)
    unit = unit_key[quarter, :]
    krg[x] = (
        (key_sum - unit * jnp.sum(unit * key_sum, axis=1, keepdims=True))
        * (1.0 / key_len[quarter, 0:1])
    ).astype(BF16)
    for k in XORDER:
        send(krg.at[x], krg.at[x], k_ss.at[4 + k], k_rs.at[4 + k], on_x(k)[1])

    for h in range(2):
        for k in ORDER:
            arrived(qa_recv.at[h, on_a(NA - k)[0]], q_rs.at[24 + 8 * h + k])
        query_sum = qa_recv[h, 0].astype(F32)
        for i in range(1, NA):
            query_sum = query_sum + qa_recv[h, i].astype(F32)
        rows = pl.ds(pl.multiple_of(b * 32 + h * 16, 16), 16)
        unit = unit_all[rows, :]
        g2[0, b, h] = (
            (query_sum - unit * jnp.sum(unit * query_sum, axis=1, keepdims=True))
            * (1.0 / len_all[rows, 0:1])
        ).astype(BF16)
        for k in ORDER:
            send(g2.at[0, b, h], g2.at[0, b, h],
                 ag2_ss.at[8 * h + k], ag2_rs.at[8 * h + k], on_b(k)[1])
        send(g2.at[0, b, h], g2.at[1, b, h], ag2_ss.at[16 + 8 * h], ag2_rs.at[16 + 8 * h], partner)

    for k in XORDER:
        arrived(krg.at[on_x(NX - k)[0]], k_rs.at[4 + k])
    grads = krg[...].reshape(SLAB, D)

    @pl.loop(0, 4)
    def _(i):
        half = i // 2
        cols = pl.ds(pl.multiple_of((3 - i) * 256, 256), 256)
        spread_out = dot(grads, perm[:, cols]).astype(BF16)
        share = dot_rows(spread_out, emb_sel[...])
        rows = pl.ds(pl.multiple_of((3 - i) * 256, 256), 256)
        s_own[rows, :] = share

    s_send[...] = s_own[512:1024, :].astype(BF16)
    send(s_send, s_core, s_ss.at[0], s_rs.at[0], partner)

    arrived(s_core, s_rs.at[0])
    for i in range(NA):
        rows = slice(i * 64, i * 64 + 64)
        sb_send[i] = (s_own[rows, :] + s_core[rows, :].astype(F32)).astype(BF16)
    for k in ORDER:
        there, device = on_b(k)
        send(sb_send.at[there], sb_recv.at[b], s_ss.at[8 + k], s_rs.at[8 + k], device)
    sb_recv[b] = sb_send[b]

    shifted_grad = dot_cols(g2[0, b].reshape(32, D), proj_ref[...])
    block = pl.ds(pl.multiple_of(b * 32, 32), 32)
    scaled = shifted_grad * gain
    normed = normed_all[block, :]
    text = (
        scaled
        - jnp.mean(scaled, axis=1, keepdims=True)
        - normed * jnp.mean(scaled * normed, axis=1, keepdims=True)
    ) * (1.0 / spread_all[block, 0:1])
    own_text = text[0:4]
    for i in range(1, NA):
        own_text = jnp.where(a == i, text[i * 4:i * 4 + 4], own_text)
    small_out[0:4, :] = own_text

    for h in range(2):
        for k in ORDER:
            place = on_b(NA - k)[0]
            arrived(g2.at[0, place, h], ag2_rs.at[8 * h + k])
            send(g2.at[0, place, h], g2.at[1, place, h],
                 ag2_ss.at[16 + 8 * h + k], ag2_rs.at[16 + 8 * h + k], partner)
    for h in range(2):
        for k in (0,) + ORDER:
            arrived(g2.at[1, from_core(k), h], ag2_rs.at[16 + 8 * h + k])

    cols = pl.ds(pl.multiple_of(c * 384, 128), 384)
    half = g2[:, :, :, :, cols].reshape(GROUP, 384)
    for i in range(D // 128):
        band = slice(i * 128, i * 128 + 128)
        p_send[band, :] = dot_rows(shifted_all[:, band], half).astype(BF16)
    for h in range(2):
        for k in XORDER:
            there, device = on_x(k)
            send(p_send.at[pl.ds(pl.multiple_of(there * 192 + h * 96, 32), 96), :],
                 p_recv.at[h, x], p_ss.at[4 * h + k], p_rs.at[4 * h + k], device)
        p_recv[h, x] = p_send[pl.ds(pl.multiple_of(x * 192 + h * 96, 32), 96), :]

    for k in ORDER:
        arrived(sb_recv.at[on_b(NA - k)[0]], s_rs.at[8 + k])
    part = sb_recv[0].astype(F32)
    for i in range(1, NA):
        part = part + sb_recv[i].astype(F32)
    for i in range(NA):
        sa_send[i] = part[i * 8:i * 8 + 8, :]
    for k in ORDER:
        there, device = on_a(k)
        send(sa_send.at[there], sa_recv.at[a], s_ss.at[k], s_rs.at[k], device)
    sa_recv[a] = sa_send[a]

    gain_sum = jnp.zeros((1, D), F32)
    bias_sum = jnp.zeros((1, D), F32)
    for i in range(4):
        rows = slice(i * 128, i * 128 + 128)
        quads = slice(i % 2 * 4, i % 2 * 4 + 4)
        grad = dot_cols(g2[i // 2, quads].reshape(128, D), proj_ref[...])
        gain_sum = gain_sum + jnp.sum(grad * normed_all[rows, :], axis=0, keepdims=True)
        bias_sum = bias_sum + jnp.sum(grad, axis=0, keepdims=True)
    gb_recv[x] = jnp.concatenate([gain_sum, bias_sum, jnp.zeros((6, D), F32)], axis=0)
    for k in XORDER:
        send(gb_recv.at[x], gb_recv.at[x], p_ss.at[8 + k], p_rs.at[8 + k], on_x(k)[1])

    for h in range(2):
        for k in XORDER:
            arrived(p_recv.at[h, on_x(NX - k)[0]], p_rs.at[4 * h + k])
        total = (
            (p_recv[h, 0].astype(F32) + p_recv[h, 1].astype(F32)) + p_recv[h, 2].astype(F32)
        ) + p_recv[h, 3].astype(F32)
        p_out[0, x, h] = total.astype(BF16)
        for k in XORDER:
            send(p_out.at[0, x, h], p_out.at[0, x, h],
                 p_ss.at[12 + 4 * h + k], p_rs.at[12 + 4 * h + k], on_x(k)[1])
        send(p_out.at[0, x, h], p_out.at[1, x, h], p_ss.at[20 + 4 * h], p_rs.at[20 + 4 * h], partner)

    for k in XORDER:
        arrived(gb_recv.at[on_x(NX - k)[0]], p_rs.at[8 + k])
    small_out[4:6, :] = jnp.sum(gb_recv[...], axis=0)[0:2]

    for k in ORDER:
        arrived(sa_recv.at[on_a(NA - k)[0]], s_rs.at[k])
    small_out[8:16, 0:256] = jnp.sum(sa_recv[...], axis=0)

    for h in range(2):
        for k in XORDER:
            there = on_x(NX - k)[0]
            arrived(p_out.at[0, there, h], p_rs.at[12 + 4 * h + k])
            send(p_out.at[0, there, h], p_out.at[1, there, h],
                 p_ss.at[20 + 4 * h + k], p_rs.at[20 + 4 * h + k], partner)
    for i in range(NX):
        proj_out[i * 192:i * 192 + 192, cols] = p_out[0, i].reshape(192, 384)
    other = pl.ds(pl.multiple_of((1 - c) * 384, 128), 384)
    for h in range(2):
        arrived(p_out.at[1, x, h], p_rs.at[20 + 4 * h])
        for k in XORDER:
            arrived(p_out.at[1, on_x(NX - k)[0], h], p_rs.at[20 + 4 * h + k])
    for i in range(NX):
        proj_out[i * 192:i * 192 + 192, other] = p_out[1, i].reshape(192, 384)

    for copy in pending:
        copy.wait_send()


def shards(
    text_features, norm_gain, norm_bias, projection, image_embeddings, adapter, slab_ids,
    positive_rows,
):
    whole = pl.BlockSpec(memory_space=pltpu.VMEM)
    dma = pltpu.SemaphoreType.DMA
    small, projection_grad = pl.pallas_call(
        kernel,
        out_shape=(
            jax.ShapeDtypeStruct((16, D), F32),
            jax.ShapeDtypeStruct((D, D), BF16),
        ),
        in_specs=[pl.BlockSpec(memory_space=pl.ANY)] * 8,
        out_specs=(whole,) * 2,
        scratch_shapes=[
            pltpu.VMEM((ROWS, D), BF16),
            pltpu.VMEM((D,), F32),
            pltpu.VMEM((D,), F32),
            pltpu.VMEM((D, D), BF16),
            pltpu.VMEM((SLAB, D), BF16),
            pltpu.VMEM((D, D), BF16),
            pltpu.VMEM((SLAB,), jnp.int32),
            pltpu.VMEM((ROWS,), jnp.int32),
            pltpu.VMEM((NA, ROWS, D), BF16),
            pltpu.VMEM((128, 256), BF16),
            pltpu.VMEM((2, NA, 32, D), BF16),
            pltpu.VMEM((2, NA, 32, 256), BF16),
            pltpu.VMEM((2, NA, 2, 16, D), BF16),
            pltpu.VMEM((SLAB, D), F32),
            pltpu.VMEM((SLAB, D), BF16),
            pltpu.VMEM((SLAB, 128), F32),
            pltpu.VMEM((SLAB, 256), BF16),
            pltpu.VMEM((D, 1024), BF16),
            pltpu.VMEM((GROUP, D), F32),
            pltpu.VMEM((GROUP, D), BF16),
            pltpu.VMEM((GROUP, D), BF16),
            pltpu.VMEM((GROUP // 2, D), F32),
            pltpu.VMEM((GROUP // 2, 128), F32),
            pltpu.VMEM((GROUP // 2, 128), F32),
            pltpu.VMEM((256, GROUP), F32),
            pltpu.VMEM((SLAB, GROUP), F32),
            pltpu.VMEM((SLAB, GROUP), F32),
            pltpu.VMEM((SLAB, GROUP), BF16),
            pltpu.VMEM((SLAB, GROUP), BF16),
            pltpu.VMEM((SLAB, GROUP), BF16),
            pltpu.VMEM((1, 8, 128), F32),
            pltpu.VMEM((8, 128), F32),
            pltpu.VMEM((NA, 8, 128), F32),
            pltpu.VMEM((NA, 8, 128), F32),
            pltpu.VMEM((2, 256, D), BF16),
            pltpu.VMEM((2, 256, D), F32),
            pltpu.VMEM((2, 256, D), BF16),
            pltpu.VMEM((NA, 2, 2, 16, D), BF16),
            pltpu.VMEM((NA, 2, 2, 16, D), BF16),
            pltpu.VMEM((2, NA, 16, D), BF16),
            pltpu.VMEM((NX, 64, D), BF16),
            pltpu.VMEM((NX, 64, D), BF16),
            pltpu.VMEM((NX, 64, D), BF16),
            pltpu.VMEM((1024, 256), F32),
            pltpu.VMEM((512, 256), BF16),
            pltpu.VMEM((512, 256), BF16),
            pltpu.VMEM((NA, 64, 256), BF16),
            pltpu.VMEM((NA, 64, 256), BF16),
            pltpu.VMEM((NA, 8, 256), F32),
            pltpu.VMEM((NA, 8, 256), F32),
            pltpu.VMEM((D, 384), BF16),
            pltpu.VMEM((2, NX, 96, 384), BF16),
            pltpu.VMEM((2, NX, 2, 96, 384), BF16),
            pltpu.VMEM((NX, 8, D), F32),
            dma((24,)), dma((24,)),
            dma((24,)), dma((24,)),
            dma((16,)), dma((16,)),
            dma((40,)), dma((40,)),
            dma((32,)), dma((32,)),
            dma((8,)), dma((8,)),
            dma((16,)), dma((16,)),
            dma((28,)), dma((28,)),
            dma((8,)),
        ],
        compiler_params=pltpu.CompilerParams(
            collective_id=0, has_side_effects=True, vmem_limit_bytes=62 * 1024 * 1024
        ),
    )(
        text_features,
        norm_gain,
        norm_bias,
        projection,
        image_embeddings,
        adapter,
        slab_ids,
        positive_rows,
    )
    return small[0:4], small[4], small[5], projection_grad, small[8:14, 0:192].T


def solution(mesh):
    placed = (
        P(("corpus", "query"), None),
        P(),
        P(),
        P(),
        P("corpus", None),
        P(),
        P("corpus"),
        P(("corpus", "query")),
    )
    return jax.shard_map(
        shards,
        mesh=mesh,
        in_specs=placed,
        out_specs=(P(("corpus", "query"), None), P(), P(), P(), P("query", "corpus")),
        check_vma=False,
    )
```

```python
import functools

import jax
import jax.numpy as jnp
from jax import lax
from jax.experimental import pallas as pl
from jax.experimental.pallas import tpu as pltpu
from jax.sharding import PartitionSpec as P

F32 = jnp.float32
BF16 = jnp.bfloat16
MESH = pl.DeviceIdType.MESH

D = 768
SLAB = 256
ROWS = 4
NA = 8
NX = 4
GROUP = 512
ORDER = (1, 7, 2, 6, 3, 5, 4)
XORDER = (1, 3, 2)


def dot(a, b):
    return jnp.dot(a, b, preferred_element_type=F32)


def dot_rows(a, b):
    return lax.dot_general(a, b, (((0,), (0,)), ((), ())), preferred_element_type=F32)


def dot_cols(a, b):
    return lax.dot_general(a, b, (((1,), (1,)), ((), ())), preferred_element_type=F32)


def iota(shape, axis):
    return lax.broadcasted_iota(jnp.int32, shape, axis)


def spread_matrix():
    row, col = iota((32, 128), 0), iota((32, 128), 1)
    return jnp.where((row >> 2) * 16 + (row & 3) == col, F32(1.0), F32(0.0)).astype(BF16)


def normalise(features, gain, bias):
    average = jnp.mean(features, axis=1, keepdims=True)
    centred = features - average
    spread = jnp.sqrt(jnp.mean(centred * centred, axis=1, keepdims=True) + 1e-5)
    normed = centred * (1.0 / spread)
    return normed, spread, (normed * gain + bias).astype(BF16)


def unit_rows(raw):
    length = jnp.sqrt(jnp.sum(raw * raw, axis=1, keepdims=True) + 1e-6)
    return raw * (1.0 / length), length


def kernel(
    tf_hbm, gain_hbm, bias_hbm, proj_hbm, emb_hbm, adapter_hbm, ids_hbm, rows_hbm,
    small_out, proj_out,
    gain_ref, bias_ref, proj_ref, emb_ref, adapter_ref, ids_ref, rows_ref,
    gt, g0, g1, gx, g2, unit_key, key_half, key_len, emb_sel, perm,
    normed_all, shifted_all, query_half, unit_all, len_all, spread_all, xt,
    negs, poss, negs_half, poss_half, weights,
    stat_send, stat_core, stat_a, stat_b,
    q_send, q_own, q_core, qb_send, qb_recv, qa_recv,
    k_send, k_recv, krg, s_own, s_send, s_core, sb_send, sb_recv, sa_send, sa_recv,
    p_send, p_recv, p_out, gb_recv,
    ag1_ss, ag1_rs, x_ss, x_rs, st_ss, st_rs, q_ss, q_rs, ag2_ss, ag2_rs, k_ss, k_rs,
    s_ss, s_rs, p_ss, p_rs, in_sem, out_sem,
):
    corpus = lax.axis_index("corpus")
    x = lax.axis_index("query")
    c = lax.rem(corpus, 2)
    y = corpus // 16
    z = lax.rem(corpus // 2, 8)
    a = z + c * (y - z)
    b = y + c * (z - y)
    step_a = 2 + 14 * c
    step_b = 16 - 14 * c

    def on_a(k):
        place = lax.rem(a + k, NA)
        return place, (place * step_a + b * step_b + c, x)

    def on_b(k):
        place = lax.rem(b + k, NA)
        return place, (a * step_a + place * step_b + c, x)

    def on_x(k):
        place = lax.rem(x + k, NX)
        return place, (corpus, place)

    partner = (corpus + 1 - 2 * c, x)
    pending = []

    def send(src, dst, send_sem, recv_sem, device):
        copy = pltpu.make_async_remote_copy(
            src_ref=src, dst_ref=dst, send_sem=send_sem, recv_sem=recv_sem,
            device_id=device, device_id_type=MESH,
        )
        copy.start()
        pending.append(copy)

    def arrived(dst, recv_sem):
        pltpu.make_async_remote_copy(
            src_ref=dst, dst_ref=dst, send_sem=recv_sem, recv_sem=recv_sem,
            device_id=partner, device_id_type=MESH,
        ).wait_recv()

    barrier = pltpu.get_barrier_semaphore()
    pl.semaphore_signal(barrier, inc=1, device_id=partner, device_id_type=MESH)
    for k in range(1, NA):
        pl.semaphore_signal(barrier, inc=1, device_id=on_a(k)[1], device_id_type=MESH)
        pl.semaphore_signal(barrier, inc=1, device_id=on_b(k)[1], device_id_type=MESH)
    for k in range(1, NX):
        pl.semaphore_signal(barrier, inc=1, device_id=on_x(k)[1], device_id_type=MESH)

    loads = [
        pltpu.make_async_copy(src, dst, in_sem.at[i])
        for i, (src, dst) in enumerate((
            (tf_hbm, gt.at[a]), (ids_hbm, ids_ref), (rows_hbm, rows_ref), (emb_hbm, emb_ref),
            (adapter_hbm, adapter_ref), (gain_hbm, gain_ref), (bias_hbm, bias_ref),
            (proj_hbm, proj_ref),
        ))
    ]
    for load in loads:
        load.start()

    pl.semaphore_wait(barrier, 2 * (NA - 1) + NX)
    for k in ORDER:
        send(tf_hbm, gt.at[a], ag1_ss.at[k], ag1_rs.at[k], on_a(k)[1])

    for load in loads[1:3]:
        load.wait()
    id_row = ids_ref[...].reshape(1, SLAB)
    row16, col16 = iota((16, SLAB), 0), iota((16, SLAB), 1)
    quarter_ids = jnp.where(col16 >> 6 == row16, id_row, 0)
    both = jnp.concatenate([quarter_ids >> 7, quarter_ids & 127], axis=1)
    bring = jnp.where(
        iota((512, 128), 1) == (iota((512, 128), 0) & 63) + 64 * (iota((512, 128), 0) >> 8),
        F32(1.0), F32(0.0),
    ).astype(BF16)
    listed = dot(both.astype(F32).astype(BF16), bring)
    wanted_row = jnp.sum(
        jnp.where(
            iota((16, ROWS), 0) == iota((16, ROWS), 1),
            rows_ref[...].reshape(1, ROWS).astype(F32), F32(0.0),
        ),
        axis=1, keepdims=True,
    ).astype(jnp.int32)
    device, inner = wanted_row >> 8, wanted_row & 255
    core, there_y, there_z = device & 1, device >> 4, (device >> 1) & 7
    slot = core * 64 + jnp.where(core == 0, there_y * 8 + there_z, there_z * 8 + there_y)
    row = slot * 4 + (inner >> 6)
    lane = iota((16, 128), 1)
    places = jnp.where(
        lane == 0, row >> 3, jnp.where(lane == 1, row & 7, jnp.where(lane == 2, inner & 63, 0))
    ).astype(F32)
    rest = jnp.concatenate([listed, places], axis=1)
    own = g0.at[pl.ds(pl.multiple_of(a * 16, 16), 16), :]
    g0[pl.ds(pl.multiple_of(a * 16, 16), 16), :] = rest.astype(BF16)
    for k in ORDER:
        send(own, own, x_ss.at[k], x_rs.at[k], on_a(k)[1])

    for load in loads[3:]:
        load.wait()
    gain = gain_ref[...].reshape(1, D)
    bias = bias_ref[...].reshape(1, D)

    @pl.loop(0, SLAB // 128)
    def _(i):
        rows = pl.ds(pl.multiple_of(i * 128, 128), 128)
        unit, length = unit_rows(dot(emb_ref[rows, :], adapter_ref[...]))
        unit_key[rows, :] = unit
        key_half[rows, :] = unit.astype(BF16)
        key_len[rows, :] = jnp.broadcast_to(length, (128, 128))

    for k in ORDER:
        arrived(gt.at[on_a(NA - k)[0]], ag1_rs.at[k])

    def widen(g, ss, rs):
        for k in ORDER:
            send(g.at[0, b], g.at[0, b], ss.at[8 + k], rs.at[8 + k], on_b(k)[1])

    loads[0].wait()
    g1[0, b] = jnp.concatenate([gt[i].astype(F32) for i in range(NA)], axis=0).astype(BF16)
    widen(g1, ag1_ss, ag1_rs)
    send(g1.at[0, b], g1.at[1, b], ag1_ss.at[16], ag1_rs.at[16], partner)
    for k in ORDER:
        place = on_a(NA - k)[0]
        arrived(g0.at[pl.ds(pl.multiple_of(place * 16, 16), 16), :], x_rs.at[k])
    gx[0, b] = dot(spread_matrix(), g0[...]).astype(BF16)
    widen(gx, x_ss, x_rs)

    def forward(g, ss, rs, k):
        place = on_b(NA - k)[0]
        arrived(g.at[0, place], rs.at[8 + k])
        send(g.at[0, place], g.at[1, place], ss.at[16 + k], rs.at[16 + k], partner)

    def from_core(k):
        return lax.rem(a + NA - k, NA) if k else a

    def query_block(region, places):
        shifts = []
        for place in places:
            normed, spread, shifted = normalise(g1[region, place].astype(F32), gain, bias)
            rows = pl.ds(pl.multiple_of(region * 256 + place * 32, 32), 32)
            normed_all[rows, :] = normed
            shifted_all[rows, :] = shifted
            if region == 0:
                spread_all[rows, :] = jnp.broadcast_to(spread, (32, 128))
            shifts.append(shifted)
        unit, length = unit_rows(dot(jnp.concatenate(shifts, axis=0), proj_ref[...]))
        for i, place in enumerate(places):
            rows = pl.ds(pl.multiple_of(region * 256 + place * 32, 32), 32)
            piece = slice(i * 32, i * 32 + 32)
            query_half[rows, :] = unit[piece].astype(BF16)
            if region == 0:
                unit_all[rows, :] = unit[piece]
                len_all[rows, :] = jnp.broadcast_to(length[piece], (32, 128))

    near, far = ORDER[:3], ORDER[3:]
    for k in near:
        forward(g1, ag1_ss, ag1_rs, k)
    query_block(0, [b] + [on_b(NA - k)[0] for k in near])
    for k in (0,) + near:
        arrived(g1.at[1, from_core(k)], ag1_rs.at[16 + k])
    query_block(1, [from_core(k) for k in (0,) + near])
    for k in far:
        forward(g1, ag1_ss, ag1_rs, k)
    query_block(0, [on_b(NA - k)[0] for k in far])
    for k in ORDER:
        arrived(gx.at[0, on_b(NA - k)[0]], x_rs.at[8 + k])
    send(gx.at[0], gx.at[1], x_ss.at[16], x_rs.at[16], partner)
    for k in far:
        arrived(g1.at[1, from_core(k)], ag1_rs.at[16 + k])
    query_block(1, [from_core(k) for k in far])
    arrived(gx.at[1], x_rs.at[16])

    for region in range(2):
        for i in range(2):
            table = gx[region, i * 4:i * 4 + 4].reshape(128, 256).astype(F32)
            first = region * 256 + i * 128
            xt[:, first:first + 128] = table.T

    high = xt[128:129, :].astype(jnp.int32)
    low = xt[129:130, :].astype(jnp.int32)
    lane = xt[130:131, :].astype(jnp.int32)
    slot = (high * 8 + low + 256 * c) & 511
    choose = jnp.where(iota((512, 512), 0) == slot, F32(1.0), F32(0.0)).astype(BF16)
    found = dot(xt[0:128, :].astype(BF16), choose)
    where_row = iota((128, 512), 0)
    target = jnp.sum(
        jnp.where(where_row == lane, found * 128.0, F32(0.0))
        + jnp.where(where_row == lane + 64, found, F32(0.0)),
        axis=0, keepdims=True,
    )
    own_ids = jnp.broadcast_to(id_row.astype(F32), (128, SLAB)).T[:, 0:1]

    negatives, positives = [], []
    for i in range(4):
        cols = slice(i * 128, i * 128 + 128)
        e = jnp.exp(64.0 * dot_cols(key_half[...], query_half[cols, :]))
        hit = own_ids == target[:, cols]
        n = jnp.where(hit, F32(0.0), e)
        p = jnp.where(hit, e, F32(0.0))
        negs[:, cols] = n
        poss[:, cols] = p
        negs_half[:, cols] = n.astype(BF16)
        poss_half[:, cols] = p.astype(BF16)
        negatives.append(jnp.sum(n, axis=0, keepdims=True))
        positives.append(jnp.sum(p, axis=0, keepdims=True))
    mine = jnp.concatenate(negatives + positives, axis=0)
    stat_send[0] = jnp.concatenate(
        [negatives[2], negatives[3], negatives[0], negatives[1],
         positives[2], positives[3], positives[0], positives[1]], axis=0
    )

    send(stat_send.at[0], stat_core, st_ss.at[0], st_rs.at[0], partner)
    for part, half in enumerate((negs_half, poss_half)):
        q_send[part] = dot_rows(half[:, 256:512], key_half[...]).astype(BF16)
        send(q_send.at[part], q_core.at[part], q_ss.at[part], q_rs.at[part], partner)

    arrived(stat_core, st_rs.at[0])
    mine = mine + stat_core[...]
    stat_a[a] = mine
    for k in ORDER:
        send(stat_a.at[a], stat_a.at[a], st_ss.at[k], st_rs.at[k], on_a(k)[1])

    for part, half in enumerate((negs_half, poss_half)):
        q_own[part] = dot_rows(half[:, 0:256], key_half[...])
    for part in range(2):
        arrived(q_core.at[part], q_rs.at[part])

    for h in range(2):

        @pl.loop(0, NA)
        def _(i):
            rows = pl.ds(pl.multiple_of(i * 32 + h * 16, 16), 16)
            for part in range(2):
                qb_send[i, h, part] = (
                    q_own[part, rows, :] + q_core[part, rows, :].astype(F32)
                ).astype(BF16)

        for k in ORDER:
            there, device = on_b(k)
            send(qb_send.at[there, h], qb_recv.at[b, h],
                 q_ss.at[8 + 8 * h + k], q_rs.at[8 + 8 * h + k], device)
    qb_recv[b] = qb_send[b]

    for k in ORDER:
        arrived(stat_a.at[on_a(NA - k)[0]], st_rs.at[k])
    stat_b[b] = jnp.sum(stat_a[...], axis=0)
    for k in ORDER:
        send(stat_b.at[b], stat_b.at[b], st_ss.at[8 + k], st_rs.at[8 + k], on_b(k)[1])

    pick = jnp.where(
        (iota((D, 256), 0) == iota((D, 256), 1) + x * 192) & (iota((D, 256), 1) < 192),
        F32(1.0), F32(0.0),
    ).astype(BF16)
    emb_sel[...] = dot(emb_ref[...], pick).astype(BF16)
    place = iota((1, 1024), 1)
    core = ((place >> 9) + c) & 1
    place_b, place_a = (place >> 6) & 7, (place >> 3) & 7
    place_y = jnp.where(core == 0, place_b, place_a)
    place_z = place_a + place_b - place_y
    column = jnp.where(
        (place & 7) < 6, 6 * (place_y * 16 + place_z * 2 + core) + (place & 7), -1
    )

    @pl.loop(0, D // 128)
    def _(i):
        rows = pl.ds(pl.multiple_of(i * 128, 128), 128)
        perm[rows, :] = jnp.where(
            iota((128, 1024), 0) + i * 128 == column, F32(1.0), F32(0.0)
        ).astype(BF16)

    for k in ORDER:
        arrived(stat_b.at[on_b(NA - k)[0]], st_rs.at[8 + k])
    stats = jnp.sum(stat_b[...], axis=0)
    by_total = 64.0 / (stats[0:4] + stats[4:8])
    by_positive = 1.0 / stats[4:8]
    share_negative = stats[0:4] * by_total

    for i in range(4):
        cols = slice(i * 128, i * 128 + 128)
        weights[:, cols] = (
            negs[:, cols] * by_total[i:i + 1, :]
            - (poss[:, cols] * by_positive[i:i + 1, :]) * share_negative[i:i + 1, :]
        ).astype(BF16)

    @pl.loop(0, NX)
    def _(i):
        rows = pl.ds(pl.multiple_of(i * 64, 64), 64)
        k_send[i] = dot(weights[rows, :], query_half[...]).astype(BF16)

    for k in XORDER:
        there, device = on_x(k)
        send(k_send.at[there], k_recv.at[x], k_ss.at[k], k_rs.at[k], device)
    k_recv[x] = k_send[x]

    def as_column(rows, h):
        wide = jnp.concatenate([rows[0:1], rows[1:2]], axis=1)
        diagonal = iota((16, SLAB), 1) == iota((16, SLAB), 0) + (b * 32 + h * 16)
        return jnp.sum(jnp.where(diagonal, wide, F32(0.0)), axis=1, keepdims=True)

    for h in range(2):
        for k in ORDER:
            arrived(qb_recv.at[on_b(NA - k)[0], h], q_rs.at[8 + 8 * h + k])
        sums = []
        for part in range(2):
            total = qb_recv[0, h, part].astype(F32)
            for i in range(1, NA):
                total = total + qb_recv[i, h, part].astype(F32)
            sums.append(total)
        qa_recv[h, a] = (
            sums[0] * as_column(by_total, h)
            - (sums[1] * as_column(by_positive, h)) * as_column(share_negative, h)
        ).astype(BF16)
        for k in ORDER:
            send(qa_recv.at[h, a], qa_recv.at[h, a],
                 q_ss.at[24 + 8 * h + k], q_rs.at[24 + 8 * h + k], on_a(k)[1])

    for k in XORDER:
        arrived(k_recv.at[on_x(NX - k)[0]], k_rs.at[k])
    quarter = pl.ds(pl.multiple_of(x * 64, 64), 64)
    key_sum = (
        (k_recv[0].astype(F32) + k_recv[1].astype(F32)) + k_recv[2].astype(F32)
    ) + k_recv[3].astype(F32)
    unit = unit_key[quarter, :]
    krg[x] = (
        (key_sum - unit * jnp.sum(unit * key_sum, axis=1, keepdims=True))
        * (1.0 / key_len[quarter, 0:1])
    ).astype(BF16)
    for k in XORDER:
        send(krg.at[x], krg.at[x], k_ss.at[4 + k], k_rs.at[4 + k], on_x(k)[1])

    for h in range(2):
        for k in ORDER:
            arrived(qa_recv.at[h, on_a(NA - k)[0]], q_rs.at[24 + 8 * h + k])
        query_sum = qa_recv[h, 0].astype(F32)
        for i in range(1, NA):
            query_sum = query_sum + qa_recv[h, i].astype(F32)
        rows = pl.ds(pl.multiple_of(b * 32 + h * 16, 16), 16)
        unit = unit_all[rows, :]
        g2[0, b, h] = (
            (query_sum - unit * jnp.sum(unit * query_sum, axis=1, keepdims=True))
            * (1.0 / len_all[rows, 0:1])
        ).astype(BF16)
        for k in ORDER:
            send(g2.at[0, b, h], g2.at[0, b, h],
                 ag2_ss.at[8 * h + k], ag2_rs.at[8 * h + k], on_b(k)[1])
        send(g2.at[0, b, h], g2.at[1, b, h], ag2_ss.at[16 + 8 * h], ag2_rs.at[16 + 8 * h], partner)

    for k in XORDER:
        arrived(krg.at[on_x(NX - k)[0]], k_rs.at[4 + k])
    grads = krg[...].reshape(SLAB, D)

    @pl.loop(0, 4)
    def _(i):
        half = i // 2
        cols = pl.ds(pl.multiple_of((3 - i) * 256, 256), 256)
        spread_out = dot(grads, perm[:, cols]).astype(BF16)
        share = dot_rows(spread_out, emb_sel[...])
        rows = pl.ds(pl.multiple_of((3 - i) * 256, 256), 256)
        s_own[rows, :] = share

    s_send[...] = s_own[512:1024, :].astype(BF16)
    send(s_send, s_core, s_ss.at[0], s_rs.at[0], partner)

    arrived(s_core, s_rs.at[0])
    for i in range(NA):
        rows = slice(i * 64, i * 64 + 64)
        sb_send[i] = (s_own[rows, :] + s_core[rows, :].astype(F32)).astype(BF16)
    for k in ORDER:
        there, device = on_b(k)
        send(sb_send.at[there], sb_recv.at[b], s_ss.at[8 + k], s_rs.at[8 + k], device)
    sb_recv[b] = sb_send[b]

    shifted_grad = dot_cols(g2[0, b].reshape(32, D), proj_ref[...])
    block = pl.ds(pl.multiple_of(b * 32, 32), 32)
    scaled = shifted_grad * gain
    normed = normed_all[block, :]
    text = (
        scaled
        - jnp.mean(scaled, axis=1, keepdims=True)
        - normed * jnp.mean(scaled * normed, axis=1, keepdims=True)
    ) * (1.0 / spread_all[block, 0:1])
    own_text = text[0:4]
    for i in range(1, NA):
        own_text = jnp.where(a == i, text[i * 4:i * 4 + 4], own_text)
    small_out[0:4, :] = own_text

    for h in range(2):
        for k in ORDER:
            place = on_b(NA - k)[0]
            arrived(g2.at[0, place, h], ag2_rs.at[8 * h + k])
            send(g2.at[0, place, h], g2.at[1, place, h],
                 ag2_ss.at[16 + 8 * h + k], ag2_rs.at[16 + 8 * h + k], partner)
    for h in range(2):
        for k in (0,) + ORDER:
            arrived(g2.at[1, from_core(k), h], ag2_rs.at[16 + 8 * h + k])

    cols = pl.ds(pl.multiple_of(c * 384, 128), 384)
    half = g2[:, :, :, :, cols].reshape(GROUP, 384)
    for i in range(D // 128):
        band = slice(i * 128, i * 128 + 128)
        p_send[band, :] = dot_rows(shifted_all[:, band], half).astype(BF16)
    for h in range(2):
        for k in XORDER:
            there, device = on_x(k)
            send(p_send.at[pl.ds(pl.multiple_of(there * 192 + h * 96, 32), 96), :],
                 p_recv.at[h, x], p_ss.at[4 * h + k], p_rs.at[4 * h + k], device)
        p_recv[h, x] = p_send[pl.ds(pl.multiple_of(x * 192 + h * 96, 32), 96), :]

    for k in ORDER:
        arrived(sb_recv.at[on_b(NA - k)[0]], s_rs.at[8 + k])
    part = sb_recv[0].astype(F32)
    for i in range(1, NA):
        part = part + sb_recv[i].astype(F32)
    for i in range(NA):
        sa_send[i] = part[i * 8:i * 8 + 8, :]
    for k in ORDER:
        there, device = on_a(k)
        send(sa_send.at[there], sa_recv.at[a], s_ss.at[k], s_rs.at[k], device)
    sa_recv[a] = sa_send[a]

    gain_sum = jnp.zeros((1, D), F32)
    bias_sum = jnp.zeros((1, D), F32)
    for i in range(4):
        rows = slice(i * 128, i * 128 + 128)
        quads = slice(i % 2 * 4, i % 2 * 4 + 4)
        grad = dot_cols(g2[i // 2, quads].reshape(128, D), proj_ref[...])
        gain_sum = gain_sum + jnp.sum(grad * normed_all[rows, :], axis=0, keepdims=True)
        bias_sum = bias_sum + jnp.sum(grad, axis=0, keepdims=True)
    gb_recv[x] = jnp.concatenate([gain_sum, bias_sum, jnp.zeros((6, D), F32)], axis=0)
    for k in XORDER:
        send(gb_recv.at[x], gb_recv.at[x], p_ss.at[8 + k], p_rs.at[8 + k], on_x(k)[1])

    stores = []

    def store(side, place, h, i):
        rows = pl.ds(pl.multiple_of(place * 192 + h * 96, 32), 96)
        lanes = pl.ds(pl.multiple_of((c + side * (1 - 2 * c)) * 384, 128), 384)
        copy = pltpu.make_async_copy(
            p_out.at[side, place, h], proj_out.at[rows, lanes], out_sem.at[i]
        )
        copy.start()
        stores.append(copy)

    for copy in pending[:-30]:
        copy.wait_send()
    del pending[:-30]

    for h in range(2):
        for k in XORDER:
            arrived(p_recv.at[h, on_x(NX - k)[0]], p_rs.at[4 * h + k])
        total = (
            (p_recv[h, 0].astype(F32) + p_recv[h, 1].astype(F32)) + p_recv[h, 2].astype(F32)
        ) + p_recv[h, 3].astype(F32)
        p_out[0, x, h] = total.astype(BF16)
        for k in XORDER:
            send(p_out.at[0, x, h], p_out.at[0, x, h],
                 p_ss.at[12 + 4 * h + k], p_rs.at[12 + 4 * h + k], on_x(k)[1])
        send(p_out.at[0, x, h], p_out.at[1, x, h], p_ss.at[20 + 4 * h], p_rs.at[20 + 4 * h], partner)
        store(0, x, h, 4 * h)

    for k in XORDER:
        arrived(gb_recv.at[on_x(NX - k)[0]], p_rs.at[8 + k])
    small_out[4:6, :] = jnp.sum(gb_recv[...], axis=0)[0:2]

    for k in ORDER:
        arrived(sa_recv.at[on_a(NA - k)[0]], s_rs.at[k])
    small_out[8:16, 0:256] = jnp.sum(sa_recv[...], axis=0)

    for h in range(2):
        for k in XORDER:
            there = on_x(NX - k)[0]
            arrived(p_out.at[0, there, h], p_rs.at[12 + 4 * h + k])
            send(p_out.at[0, there, h], p_out.at[1, there, h],
                 p_ss.at[20 + 4 * h + k], p_rs.at[20 + 4 * h + k], partner)
            store(0, there, h, 4 * h + k)
    for h in range(2):
        arrived(p_out.at[1, x, h], p_rs.at[20 + 4 * h])
        store(1, x, h, 8 + 4 * h)
        for k in XORDER:
            there = on_x(NX - k)[0]
            arrived(p_out.at[1, there, h], p_rs.at[20 + 4 * h + k])
            store(1, there, h, 8 + 4 * h + k)
    for copy in stores:
        copy.wait()
    for copy in pending:
        copy.wait_send()


def finish(
    small_hbm, part_hbm, text_hbm, gain_hbm, bias_hbm, proj_hbm, adapter_hbm,
    small, held, text, gain, bias, adapter, in_sem, out_sem,
):
    bands = [pl.ds(i * 192, 192) for i in range(4)]
    into = [pltpu.make_async_copy(small_hbm, small, in_sem.at[0])] + [
        pltpu.make_async_copy(part_hbm.at[band], held.at[band], in_sem.at[1 + i])
        for i, band in enumerate(bands)
    ]
    out = [
        pltpu.make_async_copy(held.at[band], proj_hbm.at[band], out_sem.at[i])
        for i, band in enumerate(bands)
    ] + [
        pltpu.make_async_copy(src, dst, out_sem.at[4 + i])
        for i, (src, dst) in enumerate((
            (text, text_hbm), (gain, gain_hbm), (bias, bias_hbm), (adapter, adapter_hbm)
        ))
    ]
    for copy in into:
        copy.start()
    into[0].wait()
    text[...] = small[0:4, :]
    gain[...] = small[4:5, :].reshape(D)
    bias[...] = small[5:6, :].reshape(D)
    adapter[...] = small[8:14, 0:192]
    for copy in out[4:]:
        copy.start()
    for first, second in zip(into[1:], out[:4]):
        first.wait()
        second.start()
    for copy in out:
        copy.wait()


def shards(
    text_features, norm_gain, norm_bias, projection, image_embeddings, adapter, slab_ids,
    positive_rows,
):
    whole = pl.BlockSpec(memory_space=pltpu.VMEM)
    dma = pltpu.SemaphoreType.DMA
    small, projection_grad = pl.pallas_call(
        kernel,
        out_shape=(
            jax.ShapeDtypeStruct((16, D), F32),
            jax.ShapeDtypeStruct((D, D), BF16),
        ),
        in_specs=[pl.BlockSpec(memory_space=pl.ANY)] * 8,
        out_specs=(whole, pl.BlockSpec(memory_space=pl.ANY)),
        scratch_shapes=[
            pltpu.VMEM((D,), F32),
            pltpu.VMEM((D,), F32),
            pltpu.VMEM((D, D), BF16),
            pltpu.VMEM((SLAB, D), BF16),
            pltpu.VMEM((D, D), BF16),
            pltpu.VMEM((SLAB,), jnp.int32),
            pltpu.VMEM((ROWS,), jnp.int32),
            pltpu.VMEM((NA, ROWS, D), BF16),
            pltpu.VMEM((128, 256), BF16),
            pltpu.VMEM((2, NA, 32, D), BF16),
            pltpu.VMEM((2, NA, 32, 256), BF16),
            pltpu.VMEM((2, NA, 2, 16, D), BF16),
            pltpu.VMEM((SLAB, D), F32),
            pltpu.VMEM((SLAB, D), BF16),
            pltpu.VMEM((SLAB, 128), F32),
            pltpu.VMEM((SLAB, 256), BF16),
            pltpu.VMEM((D, 1024), BF16),
            pltpu.VMEM((GROUP, D), F32),
            pltpu.VMEM((GROUP, D), BF16),
            pltpu.VMEM((GROUP, D), BF16),
            pltpu.VMEM((GROUP // 2, D), F32),
            pltpu.VMEM((GROUP // 2, 128), F32),
            pltpu.VMEM((GROUP // 2, 128), F32),
            pltpu.VMEM((256, GROUP), F32),
            pltpu.VMEM((SLAB, GROUP), F32),
            pltpu.VMEM((SLAB, GROUP), F32),
            pltpu.VMEM((SLAB, GROUP), BF16),
            pltpu.VMEM((SLAB, GROUP), BF16),
            pltpu.VMEM((SLAB, GROUP), BF16),
            pltpu.VMEM((1, 8, 128), F32),
            pltpu.VMEM((8, 128), F32),
            pltpu.VMEM((NA, 8, 128), F32),
            pltpu.VMEM((NA, 8, 128), F32),
            pltpu.VMEM((2, 256, D), BF16),
            pltpu.VMEM((2, 256, D), F32),
            pltpu.VMEM((2, 256, D), BF16),
            pltpu.VMEM((NA, 2, 2, 16, D), BF16),
            pltpu.VMEM((NA, 2, 2, 16, D), BF16),
            pltpu.VMEM((2, NA, 16, D), BF16),
            pltpu.VMEM((NX, 64, D), BF16),
            pltpu.VMEM((NX, 64, D), BF16),
            pltpu.VMEM((NX, 64, D), BF16),
            pltpu.VMEM((1024, 256), F32),
            pltpu.VMEM((512, 256), BF16),
            pltpu.VMEM((512, 256), BF16),
            pltpu.VMEM((NA, 64, 256), BF16),
            pltpu.VMEM((NA, 64, 256), BF16),
            pltpu.VMEM((NA, 8, 256), F32),
            pltpu.VMEM((NA, 8, 256), F32),
            pltpu.VMEM((D, 384), BF16),
            pltpu.VMEM((2, NX, 96, 384), BF16),
            pltpu.VMEM((2, NX, 2, 96, 384), BF16),
            pltpu.VMEM((NX, 8, D), F32),
            dma((24,)), dma((24,)),
            dma((24,)), dma((24,)),
            dma((16,)), dma((16,)),
            dma((40,)), dma((40,)),
            dma((32,)), dma((32,)),
            dma((8,)), dma((8,)),
            dma((16,)), dma((16,)),
            dma((28,)), dma((28,)),
            dma((8,)), dma((16,)),
        ],
        compiler_params=pltpu.CompilerParams(
            collective_id=0, has_side_effects=True, vmem_limit_bytes=62 * 1024 * 1024
        ),
    )(
        text_features,
        norm_gain,
        norm_bias,
        projection,
        image_embeddings,
        adapter,
        slab_ids,
        positive_rows,
    )
    text_grad, gain_grad, bias_grad, projection_grad, adapter_grad = pl.pallas_call(
        finish,
        out_shape=(
            jax.ShapeDtypeStruct((ROWS, D), F32),
            jax.ShapeDtypeStruct((D,), F32),
            jax.ShapeDtypeStruct((D,), F32),
            jax.ShapeDtypeStruct((D, D), BF16),
            jax.ShapeDtypeStruct((6, 192), F32),
        ),
        in_specs=[pl.BlockSpec(memory_space=pl.ANY)] * 2,
        out_specs=(pl.BlockSpec(memory_space=pl.ANY),) * 5,
        scratch_shapes=[
            pltpu.VMEM((16, D), F32),
            pltpu.VMEM((D, D), BF16),
            pltpu.VMEM((ROWS, D), F32),
            pltpu.VMEM((D,), F32),
            pltpu.VMEM((D,), F32),
            pltpu.VMEM((6, 192), F32),
            dma((5,)), dma((8,)),
        ],
        compiler_params=pltpu.CompilerParams(vmem_limit_bytes=62 * 1024 * 1024),
    )(small, projection_grad)
    return text_grad, gain_grad, bias_grad, projection_grad, adapter_grad.T


def solution(mesh):
    placed = (
        P(("corpus", "query"), None),
        P(),
        P(),
        P(),
        P("corpus", None),
        P(),
        P("corpus"),
        P(("corpus", "query")),
    )
    return jax.shard_map(
        shards,
        mesh=mesh,
        in_specs=placed,
        out_specs=(P(("corpus", "query"), None), P(), P(), P(), P("query", "corpus")),
        check_vma=False,
    )
```

```python
import functools

import jax
import jax.numpy as jnp
from jax import lax
from jax.experimental import pallas as pl
from jax.experimental.pallas import tpu as pltpu
from jax.sharding import PartitionSpec as P

F32 = jnp.float32
BF16 = jnp.bfloat16
MESH = pl.DeviceIdType.MESH

D = 768
SLAB = 256
ROWS = 4
NA = 8
NX = 4
GROUP = 512
ORDER = (1, 7, 2, 6, 3, 5, 4)
XORDER = (1, 3, 2)


def dot(a, b):
    return jnp.dot(a, b, preferred_element_type=F32)


def dot_rows(a, b):
    return lax.dot_general(a, b, (((0,), (0,)), ((), ())), preferred_element_type=F32)


def dot_cols(a, b):
    return lax.dot_general(a, b, (((1,), (1,)), ((), ())), preferred_element_type=F32)


def iota(shape, axis):
    return lax.broadcasted_iota(jnp.int32, shape, axis)


def spread_matrix():
    row, col = iota((32, 128), 0), iota((32, 128), 1)
    return jnp.where((row >> 2) * 16 + (row & 3) == col, F32(1.0), F32(0.0)).astype(BF16)


def normalise(features, gain, bias):
    average = jnp.mean(features, axis=1, keepdims=True)
    centred = features - average
    spread = jnp.sqrt(jnp.mean(centred * centred, axis=1, keepdims=True) + 1e-5)
    normed = centred * (1.0 / spread)
    return normed, spread, (normed * gain + bias).astype(BF16)


def unit_rows(raw):
    length = jnp.sqrt(jnp.sum(raw * raw, axis=1, keepdims=True) + 1e-6)
    return raw * (1.0 / length), length


def kernel(
    tf_hbm, gain_hbm, bias_hbm, proj_hbm, emb_hbm, adapter_hbm, ids_hbm, rows_hbm,
    small_out, proj_out,
    gain_ref, bias_ref, proj_ref, emb_ref, adapter_ref, ids_ref, rows_ref,
    gt, g0, g1, gx, g2, unit_key, key_half, key_len, emb_sel, perm,
    normed_all, shifted_all, query_half, unit_all, len_all, spread_all, xt,
    negs, poss, negs_half, poss_half, weights,
    stat_send, stat_core, stat_a, stat_b,
    q_send, q_own, q_core, qb_send, qb_recv, qa_recv,
    k_send, k_recv, krg, s_own, s_send, s_core, sb_send, sb_recv, sa_send, sa_recv,
    p_send, p_recv, p_out, gb_recv,
    ag1_ss, ag1_rs, x_ss, x_rs, st_ss, st_rs, q_ss, q_rs, ag2_ss, ag2_rs, k_ss, k_rs,
    s_ss, s_rs, p_ss, p_rs, in_sem, out_sem,
):
    corpus = lax.axis_index("corpus")
    x = lax.axis_index("query")
    c = lax.rem(corpus, 2)
    y = corpus // 16
    z = lax.rem(corpus // 2, 8)
    a = z + c * (y - z)
    b = y + c * (z - y)
    step_a = 2 + 14 * c
    step_b = 16 - 14 * c

    def on_a(k):
        place = lax.rem(a + k, NA)
        return place, (place * step_a + b * step_b + c, x)

    def on_b(k):
        place = lax.rem(b + k, NA)
        return place, (a * step_a + place * step_b + c, x)

    def on_x(k):
        place = lax.rem(x + k, NX)
        return place, (corpus, place)

    partner = (corpus + 1 - 2 * c, x)
    pending = []

    def send(src, dst, send_sem, recv_sem, device):
        copy = pltpu.make_async_remote_copy(
            src_ref=src, dst_ref=dst, send_sem=send_sem, recv_sem=recv_sem,
            device_id=device, device_id_type=MESH,
        )
        copy.start()
        pending.append(copy)

    def arrived(dst, recv_sem):
        pltpu.make_async_remote_copy(
            src_ref=dst, dst_ref=dst, send_sem=recv_sem, recv_sem=recv_sem,
            device_id=partner, device_id_type=MESH,
        ).wait_recv()

    barrier = pltpu.get_barrier_semaphore()
    pl.semaphore_signal(barrier, inc=1, device_id=partner, device_id_type=MESH)
    for k in range(1, NA):
        pl.semaphore_signal(barrier, inc=1, device_id=on_a(k)[1], device_id_type=MESH)
        pl.semaphore_signal(barrier, inc=1, device_id=on_b(k)[1], device_id_type=MESH)
    for k in range(1, NX):
        pl.semaphore_signal(barrier, inc=1, device_id=on_x(k)[1], device_id_type=MESH)

    loads = [
        pltpu.make_async_copy(src, dst, in_sem.at[i])
        for i, (src, dst) in enumerate((
            (tf_hbm, gt.at[a]), (ids_hbm, ids_ref), (rows_hbm, rows_ref), (emb_hbm, emb_ref),
            (adapter_hbm, adapter_ref), (gain_hbm, gain_ref), (bias_hbm, bias_ref),
            (proj_hbm, proj_ref),
        ))
    ]
    for load in loads:
        load.start()

    pl.semaphore_wait(barrier, 2 * (NA - 1) + NX)
    for k in ORDER:
        send(tf_hbm, gt.at[a], ag1_ss.at[k], ag1_rs.at[k], on_a(k)[1])

    for load in loads[1:3]:
        load.wait()
    id_row = ids_ref[...].reshape(1, SLAB)
    row16, col16 = iota((16, SLAB), 0), iota((16, SLAB), 1)
    quarter_ids = jnp.where(col16 >> 6 == row16, id_row, 0)
    both = jnp.concatenate([quarter_ids >> 7, quarter_ids & 127], axis=1)
    bring = jnp.where(
        iota((512, 128), 1) == (iota((512, 128), 0) & 63) + 64 * (iota((512, 128), 0) >> 8),
        F32(1.0), F32(0.0),
    ).astype(BF16)
    listed = dot(both.astype(F32).astype(BF16), bring)
    wanted_row = jnp.sum(
        jnp.where(
            iota((16, ROWS), 0) == iota((16, ROWS), 1),
            rows_ref[...].reshape(1, ROWS).astype(F32), F32(0.0),
        ),
        axis=1, keepdims=True,
    ).astype(jnp.int32)
    device, inner = wanted_row >> 8, wanted_row & 255
    core, there_y, there_z = device & 1, device >> 4, (device >> 1) & 7
    slot = core * 64 + jnp.where(core == 0, there_y * 8 + there_z, there_z * 8 + there_y)
    row = slot * 4 + (inner >> 6)
    lane = iota((16, 128), 1)
    places = jnp.where(
        lane == 0, row >> 3, jnp.where(lane == 1, row & 7, jnp.where(lane == 2, inner & 63, 0))
    ).astype(F32)
    rest = jnp.concatenate([listed, places], axis=1)
    own = g0.at[pl.ds(pl.multiple_of(a * 16, 16), 16), :]
    g0[pl.ds(pl.multiple_of(a * 16, 16), 16), :] = rest.astype(BF16)
    for k in ORDER:
        send(own, own, x_ss.at[k], x_rs.at[k], on_a(k)[1])

    for load in loads[3:]:
        load.wait()
    gain = gain_ref[...].reshape(1, D)
    bias = bias_ref[...].reshape(1, D)

    @pl.loop(0, SLAB // 128)
    def _(i):
        rows = pl.ds(pl.multiple_of(i * 128, 128), 128)
        unit, length = unit_rows(dot(emb_ref[rows, :], adapter_ref[...]))
        unit_key[rows, :] = unit
        key_half[rows, :] = unit.astype(BF16)
        key_len[rows, :] = jnp.broadcast_to(length, (128, 128))

    for k in ORDER:
        arrived(gt.at[on_a(NA - k)[0]], ag1_rs.at[k])

    def widen(g, ss, rs):
        for k in ORDER:
            send(g.at[0, b], g.at[0, b], ss.at[8 + k], rs.at[8 + k], on_b(k)[1])

    loads[0].wait()
    g1[0, b] = jnp.concatenate([gt[i].astype(F32) for i in range(NA)], axis=0).astype(BF16)
    widen(g1, ag1_ss, ag1_rs)
    send(g1.at[0, b], g1.at[1, b], ag1_ss.at[16], ag1_rs.at[16], partner)
    for k in ORDER:
        place = on_a(NA - k)[0]
        arrived(g0.at[pl.ds(pl.multiple_of(place * 16, 16), 16), :], x_rs.at[k])
    gx[0, b] = dot(spread_matrix(), g0[...]).astype(BF16)
    widen(gx, x_ss, x_rs)

    def forward(g, ss, rs, k):
        place = on_b(NA - k)[0]
        arrived(g.at[0, place], rs.at[8 + k])
        send(g.at[0, place], g.at[1, place], ss.at[16 + k], rs.at[16 + k], partner)

    def from_core(k):
        return lax.rem(a + NA - k, NA) if k else a

    def query_block(region, places):
        shifts = []
        for place in places:
            normed, spread, shifted = normalise(g1[region, place].astype(F32), gain, bias)
            rows = pl.ds(pl.multiple_of(region * 256 + place * 32, 32), 32)
            normed_all[rows, :] = normed
            shifted_all[rows, :] = shifted
            if region == 0:
                spread_all[rows, :] = jnp.broadcast_to(spread, (32, 128))
            shifts.append(shifted)
        unit, length = unit_rows(dot(jnp.concatenate(shifts, axis=0), proj_ref[...]))
        for i, place in enumerate(places):
            rows = pl.ds(pl.multiple_of(region * 256 + place * 32, 32), 32)
            piece = slice(i * 32, i * 32 + 32)
            query_half[rows, :] = unit[piece].astype(BF16)
            if region == 0:
                unit_all[rows, :] = unit[piece]
                len_all[rows, :] = jnp.broadcast_to(length[piece], (32, 128))

    near, far = ORDER[:3], ORDER[3:]
    for k in near:
        forward(g1, ag1_ss, ag1_rs, k)
    query_block(0, [b] + [on_b(NA - k)[0] for k in near])
    for k in (0,) + near:
        arrived(g1.at[1, from_core(k)], ag1_rs.at[16 + k])
    query_block(1, [from_core(k) for k in (0,) + near])
    for k in far:
        forward(g1, ag1_ss, ag1_rs, k)
    query_block(0, [on_b(NA - k)[0] for k in far])
    for k in ORDER:
        arrived(gx.at[0, on_b(NA - k)[0]], x_rs.at[8 + k])
    send(gx.at[0], gx.at[1], x_ss.at[16], x_rs.at[16], partner)
    for k in far:
        arrived(g1.at[1, from_core(k)], ag1_rs.at[16 + k])
    query_block(1, [from_core(k) for k in far])
    arrived(gx.at[1], x_rs.at[16])

    for region in range(2):
        for i in range(2):
            table = gx[region, i * 4:i * 4 + 4].reshape(128, 256).astype(F32)
            first = region * 256 + i * 128
            xt[:, first:first + 128] = table.T

    high = xt[128:129, :].astype(jnp.int32)
    low = xt[129:130, :].astype(jnp.int32)
    lane = xt[130:131, :].astype(jnp.int32)
    slot = (high * 8 + low + 256 * c) & 511
    choose = jnp.where(iota((512, 512), 0) == slot, F32(1.0), F32(0.0)).astype(BF16)
    found = dot(xt[0:128, :].astype(BF16), choose)
    where_row = iota((128, 512), 0)
    target = jnp.sum(
        jnp.where(where_row == lane, found * 128.0, F32(0.0))
        + jnp.where(where_row == lane + 64, found, F32(0.0)),
        axis=0, keepdims=True,
    )
    own_ids = jnp.broadcast_to(id_row.astype(F32), (128, SLAB)).T[:, 0:1]

    negatives, positives = [], []
    for i in range(4):
        cols = slice(i * 128, i * 128 + 128)
        e = jnp.exp(64.0 * dot_cols(key_half[...], query_half[cols, :]))
        hit = own_ids == target[:, cols]
        n = jnp.where(hit, F32(0.0), e)
        p = jnp.where(hit, e, F32(0.0))
        negs[:, cols] = n
        poss[:, cols] = p
        negs_half[:, cols] = n.astype(BF16)
        poss_half[:, cols] = p.astype(BF16)
        negatives.append(jnp.sum(n, axis=0, keepdims=True))
        positives.append(jnp.sum(p, axis=0, keepdims=True))
    mine = jnp.concatenate(negatives + positives, axis=0)
    stat_send[0] = jnp.concatenate(
        [negatives[2], negatives[3], negatives[0], negatives[1],
         positives[2], positives[3], positives[0], positives[1]], axis=0
    )

    send(stat_send.at[0], stat_core, st_ss.at[0], st_rs.at[0], partner)
    for part, half in enumerate((negs_half, poss_half)):
        q_send[part] = dot_rows(half[:, 256:512], key_half[...]).astype(BF16)
        send(q_send.at[part], q_core.at[part], q_ss.at[part], q_rs.at[part], partner)

    arrived(stat_core, st_rs.at[0])
    mine = mine + stat_core[...]
    stat_a[a] = mine
    for k in ORDER:
        send(stat_a.at[a], stat_a.at[a], st_ss.at[k], st_rs.at[k], on_a(k)[1])

    for part, half in enumerate((negs_half, poss_half)):
        q_own[part] = dot_rows(half[:, 0:256], key_half[...])
    for part in range(2):
        arrived(q_core.at[part], q_rs.at[part])

    for h in range(2):

        @pl.loop(0, NA)
        def _(i):
            rows = pl.ds(pl.multiple_of(i * 32 + h * 16, 16), 16)
            for part in range(2):
                qb_send[i, h, part] = (
                    q_own[part, rows, :] + q_core[part, rows, :].astype(F32)
                ).astype(BF16)

        for k in ORDER:
            there, device = on_b(k)
            send(qb_send.at[there, h], qb_recv.at[b, h],
                 q_ss.at[8 + 8 * h + k], q_rs.at[8 + 8 * h + k], device)
    qb_recv[b] = qb_send[b]

    for k in ORDER:
        arrived(stat_a.at[on_a(NA - k)[0]], st_rs.at[k])
    stat_b[b] = jnp.sum(stat_a[...], axis=0)
    for k in ORDER:
        send(stat_b.at[b], stat_b.at[b], st_ss.at[8 + k], st_rs.at[8 + k], on_b(k)[1])

    pick = jnp.where(
        (iota((D, 256), 0) == iota((D, 256), 1) + x * 192) & (iota((D, 256), 1) < 192),
        F32(1.0), F32(0.0),
    ).astype(BF16)
    emb_sel[...] = dot(emb_ref[...], pick).astype(BF16)
    place = iota((1, 1024), 1)
    core = ((place >> 9) + c) & 1
    place_b, place_a = (place >> 6) & 7, (place >> 3) & 7
    place_y = jnp.where(core == 0, place_b, place_a)
    place_z = place_a + place_b - place_y
    column = jnp.where(
        (place & 7) < 6, 6 * (place_y * 16 + place_z * 2 + core) + (place & 7), -1
    )

    @pl.loop(0, D // 128)
    def _(i):
        rows = pl.ds(pl.multiple_of(i * 128, 128), 128)
        perm[rows, :] = jnp.where(
            iota((128, 1024), 0) + i * 128 == column, F32(1.0), F32(0.0)
        ).astype(BF16)

    for k in ORDER:
        arrived(stat_b.at[on_b(NA - k)[0]], st_rs.at[8 + k])
    stats = jnp.sum(stat_b[...], axis=0)
    by_total = 64.0 / (stats[0:4] + stats[4:8])
    by_positive = 1.0 / stats[4:8]
    share_negative = stats[0:4] * by_total

    def as_column(rows, h):
        wide = jnp.concatenate([rows[0:1], rows[1:2]], axis=1)
        diagonal = iota((16, SLAB), 1) == iota((16, SLAB), 0) + (b * 32 + h * 16)
        return jnp.sum(jnp.where(diagonal, wide, F32(0.0)), axis=1, keepdims=True)

    def combine(h):
        for k in ORDER:
            arrived(qb_recv.at[on_b(NA - k)[0], h], q_rs.at[8 + 8 * h + k])
        sums = []
        for part in range(2):
            total = qb_recv[0, h, part].astype(F32)
            for i in range(1, NA):
                total = total + qb_recv[i, h, part].astype(F32)
            sums.append(total)
        qa_recv[h, a] = (
            sums[0] * as_column(by_total, h)
            - (sums[1] * as_column(by_positive, h)) * as_column(share_negative, h)
        ).astype(BF16)
        for k in ORDER:
            send(qa_recv.at[h, a], qa_recv.at[h, a],
                 q_ss.at[24 + 8 * h + k], q_rs.at[24 + 8 * h + k], on_a(k)[1])

    combine(0)

    for i in range(4):
        cols = slice(i * 128, i * 128 + 128)
        weights[:, cols] = (
            negs[:, cols] * by_total[i:i + 1, :]
            - (poss[:, cols] * by_positive[i:i + 1, :]) * share_negative[i:i + 1, :]
        ).astype(BF16)

    @pl.loop(0, NX)
    def _(i):
        rows = pl.ds(pl.multiple_of(i * 64, 64), 64)
        k_send[i] = dot(weights[rows, :], query_half[...]).astype(BF16)

    for k in XORDER:
        there, device = on_x(k)
        send(k_send.at[there], k_recv.at[x], k_ss.at[k], k_rs.at[k], device)
    k_recv[x] = k_send[x]

    combine(1)

    for k in XORDER:
        arrived(k_recv.at[on_x(NX - k)[0]], k_rs.at[k])
    quarter = pl.ds(pl.multiple_of(x * 64, 64), 64)
    key_sum = (
        (k_recv[0].astype(F32) + k_recv[1].astype(F32)) + k_recv[2].astype(F32)
    ) + k_recv[3].astype(F32)
    unit = unit_key[quarter, :]
    krg[x] = (
        (key_sum - unit * jnp.sum(unit * key_sum, axis=1, keepdims=True))
        * (1.0 / key_len[quarter, 0:1])
    ).astype(BF16)
    for k in XORDER:
        send(krg.at[x], krg.at[x], k_ss.at[4 + k], k_rs.at[4 + k], on_x(k)[1])

    for h in range(2):
        for k in ORDER:
            arrived(qa_recv.at[h, on_a(NA - k)[0]], q_rs.at[24 + 8 * h + k])
        query_sum = qa_recv[h, 0].astype(F32)
        for i in range(1, NA):
            query_sum = query_sum + qa_recv[h, i].astype(F32)
        rows = pl.ds(pl.multiple_of(b * 32 + h * 16, 16), 16)
        unit = unit_all[rows, :]
        g2[0, b, h] = (
            (query_sum - unit * jnp.sum(unit * query_sum, axis=1, keepdims=True))
            * (1.0 / len_all[rows, 0:1])
        ).astype(BF16)
        for k in ORDER:
            send(g2.at[0, b, h], g2.at[0, b, h],
                 ag2_ss.at[8 * h + k], ag2_rs.at[8 * h + k], on_b(k)[1])
        send(g2.at[0, b, h], g2.at[1, b, h], ag2_ss.at[16 + 8 * h], ag2_rs.at[16 + 8 * h], partner)

    shifted_grad = dot_cols(g2[0, b].reshape(32, D), proj_ref[...])
    block = pl.ds(pl.multiple_of(b * 32, 32), 32)
    scaled = shifted_grad * gain
    normed = normed_all[block, :]
    text = (
        scaled
        - jnp.mean(scaled, axis=1, keepdims=True)
        - normed * jnp.mean(scaled * normed, axis=1, keepdims=True)
    ) * (1.0 / spread_all[block, 0:1])
    own_text = text[0:4]
    for i in range(1, NA):
        own_text = jnp.where(a == i, text[i * 4:i * 4 + 4], own_text)
    small_out[0:4, :] = own_text

    for k in XORDER:
        arrived(krg.at[on_x(NX - k)[0]], k_rs.at[4 + k])
    grads = krg[...].reshape(SLAB, D)

    @pl.loop(0, 4)
    def _(i):
        half = i // 2
        cols = pl.ds(pl.multiple_of((3 - i) * 256, 256), 256)
        spread_out = dot(grads, perm[:, cols]).astype(BF16)
        share = dot_rows(spread_out, emb_sel[...])
        rows = pl.ds(pl.multiple_of((3 - i) * 256, 256), 256)
        s_own[rows, :] = share

    s_send[...] = s_own[512:1024, :].astype(BF16)
    send(s_send, s_core, s_ss.at[0], s_rs.at[0], partner)

    for h in range(2):
        for k in ORDER:
            place = on_b(NA - k)[0]
            arrived(g2.at[0, place, h], ag2_rs.at[8 * h + k])
            send(g2.at[0, place, h], g2.at[1, place, h],
                 ag2_ss.at[16 + 8 * h + k], ag2_rs.at[16 + 8 * h + k], partner)
    arrived(s_core, s_rs.at[0])
    for i in range(NA):
        rows = slice(i * 64, i * 64 + 64)
        sb_send[i] = (s_own[rows, :] + s_core[rows, :].astype(F32)).astype(BF16)
    for k in ORDER:
        there, device = on_b(k)
        send(sb_send.at[there], sb_recv.at[b], s_ss.at[8 + k], s_rs.at[8 + k], device)
    sb_recv[b] = sb_send[b]

    for h in range(2):
        for k in (0,) + ORDER:
            arrived(g2.at[1, from_core(k), h], ag2_rs.at[16 + 8 * h + k])

    cols = pl.ds(pl.multiple_of(c * 384, 128), 384)
    half = g2[:, :, :, :, cols].reshape(GROUP, 384)
    for i in range(D // 128):
        band = slice(i * 128, i * 128 + 128)
        p_send[band, :] = dot_rows(shifted_all[:, band], half).astype(BF16)
    for h in range(2):
        for k in XORDER:
            there, device = on_x(k)
            send(p_send.at[pl.ds(pl.multiple_of(there * 192 + h * 96, 32), 96), :],
                 p_recv.at[h, x], p_ss.at[4 * h + k], p_rs.at[4 * h + k], device)
        p_recv[h, x] = p_send[pl.ds(pl.multiple_of(x * 192 + h * 96, 32), 96), :]

    gain_sum = jnp.zeros((1, D), F32)
    bias_sum = jnp.zeros((1, D), F32)
    for i in range(4):
        rows = slice(i * 128, i * 128 + 128)
        quads = slice(i % 2 * 4, i % 2 * 4 + 4)
        grad = dot_cols(g2[i // 2, quads].reshape(128, D), proj_ref[...])
        gain_sum = gain_sum + jnp.sum(grad * normed_all[rows, :], axis=0, keepdims=True)
        bias_sum = bias_sum + jnp.sum(grad, axis=0, keepdims=True)
    gb_recv[x] = jnp.concatenate([gain_sum, bias_sum, jnp.zeros((6, D), F32)], axis=0)
    for k in XORDER:
        send(gb_recv.at[x], gb_recv.at[x], p_ss.at[8 + k], p_rs.at[8 + k], on_x(k)[1])

    for k in ORDER:
        arrived(sb_recv.at[on_b(NA - k)[0]], s_rs.at[8 + k])
    part = sb_recv[0].astype(F32)
    for i in range(1, NA):
        part = part + sb_recv[i].astype(F32)
    for i in range(NA):
        sa_send[i] = part[i * 8:i * 8 + 8, :]
    for k in ORDER:
        there, device = on_a(k)
        send(sa_send.at[there], sa_recv.at[a], s_ss.at[k], s_rs.at[k], device)
    sa_recv[a] = sa_send[a]

    stores = []

    def store(side, place, h, i):
        rows = pl.ds(pl.multiple_of(place * 192 + h * 96, 32), 96)
        lanes = pl.ds(pl.multiple_of((c + side * (1 - 2 * c)) * 384, 128), 384)
        copy = pltpu.make_async_copy(
            p_out.at[side, place, h], proj_out.at[rows, lanes], out_sem.at[i]
        )
        copy.start()
        stores.append(copy)

    for copy in pending[:-30]:
        copy.wait_send()
    del pending[:-30]

    for h in range(2):
        for k in XORDER:
            arrived(p_recv.at[h, on_x(NX - k)[0]], p_rs.at[4 * h + k])
        total = (
            (p_recv[h, 0].astype(F32) + p_recv[h, 1].astype(F32)) + p_recv[h, 2].astype(F32)
        ) + p_recv[h, 3].astype(F32)
        p_out[0, x, h] = total.astype(BF16)
        for k in XORDER:
            send(p_out.at[0, x, h], p_out.at[0, x, h],
                 p_ss.at[12 + 4 * h + k], p_rs.at[12 + 4 * h + k], on_x(k)[1])
        send(p_out.at[0, x, h], p_out.at[1, x, h], p_ss.at[20 + 4 * h], p_rs.at[20 + 4 * h], partner)
        store(0, x, h, 4 * h)

    for k in XORDER:
        arrived(gb_recv.at[on_x(NX - k)[0]], p_rs.at[8 + k])
    small_out[4:6, :] = jnp.sum(gb_recv[...], axis=0)[0:2]

    for k in ORDER:
        arrived(sa_recv.at[on_a(NA - k)[0]], s_rs.at[k])
    small_out[8:16, 0:256] = jnp.sum(sa_recv[...], axis=0)

    for h in range(2):
        for k in XORDER:
            there = on_x(NX - k)[0]
            arrived(p_out.at[0, there, h], p_rs.at[12 + 4 * h + k])
            send(p_out.at[0, there, h], p_out.at[1, there, h],
                 p_ss.at[20 + 4 * h + k], p_rs.at[20 + 4 * h + k], partner)
            store(0, there, h, 4 * h + k)
    for h in range(2):
        arrived(p_out.at[1, x, h], p_rs.at[20 + 4 * h])
        store(1, x, h, 8 + 4 * h)
        for k in XORDER:
            there = on_x(NX - k)[0]
            arrived(p_out.at[1, there, h], p_rs.at[20 + 4 * h + k])
            store(1, there, h, 8 + 4 * h + k)
    for copy in stores:
        copy.wait()
    for copy in pending:
        copy.wait_send()


def finish(
    small_hbm, part_hbm, text_hbm, gain_hbm, bias_hbm, proj_hbm, adapter_hbm,
    small, held, text, gain, bias, adapter, in_sem, out_sem,
):
    bands = [pl.ds(i * 192, 192) for i in range(4)]
    into = [pltpu.make_async_copy(small_hbm, small, in_sem.at[0])] + [
        pltpu.make_async_copy(part_hbm.at[band], held.at[band], in_sem.at[1 + i])
        for i, band in enumerate(bands)
    ]
    out = [
        pltpu.make_async_copy(held.at[band], proj_hbm.at[band], out_sem.at[i])
        for i, band in enumerate(bands)
    ] + [
        pltpu.make_async_copy(src, dst, out_sem.at[4 + i])
        for i, (src, dst) in enumerate((
            (text, text_hbm), (gain, gain_hbm), (bias, bias_hbm), (adapter, adapter_hbm)
        ))
    ]
    for copy in into:
        copy.start()
    into[0].wait()
    text[...] = small[0:4, :]
    gain[...] = small[4:5, :].reshape(D)
    bias[...] = small[5:6, :].reshape(D)
    adapter[...] = small[8:14, 0:192]
    for copy in out[4:]:
        copy.start()
    for first, second in zip(into[1:], out[:4]):
        first.wait()
        second.start()
    for copy in out:
        copy.wait()


def shards(
    text_features, norm_gain, norm_bias, projection, image_embeddings, adapter, slab_ids,
    positive_rows,
):
    whole = pl.BlockSpec(memory_space=pltpu.VMEM)
    dma = pltpu.SemaphoreType.DMA
    small, projection_grad = pl.pallas_call(
        kernel,
        out_shape=(
            jax.ShapeDtypeStruct((16, D), F32),
            jax.ShapeDtypeStruct((D, D), BF16),
        ),
        in_specs=[pl.BlockSpec(memory_space=pl.ANY)] * 8,
        out_specs=(whole, pl.BlockSpec(memory_space=pl.ANY)),
        scratch_shapes=[
            pltpu.VMEM((D,), F32),
            pltpu.VMEM((D,), F32),
            pltpu.VMEM((D, D), BF16),
            pltpu.VMEM((SLAB, D), BF16),
            pltpu.VMEM((D, D), BF16),
            pltpu.VMEM((SLAB,), jnp.int32),
            pltpu.VMEM((ROWS,), jnp.int32),
            pltpu.VMEM((NA, ROWS, D), BF16),
            pltpu.VMEM((128, 256), BF16),
            pltpu.VMEM((2, NA, 32, D), BF16),
            pltpu.VMEM((2, NA, 32, 256), BF16),
            pltpu.VMEM((2, NA, 2, 16, D), BF16),
            pltpu.VMEM((SLAB, D), F32),
            pltpu.VMEM((SLAB, D), BF16),
            pltpu.VMEM((SLAB, 128), F32),
            pltpu.VMEM((SLAB, 256), BF16),
            pltpu.VMEM((D, 1024), BF16),
            pltpu.VMEM((GROUP, D), F32),
            pltpu.VMEM((GROUP, D), BF16),
            pltpu.VMEM((GROUP, D), BF16),
            pltpu.VMEM((GROUP // 2, D), F32),
            pltpu.VMEM((GROUP // 2, 128), F32),
            pltpu.VMEM((GROUP // 2, 128), F32),
            pltpu.VMEM((256, GROUP), F32),
            pltpu.VMEM((SLAB, GROUP), F32),
            pltpu.VMEM((SLAB, GROUP), F32),
            pltpu.VMEM((SLAB, GROUP), BF16),
            pltpu.VMEM((SLAB, GROUP), BF16),
            pltpu.VMEM((SLAB, GROUP), BF16),
            pltpu.VMEM((1, 8, 128), F32),
            pltpu.VMEM((8, 128), F32),
            pltpu.VMEM((NA, 8, 128), F32),
            pltpu.VMEM((NA, 8, 128), F32),
            pltpu.VMEM((2, 256, D), BF16),
            pltpu.VMEM((2, 256, D), F32),
            pltpu.VMEM((2, 256, D), BF16),
            pltpu.VMEM((NA, 2, 2, 16, D), BF16),
            pltpu.VMEM((NA, 2, 2, 16, D), BF16),
            pltpu.VMEM((2, NA, 16, D), BF16),
            pltpu.VMEM((NX, 64, D), BF16),
            pltpu.VMEM((NX, 64, D), BF16),
            pltpu.VMEM((NX, 64, D), BF16),
            pltpu.VMEM((1024, 256), F32),
            pltpu.VMEM((512, 256), BF16),
            pltpu.VMEM((512, 256), BF16),
            pltpu.VMEM((NA, 64, 256), BF16),
            pltpu.VMEM((NA, 64, 256), BF16),
            pltpu.VMEM((NA, 8, 256), F32),
            pltpu.VMEM((NA, 8, 256), F32),
            pltpu.VMEM((D, 384), BF16),
            pltpu.VMEM((2, NX, 96, 384), BF16),
            pltpu.VMEM((2, NX, 2, 96, 384), BF16),
            pltpu.VMEM((NX, 8, D), F32),
            dma((24,)), dma((24,)),
            dma((24,)), dma((24,)),
            dma((16,)), dma((16,)),
            dma((40,)), dma((40,)),
            dma((32,)), dma((32,)),
            dma((8,)), dma((8,)),
            dma((16,)), dma((16,)),
            dma((28,)), dma((28,)),
            dma((8,)), dma((16,)),
        ],
        compiler_params=pltpu.CompilerParams(
            collective_id=0, has_side_effects=True, vmem_limit_bytes=62 * 1024 * 1024
        ),
    )(
        text_features,
        norm_gain,
        norm_bias,
        projection,
        image_embeddings,
        adapter,
        slab_ids,
        positive_rows,
    )
    text_grad, gain_grad, bias_grad, projection_grad, adapter_grad = pl.pallas_call(
        finish,
        out_shape=(
            jax.ShapeDtypeStruct((ROWS, D), F32),
            jax.ShapeDtypeStruct((D,), F32),
            jax.ShapeDtypeStruct((D,), F32),
            jax.ShapeDtypeStruct((D, D), BF16),
            jax.ShapeDtypeStruct((6, 192), F32),
        ),
        in_specs=[pl.BlockSpec(memory_space=pl.ANY)] * 2,
        out_specs=(pl.BlockSpec(memory_space=pl.ANY),) * 5,
        scratch_shapes=[
            pltpu.VMEM((16, D), F32),
            pltpu.VMEM((D, D), BF16),
            pltpu.VMEM((ROWS, D), F32),
            pltpu.VMEM((D,), F32),
            pltpu.VMEM((D,), F32),
            pltpu.VMEM((6, 192), F32),
            dma((5,)), dma((8,)),
        ],
        compiler_params=pltpu.CompilerParams(vmem_limit_bytes=62 * 1024 * 1024),
    )(small, projection_grad)
    return text_grad, gain_grad, bias_grad, projection_grad, adapter_grad.T


def solution(mesh):
    placed = (
        P(("corpus", "query"), None),
        P(),
        P(),
        P(),
        P("corpus", None),
        P(),
        P("corpus"),
        P(("corpus", "query")),
    )
    return jax.shard_map(
        shards,
        mesh=mesh,
        in_specs=placed,
        out_specs=(P(("corpus", "query"), None), P(), P(), P(), P("query", "corpus")),
        check_vma=False,
    )
```

```python
import functools

import jax
import jax.numpy as jnp
from jax import lax
from jax.experimental import pallas as pl
from jax.experimental.pallas import tpu as pltpu
from jax.sharding import PartitionSpec as P

F32 = jnp.float32
BF16 = jnp.bfloat16
MESH = pl.DeviceIdType.MESH

D = 768
SLAB = 256
ROWS = 4
NA = 8
NX = 4
GROUP = 512
ORDER = (1, 7, 2, 6, 3, 5, 4)
XORDER = (1, 3, 2)
FIRST = ORDER[::-1]
XFIRST = XORDER[::-1]


def dot(a, b):
    return jnp.dot(a, b, preferred_element_type=F32)


def dot_rows(a, b):
    return lax.dot_general(a, b, (((0,), (0,)), ((), ())), preferred_element_type=F32)


def dot_cols(a, b):
    return lax.dot_general(a, b, (((1,), (1,)), ((), ())), preferred_element_type=F32)


def iota(shape, axis):
    return lax.broadcasted_iota(jnp.int32, shape, axis)


def spread_matrix():
    row, col = iota((32, 128), 0), iota((32, 128), 1)
    return jnp.where((row >> 2) * 16 + (row & 3) == col, F32(1.0), F32(0.0)).astype(BF16)


def normalise(features, gain, bias):
    average = jnp.mean(features, axis=1, keepdims=True)
    centred = features - average
    spread = jnp.sqrt(jnp.mean(centred * centred, axis=1, keepdims=True) + 1e-5)
    normed = centred * (1.0 / spread)
    return normed, spread, (normed * gain + bias).astype(BF16)


def unit_rows(raw):
    length = jnp.sqrt(jnp.sum(raw * raw, axis=1, keepdims=True) + 1e-6)
    return raw * (1.0 / length), length


def kernel(
    tf_hbm, gain_hbm, bias_hbm, proj_hbm, emb_hbm, adapter_hbm, ids_hbm, rows_hbm,
    small_out, proj_out,
    gain_ref, bias_ref, proj_ref, emb_ref, adapter_ref, ids_ref, rows_ref,
    gt, g0, g1, gx, g2, unit_key, key_half, key_len, emb_sel, perm,
    normed_all, shifted_all, query_half, unit_all, len_all, spread_all, xt,
    negs, poss, negs_half, poss_half, weights,
    stat_send, stat_core, stat_a, stat_b,
    q_send, q_own, q_core, qb_send, qb_recv, qa_recv,
    k_send, k_recv, krg, s_own, s_send, s_core, sb_send, sb_recv, sa_send, sa_recv,
    p_send, p_recv, p_out, gb_recv,
    ag1_ss, ag1_rs, x_ss, x_rs, st_ss, st_rs, q_ss, q_rs, ag2_ss, ag2_rs, k_ss, k_rs,
    s_ss, s_rs, p_ss, p_rs, in_sem, out_sem,
):
    corpus = lax.axis_index("corpus")
    x = lax.axis_index("query")
    c = lax.rem(corpus, 2)
    y = corpus // 16
    z = lax.rem(corpus // 2, 8)
    a = z + c * (y - z)
    b = y + c * (z - y)
    step_a = 2 + 14 * c
    step_b = 16 - 14 * c

    def on_a(k):
        place = lax.rem(a + k, NA)
        return place, (place * step_a + b * step_b + c, x)

    def on_b(k):
        place = lax.rem(b + k, NA)
        return place, (a * step_a + place * step_b + c, x)

    def on_x(k):
        place = lax.rem(x + k, NX)
        return place, (corpus, place)

    partner = (corpus + 1 - 2 * c, x)
    pending = []

    def send(src, dst, send_sem, recv_sem, device):
        copy = pltpu.make_async_remote_copy(
            src_ref=src, dst_ref=dst, send_sem=send_sem, recv_sem=recv_sem,
            device_id=device, device_id_type=MESH,
        )
        copy.start()
        pending.append(copy)

    def arrived(dst, recv_sem):
        pltpu.make_async_remote_copy(
            src_ref=dst, dst_ref=dst, send_sem=recv_sem, recv_sem=recv_sem,
            device_id=partner, device_id_type=MESH,
        ).wait_recv()

    barrier = pltpu.get_barrier_semaphore()
    pl.semaphore_signal(barrier, inc=1, device_id=partner, device_id_type=MESH)
    for k in range(1, NA):
        pl.semaphore_signal(barrier, inc=1, device_id=on_a(k)[1], device_id_type=MESH)
        pl.semaphore_signal(barrier, inc=1, device_id=on_b(k)[1], device_id_type=MESH)
    for k in range(1, NX):
        pl.semaphore_signal(barrier, inc=1, device_id=on_x(k)[1], device_id_type=MESH)

    loads = [
        pltpu.make_async_copy(src, dst, in_sem.at[i])
        for i, (src, dst) in enumerate((
            (tf_hbm, gt.at[a]), (ids_hbm, ids_ref), (rows_hbm, rows_ref), (emb_hbm, emb_ref),
            (adapter_hbm, adapter_ref), (gain_hbm, gain_ref), (bias_hbm, bias_ref),
            (proj_hbm, proj_ref),
        ))
    ]
    for load in loads:
        load.start()

    pl.semaphore_wait(barrier, 2 * (NA - 1) + NX)
    for k in FIRST:
        send(tf_hbm, gt.at[a], ag1_ss.at[k], ag1_rs.at[k], on_a(k)[1])

    for load in loads[1:3]:
        load.wait()
    id_row = ids_ref[...].reshape(1, SLAB)
    row16, col16 = iota((16, SLAB), 0), iota((16, SLAB), 1)
    quarter_ids = jnp.where(col16 >> 6 == row16, id_row, 0)
    both = jnp.concatenate([quarter_ids >> 7, quarter_ids & 127], axis=1)
    bring = jnp.where(
        iota((512, 128), 1) == (iota((512, 128), 0) & 63) + 64 * (iota((512, 128), 0) >> 8),
        F32(1.0), F32(0.0),
    ).astype(BF16)
    listed = dot(both.astype(F32).astype(BF16), bring)
    wanted_row = jnp.sum(
        jnp.where(
            iota((16, ROWS), 0) == iota((16, ROWS), 1),
            rows_ref[...].reshape(1, ROWS).astype(F32), F32(0.0),
        ),
        axis=1, keepdims=True,
    ).astype(jnp.int32)
    device, inner = wanted_row >> 8, wanted_row & 255
    core, there_y, there_z = device & 1, device >> 4, (device >> 1) & 7
    slot = core * 64 + jnp.where(core == 0, there_y * 8 + there_z, there_z * 8 + there_y)
    row = slot * 4 + (inner >> 6)
    lane = iota((16, 128), 1)
    places = jnp.where(
        lane == 0, row >> 3, jnp.where(lane == 1, row & 7, jnp.where(lane == 2, inner & 63, 0))
    ).astype(F32)
    rest = jnp.concatenate([listed, places], axis=1)
    own = g0.at[pl.ds(pl.multiple_of(a * 16, 16), 16), :]
    g0[pl.ds(pl.multiple_of(a * 16, 16), 16), :] = rest.astype(BF16)
    for k in FIRST:
        send(own, own, x_ss.at[k], x_rs.at[k], on_a(k)[1])

    own_ids = jnp.broadcast_to(id_row.astype(F32), (128, SLAB)).T[:, 0:1]

    for load in loads[3:]:
        load.wait()
    gain = gain_ref[...].reshape(1, D)
    bias = bias_ref[...].reshape(1, D)

    @pl.loop(0, SLAB // 128)
    def _(i):
        rows = pl.ds(pl.multiple_of(i * 128, 128), 128)
        unit, length = unit_rows(dot(emb_ref[rows, :], adapter_ref[...]))
        unit_key[rows, :] = unit
        key_half[rows, :] = unit.astype(BF16)
        key_len[rows, :] = jnp.broadcast_to(length, (128, 128))

    for k in ORDER:
        arrived(gt.at[on_a(NA - k)[0]], ag1_rs.at[k])

    def widen(g, ss, rs):
        for k in FIRST:
            send(g.at[0, b], g.at[0, b], ss.at[8 + k], rs.at[8 + k], on_b(k)[1])

    loads[0].wait()
    g1[0, b] = jnp.concatenate([gt[i].astype(F32) for i in range(NA)], axis=0).astype(BF16)
    widen(g1, ag1_ss, ag1_rs)
    send(g1.at[0, b], g1.at[1, b], ag1_ss.at[16], ag1_rs.at[16], partner)
    for k in ORDER:
        place = on_a(NA - k)[0]
        arrived(g0.at[pl.ds(pl.multiple_of(place * 16, 16), 16), :], x_rs.at[k])
    gx[0, b] = dot(spread_matrix(), g0[...]).astype(BF16)
    widen(gx, x_ss, x_rs)

    def forward(g, ss, rs, k):
        place = on_b(NA - k)[0]
        arrived(g.at[0, place], rs.at[8 + k])
        send(g.at[0, place], g.at[1, place], ss.at[16 + k], rs.at[16 + k], partner)

    def from_core(k):
        return lax.rem(a + NA - k, NA) if k else a

    def query_block(region, places):
        shifts = []
        for place in places:
            normed, spread, shifted = normalise(g1[region, place].astype(F32), gain, bias)
            rows = pl.ds(pl.multiple_of(region * 256 + place * 32, 32), 32)
            normed_all[rows, :] = normed
            shifted_all[rows, :] = shifted
            if region == 0:
                spread_all[rows, :] = jnp.broadcast_to(spread, (32, 128))
            shifts.append(shifted)
        unit, length = unit_rows(dot(jnp.concatenate(shifts, axis=0), proj_ref[...]))
        for i, place in enumerate(places):
            rows = pl.ds(pl.multiple_of(region * 256 + place * 32, 32), 32)
            piece = slice(i * 32, i * 32 + 32)
            query_half[rows, :] = unit[piece].astype(BF16)
            if region == 0:
                unit_all[rows, :] = unit[piece]
                len_all[rows, :] = jnp.broadcast_to(length[piece], (32, 128))

    near, far = ORDER[:3], ORDER[3:]
    for k in near:
        forward(g1, ag1_ss, ag1_rs, k)
    query_block(0, [b] + [on_b(NA - k)[0] for k in near])
    for k in (0,) + near:
        arrived(g1.at[1, from_core(k)], ag1_rs.at[16 + k])
    query_block(1, [from_core(k) for k in (0,) + near])
    for k in far:
        forward(g1, ag1_ss, ag1_rs, k)
    query_block(0, [on_b(NA - k)[0] for k in far])
    for k in ORDER:
        arrived(gx.at[0, on_b(NA - k)[0]], x_rs.at[8 + k])
    send(gx.at[0], gx.at[1], x_ss.at[16], x_rs.at[16], partner)
    for k in far:
        arrived(g1.at[1, from_core(k)], ag1_rs.at[16 + k])
    query_block(1, [from_core(k) for k in far])
    arrived(gx.at[1], x_rs.at[16])

    for region in range(2):
        for i in range(2):
            table = gx[region, i * 4:i * 4 + 4].reshape(128, 256).astype(F32)
            first = region * 256 + i * 128
            xt[:, first:first + 128] = table.T

    high = xt[128:129, :].astype(jnp.int32)
    low = xt[129:130, :].astype(jnp.int32)
    lane = xt[130:131, :].astype(jnp.int32)
    slot = (high * 8 + low + 256 * c) & 511
    choose = jnp.where(iota((512, 512), 0) == slot, F32(1.0), F32(0.0)).astype(BF16)
    found = dot(xt[0:128, :].astype(BF16), choose)
    where_row = iota((128, 512), 0)
    target = jnp.sum(
        jnp.where(where_row == lane, found * 128.0, F32(0.0))
        + jnp.where(where_row == lane + 64, found, F32(0.0)),
        axis=0, keepdims=True,
    )


    negatives, positives = [], []
    for i in range(4):
        cols = slice(i * 128, i * 128 + 128)
        e = jnp.exp(64.0 * dot_cols(key_half[...], query_half[cols, :]))
        hit = own_ids == target[:, cols]
        n = jnp.where(hit, F32(0.0), e)
        p = jnp.where(hit, e, F32(0.0))
        negs[:, cols] = n
        poss[:, cols] = p
        negs_half[:, cols] = n.astype(BF16)
        poss_half[:, cols] = p.astype(BF16)
        negatives.append(jnp.sum(n, axis=0, keepdims=True))
        positives.append(jnp.sum(p, axis=0, keepdims=True))
    mine = jnp.concatenate(negatives + positives, axis=0)
    stat_send[0] = jnp.concatenate(
        [negatives[2], negatives[3], negatives[0], negatives[1],
         positives[2], positives[3], positives[0], positives[1]], axis=0
    )

    send(stat_send.at[0], stat_core, st_ss.at[0], st_rs.at[0], partner)
    for part, half in enumerate((negs_half, poss_half)):
        q_send[part] = dot_rows(half[:, 256:512], key_half[...]).astype(BF16)
        send(q_send.at[part], q_core.at[part], q_ss.at[part], q_rs.at[part], partner)

    arrived(stat_core, st_rs.at[0])
    mine = mine + stat_core[...]
    stat_a[a] = mine
    for k in FIRST:
        send(stat_a.at[a], stat_a.at[a], st_ss.at[k], st_rs.at[k], on_a(k)[1])

    for part, half in enumerate((negs_half, poss_half)):
        q_own[part] = dot_rows(half[:, 0:256], key_half[...])
    for part in range(2):
        arrived(q_core.at[part], q_rs.at[part])

    for h in range(2):

        @pl.loop(0, NA)
        def _(i):
            rows = pl.ds(pl.multiple_of(i * 32 + h * 16, 16), 16)
            for part in range(2):
                qb_send[i, h, part] = (
                    q_own[part, rows, :] + q_core[part, rows, :].astype(F32)
                ).astype(BF16)

        for k in FIRST:
            there, device = on_b(k)
            send(qb_send.at[there, h], qb_recv.at[b, h],
                 q_ss.at[8 + 8 * h + k], q_rs.at[8 + 8 * h + k], device)
    qb_recv[b] = qb_send[b]

    for k in ORDER:
        arrived(stat_a.at[on_a(NA - k)[0]], st_rs.at[k])
    stat_b[b] = jnp.sum(stat_a[...], axis=0)
    for k in FIRST:
        send(stat_b.at[b], stat_b.at[b], st_ss.at[8 + k], st_rs.at[8 + k], on_b(k)[1])

    pick = jnp.where(
        (iota((D, 256), 0) == iota((D, 256), 1) + x * 192) & (iota((D, 256), 1) < 192),
        F32(1.0), F32(0.0),
    ).astype(BF16)
    emb_sel[...] = dot(emb_ref[...], pick).astype(BF16)
    place = iota((1, 1024), 1)
    core = ((place >> 9) + c) & 1
    place_b, place_a = (place >> 6) & 7, (place >> 3) & 7
    place_y = jnp.where(core == 0, place_b, place_a)
    place_z = place_a + place_b - place_y
    column = jnp.where(
        (place & 7) < 6, 6 * (place_y * 16 + place_z * 2 + core) + (place & 7), -1
    )

    @pl.loop(0, D // 128)
    def _(i):
        rows = pl.ds(pl.multiple_of(i * 128, 128), 128)
        perm[rows, :] = jnp.where(
            iota((128, 1024), 0) + i * 128 == column, F32(1.0), F32(0.0)
        ).astype(BF16)

    for k in ORDER:
        arrived(stat_b.at[on_b(NA - k)[0]], st_rs.at[8 + k])
    stats = jnp.sum(stat_b[...], axis=0)
    by_total = 64.0 / (stats[0:4] + stats[4:8])
    by_positive = 1.0 / stats[4:8]
    share_negative = stats[0:4] * by_total

    def as_column(rows, h):
        wide = jnp.concatenate([rows[0:1], rows[1:2]], axis=1)
        diagonal = iota((16, SLAB), 1) == iota((16, SLAB), 0) + (b * 32 + h * 16)
        return jnp.sum(jnp.where(diagonal, wide, F32(0.0)), axis=1, keepdims=True)

    def combine(h):
        for k in ORDER:
            arrived(qb_recv.at[on_b(NA - k)[0], h], q_rs.at[8 + 8 * h + k])
        sums = []
        for part in range(2):
            total = qb_recv[0, h, part].astype(F32)
            for i in range(1, NA):
                total = total + qb_recv[i, h, part].astype(F32)
            sums.append(total)
        qa_recv[h, a] = (
            sums[0] * as_column(by_total, h)
            - (sums[1] * as_column(by_positive, h)) * as_column(share_negative, h)
        ).astype(BF16)
        for k in FIRST:
            send(qa_recv.at[h, a], qa_recv.at[h, a],
                 q_ss.at[24 + 8 * h + k], q_rs.at[24 + 8 * h + k], on_a(k)[1])

    combine(0)

    for i in range(4):
        cols = slice(i * 128, i * 128 + 128)
        weights[:, cols] = (
            negs[:, cols] * by_total[i:i + 1, :]
            - (poss[:, cols] * by_positive[i:i + 1, :]) * share_negative[i:i + 1, :]
        ).astype(BF16)

    @pl.loop(0, NX)
    def _(i):
        rows = pl.ds(pl.multiple_of(i * 64, 64), 64)
        k_send[i] = dot(weights[rows, :], query_half[...]).astype(BF16)

    for k in XFIRST:
        there, device = on_x(k)
        send(k_send.at[there], k_recv.at[x], k_ss.at[k], k_rs.at[k], device)
    k_recv[x] = k_send[x]

    combine(1)

    for k in XORDER:
        arrived(k_recv.at[on_x(NX - k)[0]], k_rs.at[k])
    quarter = pl.ds(pl.multiple_of(x * 64, 64), 64)
    key_sum = (
        (k_recv[0].astype(F32) + k_recv[1].astype(F32)) + k_recv[2].astype(F32)
    ) + k_recv[3].astype(F32)
    unit = unit_key[quarter, :]
    krg[x] = (
        (key_sum - unit * jnp.sum(unit * key_sum, axis=1, keepdims=True))
        * (1.0 / key_len[quarter, 0:1])
    ).astype(BF16)
    for k in XFIRST:
        send(krg.at[x], krg.at[x], k_ss.at[4 + k], k_rs.at[4 + k], on_x(k)[1])

    for h in range(2):
        for k in ORDER:
            arrived(qa_recv.at[h, on_a(NA - k)[0]], q_rs.at[24 + 8 * h + k])
        query_sum = qa_recv[h, 0].astype(F32)
        for i in range(1, NA):
            query_sum = query_sum + qa_recv[h, i].astype(F32)
        rows = pl.ds(pl.multiple_of(b * 32 + h * 16, 16), 16)
        unit = unit_all[rows, :]
        g2[0, b, h] = (
            (query_sum - unit * jnp.sum(unit * query_sum, axis=1, keepdims=True))
            * (1.0 / len_all[rows, 0:1])
        ).astype(BF16)
        for k in FIRST:
            send(g2.at[0, b, h], g2.at[0, b, h],
                 ag2_ss.at[8 * h + k], ag2_rs.at[8 * h + k], on_b(k)[1])
        send(g2.at[0, b, h], g2.at[1, b, h], ag2_ss.at[16 + 8 * h], ag2_rs.at[16 + 8 * h], partner)

    shifted_grad = dot_cols(g2[0, b].reshape(32, D), proj_ref[...])
    block = pl.ds(pl.multiple_of(b * 32, 32), 32)
    scaled = shifted_grad * gain
    normed = normed_all[block, :]
    text = (
        scaled
        - jnp.mean(scaled, axis=1, keepdims=True)
        - normed * jnp.mean(scaled * normed, axis=1, keepdims=True)
    ) * (1.0 / spread_all[block, 0:1])
    own_text = text[0:4]
    for i in range(1, NA):
        own_text = jnp.where(a == i, text[i * 4:i * 4 + 4], own_text)
    small_out[0:4, :] = own_text

    for k in XORDER:
        arrived(krg.at[on_x(NX - k)[0]], k_rs.at[4 + k])
    grads = krg[...].reshape(SLAB, D)

    @pl.loop(0, 4)
    def _(i):
        half = i // 2
        cols = pl.ds(pl.multiple_of((3 - i) * 256, 256), 256)
        spread_out = dot(grads, perm[:, cols]).astype(BF16)
        share = dot_rows(spread_out, emb_sel[...])
        rows = pl.ds(pl.multiple_of((3 - i) * 256, 256), 256)
        s_own[rows, :] = share

    s_send[...] = s_own[512:1024, :].astype(BF16)
    send(s_send, s_core, s_ss.at[0], s_rs.at[0], partner)

    for h in range(2):
        for k in ORDER:
            place = on_b(NA - k)[0]
            arrived(g2.at[0, place, h], ag2_rs.at[8 * h + k])
            send(g2.at[0, place, h], g2.at[1, place, h],
                 ag2_ss.at[16 + 8 * h + k], ag2_rs.at[16 + 8 * h + k], partner)
    arrived(s_core, s_rs.at[0])
    for i in range(NA):
        rows = slice(i * 64, i * 64 + 64)
        sb_send[i] = (s_own[rows, :] + s_core[rows, :].astype(F32)).astype(BF16)
    for k in FIRST:
        there, device = on_b(k)
        send(sb_send.at[there], sb_recv.at[b], s_ss.at[8 + k], s_rs.at[8 + k], device)
    sb_recv[b] = sb_send[b]

    for h in range(2):
        for k in (0,) + ORDER:
            arrived(g2.at[1, from_core(k), h], ag2_rs.at[16 + 8 * h + k])

    cols = pl.ds(pl.multiple_of(c * 384, 128), 384)
    half = g2[:, :, :, :, cols].reshape(GROUP, 384)
    for i in range(D // 128):
        band = slice(i * 128, i * 128 + 128)
        p_send[band, :] = dot_rows(shifted_all[:, band], half).astype(BF16)
    for h in range(2):
        for k in XFIRST:
            there, device = on_x(k)
            send(p_send.at[pl.ds(pl.multiple_of(there * 192 + h * 96, 32), 96), :],
                 p_recv.at[h, x], p_ss.at[4 * h + k], p_rs.at[4 * h + k], device)
        p_recv[h, x] = p_send[pl.ds(pl.multiple_of(x * 192 + h * 96, 32), 96), :]

    gain_sum = jnp.zeros((1, D), F32)
    bias_sum = jnp.zeros((1, D), F32)
    for i in range(4):
        rows = slice(i * 128, i * 128 + 128)
        quads = slice(i % 2 * 4, i % 2 * 4 + 4)
        grad = dot_cols(g2[i // 2, quads].reshape(128, D), proj_ref[...])
        gain_sum = gain_sum + jnp.sum(grad * normed_all[rows, :], axis=0, keepdims=True)
        bias_sum = bias_sum + jnp.sum(grad, axis=0, keepdims=True)
    gb_recv[x] = jnp.concatenate([gain_sum, bias_sum, jnp.zeros((6, D), F32)], axis=0)
    for k in XFIRST:
        send(gb_recv.at[x], gb_recv.at[x], p_ss.at[8 + k], p_rs.at[8 + k], on_x(k)[1])

    stores = []

    def store(side, place, h, i):
        rows = pl.ds(pl.multiple_of(place * 192 + h * 96, 32), 96)
        lanes = pl.ds(pl.multiple_of((c + side * (1 - 2 * c)) * 384, 128), 384)
        copy = pltpu.make_async_copy(
            p_out.at[side, place, h], proj_out.at[rows, lanes], out_sem.at[i]
        )
        copy.start()
        stores.append(copy)

    for copy in pending[:-30]:
        copy.wait_send()
    del pending[:-30]

    for h in range(2):
        for k in XORDER:
            arrived(p_recv.at[h, on_x(NX - k)[0]], p_rs.at[4 * h + k])
        total = (
            (p_recv[h, 0].astype(F32) + p_recv[h, 1].astype(F32)) + p_recv[h, 2].astype(F32)
        ) + p_recv[h, 3].astype(F32)
        p_out[0, x, h] = total.astype(BF16)
        for k in XFIRST:
            send(p_out.at[0, x, h], p_out.at[0, x, h],
                 p_ss.at[12 + 4 * h + k], p_rs.at[12 + 4 * h + k], on_x(k)[1])
        send(p_out.at[0, x, h], p_out.at[1, x, h], p_ss.at[20 + 4 * h], p_rs.at[20 + 4 * h], partner)
        store(0, x, h, 4 * h)
        if h == 0:
            for k in ORDER:
                arrived(sb_recv.at[on_b(NA - k)[0]], s_rs.at[8 + k])
            part = sb_recv[0].astype(F32)
            for i in range(1, NA):
                part = part + sb_recv[i].astype(F32)
            for i in range(NA):
                sa_send[i] = part[i * 8:i * 8 + 8, :]
            for k in FIRST:
                there, device = on_a(k)
                send(sa_send.at[there], sa_recv.at[a], s_ss.at[k], s_rs.at[k], device)
            sa_recv[a] = sa_send[a]

    for k in XORDER:
        arrived(gb_recv.at[on_x(NX - k)[0]], p_rs.at[8 + k])
    small_out[4:6, :] = jnp.sum(gb_recv[...], axis=0)[0:2]

    for k in ORDER:
        arrived(sa_recv.at[on_a(NA - k)[0]], s_rs.at[k])
    small_out[8:16, 0:256] = jnp.sum(sa_recv[...], axis=0)

    for h in range(2):
        for k in XORDER:
            there = on_x(NX - k)[0]
            arrived(p_out.at[0, there, h], p_rs.at[12 + 4 * h + k])
            send(p_out.at[0, there, h], p_out.at[1, there, h],
                 p_ss.at[20 + 4 * h + k], p_rs.at[20 + 4 * h + k], partner)
            store(0, there, h, 4 * h + k)
    for h in range(2):
        arrived(p_out.at[1, x, h], p_rs.at[20 + 4 * h])
        store(1, x, h, 8 + 4 * h)
        for k in XORDER:
            there = on_x(NX - k)[0]
            arrived(p_out.at[1, there, h], p_rs.at[20 + 4 * h + k])
            store(1, there, h, 8 + 4 * h + k)
    for copy in stores:
        copy.wait()
    for copy in pending:
        copy.wait_send()


def finish(
    small_hbm, part_hbm, text_hbm, gain_hbm, bias_hbm, proj_hbm, adapter_hbm,
    small, held, text, gain, bias, adapter, in_sem, out_sem,
):
    bands = [pl.ds(i * 192, 192) for i in range(4)]
    into = [pltpu.make_async_copy(small_hbm, small, in_sem.at[0])] + [
        pltpu.make_async_copy(part_hbm.at[band], held.at[band], in_sem.at[1 + i])
        for i, band in enumerate(bands)
    ]
    out = [
        pltpu.make_async_copy(held.at[band], proj_hbm.at[band], out_sem.at[i])
        for i, band in enumerate(bands)
    ] + [
        pltpu.make_async_copy(src, dst, out_sem.at[4 + i])
        for i, (src, dst) in enumerate((
            (text, text_hbm), (gain, gain_hbm), (bias, bias_hbm), (adapter, adapter_hbm)
        ))
    ]
    for copy in into:
        copy.start()
    into[0].wait()
    text[...] = small[0:4, :]
    gain[...] = small[4:5, :].reshape(D)
    bias[...] = small[5:6, :].reshape(D)
    adapter[...] = small[8:14, 0:192]
    for copy in out[4:]:
        copy.start()
    for first, second in zip(into[1:], out[:4]):
        first.wait()
        second.start()
    for copy in out:
        copy.wait()


def shards(
    text_features, norm_gain, norm_bias, projection, image_embeddings, adapter, slab_ids,
    positive_rows,
):
    whole = pl.BlockSpec(memory_space=pltpu.VMEM)
    dma = pltpu.SemaphoreType.DMA
    small, projection_grad = pl.pallas_call(
        kernel,
        out_shape=(
            jax.ShapeDtypeStruct((16, D), F32),
            jax.ShapeDtypeStruct((D, D), BF16),
        ),
        in_specs=[pl.BlockSpec(memory_space=pl.ANY)] * 8,
        out_specs=(whole, pl.BlockSpec(memory_space=pl.ANY)),
        scratch_shapes=[
            pltpu.VMEM((D,), F32),
            pltpu.VMEM((D,), F32),
            pltpu.VMEM((D, D), BF16),
            pltpu.VMEM((SLAB, D), BF16),
            pltpu.VMEM((D, D), BF16),
            pltpu.VMEM((SLAB,), jnp.int32),
            pltpu.VMEM((ROWS,), jnp.int32),
            pltpu.VMEM((NA, ROWS, D), BF16),
            pltpu.VMEM((128, 256), BF16),
            pltpu.VMEM((2, NA, 32, D), BF16),
            pltpu.VMEM((2, NA, 32, 256), BF16),
            pltpu.VMEM((2, NA, 2, 16, D), BF16),
            pltpu.VMEM((SLAB, D), F32),
            pltpu.VMEM((SLAB, D), BF16),
            pltpu.VMEM((SLAB, 128), F32),
            pltpu.VMEM((SLAB, 256), BF16),
            pltpu.VMEM((D, 1024), BF16),
            pltpu.VMEM((GROUP, D), F32),
            pltpu.VMEM((GROUP, D), BF16),
            pltpu.VMEM((GROUP, D), BF16),
            pltpu.VMEM((GROUP // 2, D), F32),
            pltpu.VMEM((GROUP // 2, 128), F32),
            pltpu.VMEM((GROUP // 2, 128), F32),
            pltpu.VMEM((256, GROUP), F32),
            pltpu.VMEM((SLAB, GROUP), F32),
            pltpu.VMEM((SLAB, GROUP), F32),
            pltpu.VMEM((SLAB, GROUP), BF16),
            pltpu.VMEM((SLAB, GROUP), BF16),
            pltpu.VMEM((SLAB, GROUP), BF16),
            pltpu.VMEM((1, 8, 128), F32),
            pltpu.VMEM((8, 128), F32),
            pltpu.VMEM((NA, 8, 128), F32),
            pltpu.VMEM((NA, 8, 128), F32),
            pltpu.VMEM((2, 256, D), BF16),
            pltpu.VMEM((2, 256, D), F32),
            pltpu.VMEM((2, 256, D), BF16),
            pltpu.VMEM((NA, 2, 2, 16, D), BF16),
            pltpu.VMEM((NA, 2, 2, 16, D), BF16),
            pltpu.VMEM((2, NA, 16, D), BF16),
            pltpu.VMEM((NX, 64, D), BF16),
            pltpu.VMEM((NX, 64, D), BF16),
            pltpu.VMEM((NX, 64, D), BF16),
            pltpu.VMEM((1024, 256), F32),
            pltpu.VMEM((512, 256), BF16),
            pltpu.VMEM((512, 256), BF16),
            pltpu.VMEM((NA, 64, 256), BF16),
            pltpu.VMEM((NA, 64, 256), BF16),
            pltpu.VMEM((NA, 8, 256), F32),
            pltpu.VMEM((NA, 8, 256), F32),
            pltpu.VMEM((D, 384), BF16),
            pltpu.VMEM((2, NX, 96, 384), BF16),
            pltpu.VMEM((2, NX, 2, 96, 384), BF16),
            pltpu.VMEM((NX, 8, D), F32),
            dma((24,)), dma((24,)),
            dma((24,)), dma((24,)),
            dma((16,)), dma((16,)),
            dma((40,)), dma((40,)),
            dma((32,)), dma((32,)),
            dma((8,)), dma((8,)),
            dma((16,)), dma((16,)),
            dma((28,)), dma((28,)),
            dma((8,)), dma((16,)),
        ],
        compiler_params=pltpu.CompilerParams(
            collective_id=0, has_side_effects=True, vmem_limit_bytes=62 * 1024 * 1024
        ),
    )(
        text_features,
        norm_gain,
        norm_bias,
        projection,
        image_embeddings,
        adapter,
        slab_ids,
        positive_rows,
    )
    text_grad, gain_grad, bias_grad, projection_grad, adapter_grad = pl.pallas_call(
        finish,
        out_shape=(
            jax.ShapeDtypeStruct((ROWS, D), F32),
            jax.ShapeDtypeStruct((D,), F32),
            jax.ShapeDtypeStruct((D,), F32),
            jax.ShapeDtypeStruct((D, D), BF16),
            jax.ShapeDtypeStruct((6, 192), F32),
        ),
        in_specs=[pl.BlockSpec(memory_space=pl.ANY)] * 2,
        out_specs=(pl.BlockSpec(memory_space=pl.ANY),) * 5,
        scratch_shapes=[
            pltpu.VMEM((16, D), F32),
            pltpu.VMEM((D, D), BF16),
            pltpu.VMEM((ROWS, D), F32),
            pltpu.VMEM((D,), F32),
            pltpu.VMEM((D,), F32),
            pltpu.VMEM((6, 192), F32),
            dma((5,)), dma((8,)),
        ],
        compiler_params=pltpu.CompilerParams(vmem_limit_bytes=62 * 1024 * 1024),
    )(small, projection_grad)
    return text_grad, gain_grad, bias_grad, projection_grad, adapter_grad.T


def solution(mesh):
    placed = (
        P(("corpus", "query"), None),
        P(),
        P(),
        P(),
        P("corpus", None),
        P(),
        P("corpus"),
        P(("corpus", "query")),
    )
    return jax.shard_map(
        shards,
        mesh=mesh,
        in_specs=placed,
        out_specs=(P(("corpus", "query"), None), P(), P(), P(), P("query", "corpus")),
        check_vma=False,
    )
```

```python
import functools

import jax
import jax.numpy as jnp
from jax import lax
from jax.experimental import pallas as pl
from jax.experimental.pallas import tpu as pltpu
from jax.sharding import PartitionSpec as P

F32 = jnp.float32
BF16 = jnp.bfloat16
MESH = pl.DeviceIdType.MESH

D = 768
SLAB = 256
ROWS = 4
NA = 8
NX = 4
GROUP = 512
ORDER = (1, 7, 2, 6, 3, 5, 4)
XORDER = (1, 3, 2)
FIRST = ORDER[::-1]
XFIRST = XORDER[::-1]


def dot(a, b):
    return jnp.dot(a, b, preferred_element_type=F32)


def dot_rows(a, b):
    return lax.dot_general(a, b, (((0,), (0,)), ((), ())), preferred_element_type=F32)


def dot_cols(a, b):
    return lax.dot_general(a, b, (((1,), (1,)), ((), ())), preferred_element_type=F32)


def iota(shape, axis):
    return lax.broadcasted_iota(jnp.int32, shape, axis)


def spread_matrix():
    row, col = iota((32, 128), 0), iota((32, 128), 1)
    return jnp.where((row >> 2) * 16 + (row & 3) == col, F32(1.0), F32(0.0)).astype(BF16)


def normalise(features, gain, bias):
    average = jnp.mean(features, axis=1, keepdims=True)
    centred = features - average
    spread = jnp.sqrt(jnp.mean(centred * centred, axis=1, keepdims=True) + 1e-5)
    normed = centred * (1.0 / spread)
    return normed, spread, (normed * gain + bias).astype(BF16)


def unit_rows(raw):
    length = jnp.sqrt(jnp.sum(raw * raw, axis=1, keepdims=True) + 1e-6)
    return raw * (1.0 / length), length


def kernel(
    tf_hbm, gain_hbm, bias_hbm, proj_hbm, emb_hbm, adapter_hbm, ids_hbm, rows_hbm,
    small_out, proj_out,
    gain_ref, bias_ref, proj_ref, emb_ref, adapter_ref, ids_ref, rows_ref,
    gt, g0, g1, gx, g2, unit_key, key_half, key_len, emb_sel, perm,
    normed_all, shifted_all, query_half, unit_all, len_all, spread_all, xt,
    negs, poss, negs_half, poss_half, weights,
    stat_send, stat_core, stat_a, stat_b,
    q_send, q_own, q_core, qb_send, qb_recv, qa_recv,
    k_send, k_recv, krg, s_own, s_send, s_core, sb_send, sb_recv, sa_send, sa_recv,
    p_send, p_recv, p_out, gb_recv,
    ag1_ss, ag1_rs, x_ss, x_rs, st_ss, st_rs, q_ss, q_rs, ag2_ss, ag2_rs, k_ss, k_rs,
    s_ss, s_rs, p_ss, p_rs, in_sem, out_sem,
):
    corpus = lax.axis_index("corpus")
    x = lax.axis_index("query")
    c = lax.rem(corpus, 2)
    y = corpus // 16
    z = lax.rem(corpus // 2, 8)
    a = z + c * (y - z)
    b = y + c * (z - y)
    step_a = 2 + 14 * c
    step_b = 16 - 14 * c

    def on_a(k):
        place = lax.rem(a + k, NA)
        return place, (place * step_a + b * step_b + c, x)

    def on_b(k):
        place = lax.rem(b + k, NA)
        return place, (a * step_a + place * step_b + c, x)

    def on_x(k):
        place = lax.rem(x + k, NX)
        return place, (corpus, place)

    partner = (corpus + 1 - 2 * c, x)
    pending = []

    def send(src, dst, send_sem, recv_sem, device):
        copy = pltpu.make_async_remote_copy(
            src_ref=src, dst_ref=dst, send_sem=send_sem, recv_sem=recv_sem,
            device_id=device, device_id_type=MESH,
        )
        copy.start()
        pending.append(copy)

    def arrived(dst, recv_sem):
        pltpu.make_async_remote_copy(
            src_ref=dst, dst_ref=dst, send_sem=recv_sem, recv_sem=recv_sem,
            device_id=partner, device_id_type=MESH,
        ).wait_recv()

    barrier = pltpu.get_barrier_semaphore()
    pl.semaphore_signal(barrier, inc=1, device_id=partner, device_id_type=MESH)
    for k in range(1, NA):
        pl.semaphore_signal(barrier, inc=1, device_id=on_a(k)[1], device_id_type=MESH)
        pl.semaphore_signal(barrier, inc=1, device_id=on_b(k)[1], device_id_type=MESH)
    for k in range(1, NX):
        pl.semaphore_signal(barrier, inc=1, device_id=on_x(k)[1], device_id_type=MESH)

    loads = [
        pltpu.make_async_copy(src, dst, in_sem.at[i])
        for i, (src, dst) in enumerate((
            (tf_hbm, gt.at[a]), (ids_hbm, ids_ref), (rows_hbm, rows_ref), (emb_hbm, emb_ref),
            (adapter_hbm, adapter_ref), (gain_hbm, gain_ref), (bias_hbm, bias_ref),
            (proj_hbm, proj_ref),
        ))
    ]
    for load in loads:
        load.start()

    pl.semaphore_wait(barrier, 2 * (NA - 1) + NX)
    for k in FIRST:
        send(tf_hbm, gt.at[a], ag1_ss.at[k], ag1_rs.at[k], on_a(k)[1])

    for load in loads[1:3]:
        load.wait()
    id_row = ids_ref[...].reshape(1, SLAB)
    row16, col16 = iota((16, SLAB), 0), iota((16, SLAB), 1)
    quarter_ids = jnp.where(col16 >> 6 == row16, id_row, 0)
    both = jnp.concatenate([quarter_ids >> 7, quarter_ids & 127], axis=1)
    bring = jnp.where(
        iota((512, 128), 1) == (iota((512, 128), 0) & 63) + 64 * (iota((512, 128), 0) >> 8),
        F32(1.0), F32(0.0),
    ).astype(BF16)
    listed = dot(both.astype(F32).astype(BF16), bring)
    wanted_row = jnp.sum(
        jnp.where(
            iota((16, ROWS), 0) == iota((16, ROWS), 1),
            rows_ref[...].reshape(1, ROWS).astype(F32), F32(0.0),
        ),
        axis=1, keepdims=True,
    ).astype(jnp.int32)
    device, inner = wanted_row >> 8, wanted_row & 255
    core, there_y, there_z = device & 1, device >> 4, (device >> 1) & 7
    slot = core * 64 + jnp.where(core == 0, there_y * 8 + there_z, there_z * 8 + there_y)
    row = slot * 4 + (inner >> 6)
    lane = iota((16, 128), 1)
    places = jnp.where(
        lane == 0, row >> 3, jnp.where(lane == 1, row & 7, jnp.where(lane == 2, inner & 63, 0))
    ).astype(F32)
    rest = jnp.concatenate([listed, places], axis=1)
    own = g0.at[pl.ds(pl.multiple_of(a * 16, 16), 16), :]
    g0[pl.ds(pl.multiple_of(a * 16, 16), 16), :] = rest.astype(BF16)
    for k in FIRST:
        send(own, own, x_ss.at[k], x_rs.at[k], on_a(k)[1])

    own_ids = jnp.broadcast_to(id_row.astype(F32), (128, SLAB)).T[:, 0:1]

    for load in loads[3:]:
        load.wait()
    gain = gain_ref[...].reshape(1, D)
    bias = bias_ref[...].reshape(1, D)

    @pl.loop(0, SLAB // 128)
    def _(i):
        rows = pl.ds(pl.multiple_of(i * 128, 128), 128)
        unit, length = unit_rows(dot(emb_ref[rows, :], adapter_ref[...]))
        unit_key[rows, :] = unit
        key_half[rows, :] = unit.astype(BF16)
        key_len[rows, :] = jnp.broadcast_to(length, (128, 128))

    for k in ORDER:
        arrived(gt.at[on_a(NA - k)[0]], ag1_rs.at[k])

    def widen(g, ss, rs):
        for k in FIRST:
            send(g.at[0, b], g.at[0, b], ss.at[8 + k], rs.at[8 + k], on_b(k)[1])

    loads[0].wait()
    g1[0, b] = jnp.concatenate([gt[i].astype(F32) for i in range(NA)], axis=0).astype(BF16)
    widen(g1, ag1_ss, ag1_rs)
    send(g1.at[0, b], g1.at[1, b], ag1_ss.at[16], ag1_rs.at[16], partner)
    for k in ORDER:
        place = on_a(NA - k)[0]
        arrived(g0.at[pl.ds(pl.multiple_of(place * 16, 16), 16), :], x_rs.at[k])
    gx[0, b] = dot(spread_matrix(), g0[...]).astype(BF16)
    widen(gx, x_ss, x_rs)

    def forward(g, ss, rs, k):
        place = on_b(NA - k)[0]
        arrived(g.at[0, place], rs.at[8 + k])
        send(g.at[0, place], g.at[1, place], ss.at[16 + k], rs.at[16 + k], partner)

    def from_core(k):
        return lax.rem(a + NA - k, NA) if k else a

    def query_block(region, places):
        shifts = []
        for place in places:
            normed, spread, shifted = normalise(g1[region, place].astype(F32), gain, bias)
            rows = pl.ds(pl.multiple_of(region * 256 + place * 32, 32), 32)
            normed_all[rows, :] = normed
            shifted_all[rows, :] = shifted
            if region == 0:
                spread_all[rows, :] = jnp.broadcast_to(spread, (32, 128))
            shifts.append(shifted)
        unit, length = unit_rows(dot(jnp.concatenate(shifts, axis=0), proj_ref[...]))
        for i, place in enumerate(places):
            rows = pl.ds(pl.multiple_of(region * 256 + place * 32, 32), 32)
            piece = slice(i * 32, i * 32 + 32)
            query_half[rows, :] = unit[piece].astype(BF16)
            if region == 0:
                unit_all[rows, :] = unit[piece]
                len_all[rows, :] = jnp.broadcast_to(length[piece], (32, 128))

    near, far = ORDER[:3], ORDER[3:]
    for k in near:
        forward(g1, ag1_ss, ag1_rs, k)
    query_block(0, [b] + [on_b(NA - k)[0] for k in near])
    for k in (0,) + near:
        arrived(g1.at[1, from_core(k)], ag1_rs.at[16 + k])
    query_block(1, [from_core(k) for k in (0,) + near])
    for k in far:
        forward(g1, ag1_ss, ag1_rs, k)
    query_block(0, [on_b(NA - k)[0] for k in far])
    for k in ORDER:
        arrived(gx.at[0, on_b(NA - k)[0]], x_rs.at[8 + k])
    send(gx.at[0], gx.at[1], x_ss.at[16], x_rs.at[16], partner)
    for k in far:
        arrived(g1.at[1, from_core(k)], ag1_rs.at[16 + k])
    query_block(1, [from_core(k) for k in far])
    arrived(gx.at[1], x_rs.at[16])

    for region in range(2):
        for i in range(2):
            table = gx[region, i * 4:i * 4 + 4].reshape(128, 256).astype(F32)
            first = region * 256 + i * 128
            xt[:, first:first + 128] = table.T

    high = xt[128:129, :].astype(jnp.int32)
    low = xt[129:130, :].astype(jnp.int32)
    lane = xt[130:131, :].astype(jnp.int32)
    slot = (high * 8 + low + 256 * c) & 511
    choose = jnp.where(iota((512, 512), 0) == slot, F32(1.0), F32(0.0)).astype(BF16)
    found = dot(xt[0:128, :].astype(BF16), choose)
    where_row = iota((128, 512), 0)
    target = jnp.sum(
        jnp.where(where_row == lane, found * 128.0, F32(0.0))
        + jnp.where(where_row == lane + 64, found, F32(0.0)),
        axis=0, keepdims=True,
    )


    negatives, positives = [], []
    for i in range(4):
        cols = slice(i * 128, i * 128 + 128)
        e = jnp.exp(64.0 * dot_cols(key_half[...], query_half[cols, :]))
        hit = own_ids == target[:, cols]
        n = jnp.where(hit, F32(0.0), e)
        p = jnp.where(hit, e, F32(0.0))
        negs[:, cols] = n
        poss[:, cols] = p
        negs_half[:, cols] = n.astype(BF16)
        poss_half[:, cols] = p.astype(BF16)
        negatives.append(jnp.sum(n, axis=0, keepdims=True))
        positives.append(jnp.sum(p, axis=0, keepdims=True))
    mine = jnp.concatenate(negatives + positives, axis=0)
    stat_send[0] = jnp.concatenate(
        [negatives[2], negatives[3], negatives[0], negatives[1],
         positives[2], positives[3], positives[0], positives[1]], axis=0
    )

    send(stat_send.at[0], stat_core, st_ss.at[0], st_rs.at[0], partner)
    for part, half in enumerate((negs_half, poss_half)):
        q_send[part] = dot_rows(half[:, 256:512], key_half[...]).astype(BF16)
        send(q_send.at[part], q_core.at[part], q_ss.at[part], q_rs.at[part], partner)

    arrived(stat_core, st_rs.at[0])
    mine = mine + stat_core[...]
    stat_a[a] = mine
    for k in FIRST:
        send(stat_a.at[a], stat_a.at[a], st_ss.at[k], st_rs.at[k], on_a(k)[1])

    for part, half in enumerate((negs_half, poss_half)):
        q_own[part] = dot_rows(half[:, 0:256], key_half[...])
    for part in range(2):
        arrived(q_core.at[part], q_rs.at[part])

    for h in range(2):

        @pl.loop(0, NA)
        def _(i):
            rows = pl.ds(pl.multiple_of(i * 32 + h * 16, 16), 16)
            for part in range(2):
                qb_send[i, h, part] = (
                    q_own[part, rows, :] + q_core[part, rows, :].astype(F32)
                ).astype(BF16)

        for k in FIRST:
            there, device = on_b(k)
            send(qb_send.at[there, h], qb_recv.at[b, h],
                 q_ss.at[8 + 8 * h + k], q_rs.at[8 + 8 * h + k], device)
    qb_recv[b] = qb_send[b]

    for k in ORDER:
        arrived(stat_a.at[on_a(NA - k)[0]], st_rs.at[k])
    stat_b[b] = jnp.sum(stat_a[...], axis=0)
    for k in FIRST:
        send(stat_b.at[b], stat_b.at[b], st_ss.at[8 + k], st_rs.at[8 + k], on_b(k)[1])

    pick = jnp.where(
        (iota((D, 256), 0) == iota((D, 256), 1) + x * 192) & (iota((D, 256), 1) < 192),
        F32(1.0), F32(0.0),
    ).astype(BF16)
    emb_sel[...] = dot(emb_ref[...], pick).astype(BF16)
    place = iota((1, 1024), 1)
    core = ((place >> 9) + c) & 1
    place_b, place_a = (place >> 6) & 7, (place >> 3) & 7
    place_y = jnp.where(core == 0, place_b, place_a)
    place_z = place_a + place_b - place_y
    column = jnp.where(
        (place & 7) < 6, 6 * (place_y * 16 + place_z * 2 + core) + (place & 7), -1
    )

    @pl.loop(0, D // 128)
    def _(i):
        rows = pl.ds(pl.multiple_of(i * 128, 128), 128)
        perm[rows, :] = jnp.where(
            iota((128, 1024), 0) + i * 128 == column, F32(1.0), F32(0.0)
        ).astype(BF16)

    for k in ORDER:
        arrived(stat_b.at[on_b(NA - k)[0]], st_rs.at[8 + k])
    stats = jnp.sum(stat_b[...], axis=0)
    by_total = 64.0 / (stats[0:4] + stats[4:8])
    by_positive = 1.0 / stats[4:8]
    share_negative = stats[0:4] * by_total

    def as_column(rows, h):
        wide = jnp.concatenate([rows[0:1], rows[1:2]], axis=1)
        diagonal = iota((16, SLAB), 1) == iota((16, SLAB), 0) + (b * 32 + h * 16)
        return jnp.sum(jnp.where(diagonal, wide, F32(0.0)), axis=1, keepdims=True)

    def combine(h):
        for k in ORDER:
            arrived(qb_recv.at[on_b(NA - k)[0], h], q_rs.at[8 + 8 * h + k])
        sums = []
        for part in range(2):
            total = qb_recv[0, h, part].astype(F32)
            for i in range(1, NA):
                total = total + qb_recv[i, h, part].astype(F32)
            sums.append(total)
        qa_recv[h, a] = (
            sums[0] * as_column(by_total, h)
            - (sums[1] * as_column(by_positive, h)) * as_column(share_negative, h)
        ).astype(BF16)
        for k in FIRST:
            send(qa_recv.at[h, a], qa_recv.at[h, a],
                 q_ss.at[24 + 8 * h + k], q_rs.at[24 + 8 * h + k], on_a(k)[1])

    combine(0)

    for i in range(4):
        cols = slice(i * 128, i * 128 + 128)
        weights[:, cols] = (
            negs[:, cols] * by_total[i:i + 1, :]
            - (poss[:, cols] * by_positive[i:i + 1, :]) * share_negative[i:i + 1, :]
        ).astype(BF16)

    @pl.loop(0, NX)
    def _(i):
        rows = pl.ds(pl.multiple_of(i * 64, 64), 64)
        k_send[i] = dot(weights[rows, :], query_half[...]).astype(BF16)

    for k in XFIRST:
        there, device = on_x(k)
        send(k_send.at[there], k_recv.at[x], k_ss.at[k], k_rs.at[k], device)
    k_recv[x] = k_send[x]

    combine(1)

    for k in XORDER:
        arrived(k_recv.at[on_x(NX - k)[0]], k_rs.at[k])
    quarter = pl.ds(pl.multiple_of(x * 64, 64), 64)
    key_sum = (
        (k_recv[0].astype(F32) + k_recv[1].astype(F32)) + k_recv[2].astype(F32)
    ) + k_recv[3].astype(F32)
    unit = unit_key[quarter, :]
    krg[x] = (
        (key_sum - unit * jnp.sum(unit * key_sum, axis=1, keepdims=True))
        * (1.0 / key_len[quarter, 0:1])
    ).astype(BF16)
    for k in XFIRST:
        send(krg.at[x], krg.at[x], k_ss.at[4 + k], k_rs.at[4 + k], on_x(k)[1])

    for h in range(2):
        for k in ORDER:
            arrived(qa_recv.at[h, on_a(NA - k)[0]], q_rs.at[24 + 8 * h + k])
        query_sum = qa_recv[h, 0].astype(F32)
        for i in range(1, NA):
            query_sum = query_sum + qa_recv[h, i].astype(F32)
        rows = pl.ds(pl.multiple_of(b * 32 + h * 16, 16), 16)
        unit = unit_all[rows, :]
        g2[0, b, h] = (
            (query_sum - unit * jnp.sum(unit * query_sum, axis=1, keepdims=True))
            * (1.0 / len_all[rows, 0:1])
        ).astype(BF16)
        for k in FIRST:
            send(g2.at[0, b, h], g2.at[0, b, h],
                 ag2_ss.at[8 * h + k], ag2_rs.at[8 * h + k], on_b(k)[1])
        send(g2.at[0, b, h], g2.at[1, b, h], ag2_ss.at[16 + 8 * h], ag2_rs.at[16 + 8 * h], partner)

    shifted_grad = dot_cols(g2[0, b].reshape(32, D), proj_ref[...])
    block = pl.ds(pl.multiple_of(b * 32, 32), 32)
    scaled = shifted_grad * gain
    normed = normed_all[block, :]
    text = (
        scaled
        - jnp.mean(scaled, axis=1, keepdims=True)
        - normed * jnp.mean(scaled * normed, axis=1, keepdims=True)
    ) * (1.0 / spread_all[block, 0:1])
    own_text = text[0:4]
    for i in range(1, NA):
        own_text = jnp.where(a == i, text[i * 4:i * 4 + 4], own_text)
    small_out[0:4, :] = own_text

    for k in XORDER:
        arrived(krg.at[on_x(NX - k)[0]], k_rs.at[4 + k])
    grads = krg[...].reshape(SLAB, D)

    @pl.loop(0, 4)
    def _(i):
        half = i // 2
        cols = pl.ds(pl.multiple_of((3 - i) * 256, 256), 256)
        spread_out = dot(grads, perm[:, cols]).astype(BF16)
        share = dot_rows(spread_out, emb_sel[...])
        rows = pl.ds(pl.multiple_of((3 - i) * 256, 256), 256)
        s_own[rows, :] = share

    s_send[...] = s_own[512:1024, :].astype(BF16)
    send(s_send, s_core, s_ss.at[0], s_rs.at[0], partner)

    for h in range(2):
        for k in ORDER:
            place = on_b(NA - k)[0]
            arrived(g2.at[0, place, h], ag2_rs.at[8 * h + k])
            send(g2.at[0, place, h], g2.at[1, place, h],
                 ag2_ss.at[16 + 8 * h + k], ag2_rs.at[16 + 8 * h + k], partner)
    arrived(s_core, s_rs.at[0])
    for i in range(NA):
        rows = slice(i * 64, i * 64 + 64)
        sb_send[i] = (s_own[rows, :] + s_core[rows, :].astype(F32)).astype(BF16)
    for k in FIRST:
        there, device = on_b(k)
        send(sb_send.at[there], sb_recv.at[b], s_ss.at[8 + k], s_rs.at[8 + k], device)
    sb_recv[b] = sb_send[b]

    for h in range(2):
        for k in (0,) + ORDER:
            arrived(g2.at[1, from_core(k), h], ag2_rs.at[16 + 8 * h + k])

    cols = pl.ds(pl.multiple_of(c * 384, 128), 384)
    half = g2[:, :, :, :, cols].reshape(GROUP, 384)
    for i in range(D // 128):
        band = slice(i * 128, i * 128 + 128)
        p_send[band, :] = dot_rows(shifted_all[:, band], half).astype(BF16)
    for h in range(2):
        for k in XFIRST:
            there, device = on_x(k)
            send(p_send.at[pl.ds(pl.multiple_of(there * 192 + h * 96, 32), 96), :],
                 p_recv.at[h, x], p_ss.at[4 * h + k], p_rs.at[4 * h + k], device)
        p_recv[h, x] = p_send[pl.ds(pl.multiple_of(x * 192 + h * 96, 32), 96), :]

    gain_sum = jnp.zeros((1, D), F32)
    bias_sum = jnp.zeros((1, D), F32)
    for i in range(4):
        rows = slice(i * 128, i * 128 + 128)
        quads = slice(i % 2 * 4, i % 2 * 4 + 4)
        grad = dot_cols(g2[i // 2, quads].reshape(128, D), proj_ref[...])
        gain_sum = gain_sum + jnp.sum(grad * normed_all[rows, :], axis=0, keepdims=True)
        bias_sum = bias_sum + jnp.sum(grad, axis=0, keepdims=True)
    gb_recv[x] = jnp.concatenate([gain_sum, bias_sum, jnp.zeros((6, D), F32)], axis=0)
    for k in XFIRST:
        send(gb_recv.at[x], gb_recv.at[x], p_ss.at[8 + k], p_rs.at[8 + k], on_x(k)[1])

    stores = []

    def store(side, place, h, i):
        rows = pl.ds(pl.multiple_of(place * 192 + h * 96, 32), 96)
        lanes = pl.ds(pl.multiple_of((c + side * (1 - 2 * c)) * 384, 128), 384)
        copy = pltpu.make_async_copy(
            p_out.at[side, place, h], proj_out.at[rows, lanes], out_sem.at[i]
        )
        copy.start()
        stores.append(copy)

    for copy in pending[:-30]:
        copy.wait_send()
    del pending[:-30]

    for h in range(2):
        for k in XORDER:
            arrived(p_recv.at[h, on_x(NX - k)[0]], p_rs.at[4 * h + k])
        total = (
            (p_recv[h, 0].astype(F32) + p_recv[h, 1].astype(F32)) + p_recv[h, 2].astype(F32)
        ) + p_recv[h, 3].astype(F32)
        p_out[0, x, h] = total.astype(BF16)
        for k in XFIRST:
            send(p_out.at[0, x, h], p_out.at[0, x, h],
                 p_ss.at[12 + 4 * h + k], p_rs.at[12 + 4 * h + k], on_x(k)[1])
        send(p_out.at[0, x, h], p_out.at[1, x, h], p_ss.at[20 + 4 * h], p_rs.at[20 + 4 * h], partner)
        store(0, x, h, 4 * h)
        if h == 0:
            for k in ORDER:
                arrived(sb_recv.at[on_b(NA - k)[0]], s_rs.at[8 + k])
            part = sb_recv[0].astype(F32)
            for i in range(1, NA):
                part = part + sb_recv[i].astype(F32)
            for i in range(NA):
                sa_send[i] = part[i * 8:i * 8 + 8, :]
            for k in FIRST:
                there, device = on_a(k)
                send(sa_send.at[there], sa_recv.at[a], s_ss.at[k], s_rs.at[k], device)
            sa_recv[a] = sa_send[a]

    for h in range(2):
        for k in XORDER:
            there = on_x(NX - k)[0]
            arrived(p_out.at[0, there, h], p_rs.at[12 + 4 * h + k])
            send(p_out.at[0, there, h], p_out.at[1, there, h],
                 p_ss.at[20 + 4 * h + k], p_rs.at[20 + 4 * h + k], partner)
            store(0, there, h, 4 * h + k)
    for k in XORDER:
        arrived(gb_recv.at[on_x(NX - k)[0]], p_rs.at[8 + k])
    small_out[4:6, :] = jnp.sum(gb_recv[...], axis=0)[0:2]

    for k in ORDER:
        arrived(sa_recv.at[on_a(NA - k)[0]], s_rs.at[k])
    small_out[8:16, 0:256] = jnp.sum(sa_recv[...], axis=0)

    for h in range(2):
        arrived(p_out.at[1, x, h], p_rs.at[20 + 4 * h])
        store(1, x, h, 8 + 4 * h)
        for k in XORDER:
            there = on_x(NX - k)[0]
            arrived(p_out.at[1, there, h], p_rs.at[20 + 4 * h + k])
            store(1, there, h, 8 + 4 * h + k)
    for copy in stores:
        copy.wait()
    for copy in pending:
        copy.wait_send()


def finish(
    small_hbm, part_hbm, text_hbm, gain_hbm, bias_hbm, proj_hbm, adapter_hbm,
    small, held, text, gain, bias, adapter, in_sem, out_sem,
):
    bands = [pl.ds(i * 192, 192) for i in range(4)]
    into = [pltpu.make_async_copy(small_hbm, small, in_sem.at[0])] + [
        pltpu.make_async_copy(part_hbm.at[band], held.at[band], in_sem.at[1 + i])
        for i, band in enumerate(bands)
    ]
    out = [
        pltpu.make_async_copy(held.at[band], proj_hbm.at[band], out_sem.at[i])
        for i, band in enumerate(bands)
    ] + [
        pltpu.make_async_copy(src, dst, out_sem.at[4 + i])
        for i, (src, dst) in enumerate((
            (text, text_hbm), (gain, gain_hbm), (bias, bias_hbm), (adapter, adapter_hbm)
        ))
    ]
    for copy in into:
        copy.start()
    into[0].wait()
    text[...] = small[0:4, :]
    gain[...] = small[4:5, :].reshape(D)
    bias[...] = small[5:6, :].reshape(D)
    adapter[...] = small[8:14, 0:192]
    for copy in out[4:]:
        copy.start()
    for first, second in zip(into[1:], out[:4]):
        first.wait()
        second.start()
    for copy in out:
        copy.wait()


def shards(
    text_features, norm_gain, norm_bias, projection, image_embeddings, adapter, slab_ids,
    positive_rows,
):
    whole = pl.BlockSpec(memory_space=pltpu.VMEM)
    dma = pltpu.SemaphoreType.DMA
    small, projection_grad = pl.pallas_call(
        kernel,
        out_shape=(
            jax.ShapeDtypeStruct((16, D), F32),
            jax.ShapeDtypeStruct((D, D), BF16),
        ),
        in_specs=[pl.BlockSpec(memory_space=pl.ANY)] * 8,
        out_specs=(whole, pl.BlockSpec(memory_space=pl.ANY)),
        scratch_shapes=[
            pltpu.VMEM((D,), F32),
            pltpu.VMEM((D,), F32),
            pltpu.VMEM((D, D), BF16),
            pltpu.VMEM((SLAB, D), BF16),
            pltpu.VMEM((D, D), BF16),
            pltpu.VMEM((SLAB,), jnp.int32),
            pltpu.VMEM((ROWS,), jnp.int32),
            pltpu.VMEM((NA, ROWS, D), BF16),
            pltpu.VMEM((128, 256), BF16),
            pltpu.VMEM((2, NA, 32, D), BF16),
            pltpu.VMEM((2, NA, 32, 256), BF16),
            pltpu.VMEM((2, NA, 2, 16, D), BF16),
            pltpu.VMEM((SLAB, D), F32),
            pltpu.VMEM((SLAB, D), BF16),
            pltpu.VMEM((SLAB, 128), F32),
            pltpu.VMEM((SLAB, 256), BF16),
            pltpu.VMEM((D, 1024), BF16),
            pltpu.VMEM((GROUP, D), F32),
            pltpu.VMEM((GROUP, D), BF16),
            pltpu.VMEM((GROUP, D), BF16),
            pltpu.VMEM((GROUP // 2, D), F32),
            pltpu.VMEM((GROUP // 2, 128), F32),
            pltpu.VMEM((GROUP // 2, 128), F32),
            pltpu.VMEM((256, GROUP), F32),
            pltpu.VMEM((SLAB, GROUP), F32),
            pltpu.VMEM((SLAB, GROUP), F32),
            pltpu.VMEM((SLAB, GROUP), BF16),
            pltpu.VMEM((SLAB, GROUP), BF16),
            pltpu.VMEM((SLAB, GROUP), BF16),
            pltpu.VMEM((1, 8, 128), F32),
            pltpu.VMEM((8, 128), F32),
            pltpu.VMEM((NA, 8, 128), F32),
            pltpu.VMEM((NA, 8, 128), F32),
            pltpu.VMEM((2, 256, D), BF16),
            pltpu.VMEM((2, 256, D), F32),
            pltpu.VMEM((2, 256, D), BF16),
            pltpu.VMEM((NA, 2, 2, 16, D), BF16),
            pltpu.VMEM((NA, 2, 2, 16, D), BF16),
            pltpu.VMEM((2, NA, 16, D), BF16),
            pltpu.VMEM((NX, 64, D), BF16),
            pltpu.VMEM((NX, 64, D), BF16),
            pltpu.VMEM((NX, 64, D), BF16),
            pltpu.VMEM((1024, 256), F32),
            pltpu.VMEM((512, 256), BF16),
            pltpu.VMEM((512, 256), BF16),
            pltpu.VMEM((NA, 64, 256), BF16),
            pltpu.VMEM((NA, 64, 256), BF16),
            pltpu.VMEM((NA, 8, 256), F32),
            pltpu.VMEM((NA, 8, 256), F32),
            pltpu.VMEM((D, 384), BF16),
            pltpu.VMEM((2, NX, 96, 384), BF16),
            pltpu.VMEM((2, NX, 2, 96, 384), BF16),
            pltpu.VMEM((NX, 8, D), F32),
            dma((24,)), dma((24,)),
            dma((24,)), dma((24,)),
            dma((16,)), dma((16,)),
            dma((40,)), dma((40,)),
            dma((32,)), dma((32,)),
            dma((8,)), dma((8,)),
            dma((16,)), dma((16,)),
            dma((28,)), dma((28,)),
            dma((8,)), dma((16,)),
        ],
        compiler_params=pltpu.CompilerParams(
            collective_id=0, has_side_effects=True, vmem_limit_bytes=62 * 1024 * 1024
        ),
    )(
        text_features,
        norm_gain,
        norm_bias,
        projection,
        image_embeddings,
        adapter,
        slab_ids,
        positive_rows,
    )
    text_grad, gain_grad, bias_grad, projection_grad, adapter_grad = pl.pallas_call(
        finish,
        out_shape=(
            jax.ShapeDtypeStruct((ROWS, D), F32),
            jax.ShapeDtypeStruct((D,), F32),
            jax.ShapeDtypeStruct((D,), F32),
            jax.ShapeDtypeStruct((D, D), BF16),
            jax.ShapeDtypeStruct((6, 192), F32),
        ),
        in_specs=[pl.BlockSpec(memory_space=pl.ANY)] * 2,
        out_specs=(pl.BlockSpec(memory_space=pl.ANY),) * 5,
        scratch_shapes=[
            pltpu.VMEM((16, D), F32),
            pltpu.VMEM((D, D), BF16),
            pltpu.VMEM((ROWS, D), F32),
            pltpu.VMEM((D,), F32),
            pltpu.VMEM((D,), F32),
            pltpu.VMEM((6, 192), F32),
            dma((5,)), dma((8,)),
        ],
        compiler_params=pltpu.CompilerParams(vmem_limit_bytes=62 * 1024 * 1024),
    )(small, projection_grad)
    return text_grad, gain_grad, bias_grad, projection_grad, adapter_grad.T


def solution(mesh):
    placed = (
        P(("corpus", "query"), None),
        P(),
        P(),
        P(),
        P("corpus", None),
        P(),
        P("corpus"),
        P(("corpus", "query")),
    )
    return jax.shard_map(
        shards,
        mesh=mesh,
        in_specs=placed,
        out_specs=(P(("corpus", "query"), None), P(), P(), P(), P("query", "corpus")),
        check_vma=False,
    )
```
